32 devices in a mesh: mesh: 16 (over z, x, core), state: 2 (over y).
Axes of the slice: x: 2, y: 2, z: 4, core: 2. Of those that a mesh axis runs over, the one named last changes fastest.
Arguments:
- subspace: float32 [2048, 4096], P('state', 'mesh'), may hold values from -6 to 6
- ritz: float32 [1024, 2048], P('state'), may hold values from -0.125 to 0.125
- element_ham: float32 [256, 125, 125], P('mesh'), may hold values from -0.6 to 0.6
- connect: int32 [256, 125], P('mesh'), may hold values from 0 to 383, as said below
- send_rows: int32 [16, 4, 32], P('mesh'), may hold values from 0 to 255, as said below
Outputs:
- filtered: float32 [1024, 4096], P('state', 'mesh')
The draws below stay inside these ranges and needn't reach their ends.
Inputs may be any that keep to these rules, and one draw needn't show every extreme that they name: send_rows[p][k] lists nodes of partition p, local numbering, that neighbour k of p uses; only a leading part of each list, of 32 entries or fewer, is used, and some partition uses a whole list. `connect`: entries below 256 are the partition's own nodes; an entry 256 + k * 32 + j is entry j of the list that neighbour k keeps for this partition.
All inputs are finite; a program needn't handle non-finite values.
Results may differ from the reference program's by a relative error of at most 0.0001.
Values sent between devices are 32-bit elements; how exact they have to be, the bound alone decides.
No kernel may reach another device: no remote copies, remote signals or barrier semaphores. Data moves between devices by JAX's collectives and lax.ppermute only.
A program may use at most 64 MiB of HBM per device.

```python
import jax
import jax.numpy as jnp
from jax import lax

STATES = 2048
BLOCK = 1024
ELEM_NODES = 125
NODE_DEV = 256
ELEM_DEV = 16
HALO = 32
NODES = 4096
ELEMS = 256
N_MESH = 16


def topology(key):
    base = jax.random.fold_in(key, 11)
    keys = jax.random.split(base, 3)
    across = N_MESH // 2
    offsets = jnp.array([1, -1, across, -across], jnp.int32)
    partition = jnp.arange(N_MESH, dtype=jnp.int32)
    neighbour_ids = (partition[:, None] + offsets[None, :] + N_MESH) % N_MESH
    lowest = max(1, HALO // 4)
    counts = jax.random.randint(keys[1], (N_MESH, 4), lowest, HALO + 1)
    chosen = jax.random.randint(keys[2], (), 0, N_MESH)
    counts = counts.at[chosen, 2].set(HALO)
    return (neighbour_ids.astype(jnp.int32), counts, chosen)


def draw_send_rows(key, part):
    return jax.random.randint(jax.random.fold_in(key, 13), (N_MESH, 4, HALO), 0, NODE_DEV).astype(jnp.int32)


def draw_connect(key, part):
    neighbour_ids, counts, chosen = topology(key)
    reverse = jnp.array([1, 0, 3, 2], jnp.int32)
    incoming = counts[neighbour_ids, reverse[None, :]]
    keys = jax.random.split(jax.random.fold_in(key, 17), 4)
    total_rows = ELEM_DEV * N_MESH
    shape = (total_rows, ELEM_NODES)
    device = jnp.arange(total_rows, dtype=jnp.int32) // ELEM_DEV
    ghost = jax.random.randint(keys[0], shape, 0, 4) == 0
    slot_index = jax.random.randint(keys[1], shape, 0, 4)
    spread = jax.random.randint(keys[2], shape, 0, 1 << 20)
    limit = incoming[device[:, None], slot_index]
    place = spread % limit
    own_rows = jax.random.randint(keys[3], shape, 0, NODE_DEV)
    result = jnp.where(ghost, NODE_DEV + slot_index * HALO + place, own_rows)
    target = neighbour_ids[chosen, 2]
    result = result.at[target * ELEM_DEV, 0].set(NODE_DEV + 4 * HALO - 1)
    return result.astype(jnp.int32)


def levels(own_key, dims, cuts, smallest, high):
    level, own = 1.0, jax.random.fold_in(own_key, 6)
    for position, blocks in cuts:
        heights = jnp.exp(jax.random.uniform(jax.random.fold_in(own, position), (blocks,), jnp.float32, smallest / len(cuts), high / len(cuts)))
        level = level * jnp.repeat(heights, dims[position] // blocks).reshape([-1 if axis == position else 1 for axis in range(len(dims))])
    return level


def noise(key, extent, width, bound, shards=(), kind=jnp.bfloat16):
    drawn = jax.random.normal(key, extent, jnp.float32) * width
    if len(shards) > 0:
        drawn = levels(key, extent, shards, -0.22, 0.18) * drawn
    return jnp.clip(drawn, min=-bound, max=bound).astype(kind)


def setup_inputs(seed: int = 0) -> dict:
    key_list = jax.random.split(jax.random.key(seed), 6)
    subspace = noise(key_list[0], (STATES, NODES), 1.0, 6.0, ((0, 2), (1, 16)), jnp.float32)
    ritz = noise(key_list[1], (BLOCK, STATES), STATES ** -0.5, 0.125, ((0, 2),), jnp.float32)
    element_ham = noise(key_list[2], (ELEMS, ELEM_NODES, ELEM_NODES), 0.1, 0.6, ((0, 16),), jnp.float32)
    connect = draw_connect(jax.random.fold_in(key_list[5], 71), 0)
    send_rows = draw_send_rows(jax.random.fold_in(key_list[5], 71), 0)
    return dict(subspace=subspace, ritz=ritz, element_ham=element_ham, connect=connect, send_rows=send_rows)


def global_connect(connect, send_rows):
    grouped = connect.reshape(N_MESH, ELEM_DEV, ELEM_NODES).astype(jnp.int32)
    partition = jnp.arange(N_MESH, dtype=jnp.int32)[:, None, None]
    across = N_MESH // 2
    offsets = jnp.array([1, -1, across, -across], jnp.int32)
    offset = jnp.maximum(grouped - NODE_DEV, 0)
    slot_index = offset // HALO
    place = offset % HALO
    owner = (partition + offsets[slot_index] + N_MESH) % N_MESH
    back_slot = slot_index + 1 - 2 * (slot_index % 2)
    remote = owner * NODE_DEV + send_rows[owner, back_slot, place]
    return jnp.where(grouped < NODE_DEV, partition * NODE_DEV + grouped, remote).astype(jnp.int32)


def apply_ham(vectors, node_table, element_ham):
    hams = element_ham.reshape(N_MESH, ELEM_DEV, ELEM_NODES, ELEM_NODES)

    def visit(result, item):
        indices, matrices = item
        gathered = vectors[:, indices]
        product = jnp.einsum('eab,ceb->cea', matrices, gathered, precision=lax.Precision.HIGHEST)
        return result.at[:, indices].add(product), None

    result, _ = lax.scan(visit, jnp.zeros_like(vectors), (node_table, hams))
    return result


def reference(subspace, ritz, element_ham, connect, send_rows):
    node_table = global_connect(connect, send_rows)
    half = 1.5
    centre = 2.5
    sigma_one = half / (-1.0 - centre)
    sigma_two = 1.0 / (2.0 / sigma_one - sigma_one)
    start_block = jnp.dot(ritz, subspace, precision=lax.Precision.HIGHEST, preferred_element_type=jnp.float32)
    first = (sigma_one / half) * (apply_ham(start_block, node_table, element_ham) - centre * start_block)
    second = (2.0 * sigma_two / half) * (apply_ham(first, node_table, element_ham) - centre * first)
    return second - sigma_one * sigma_two * start_block
```

```python
import jax
import jax.numpy as jnp
from jax import lax
from jax.sharding import PartitionSpec as P

F32 = jnp.float32
HIGH = lax.Precision.HIGH


def mm(a, b, dims=((1,), (0,))):
    return lax.dot_general(a, b, (dims, ((), ())), precision=HIGH, preferred_element_type=F32)


def per_device(subspace, ritz, element_ham, connect, send_rows):
    depth, nodes = subspace.shape
    elems, size = connect.shape
    slots, halo = send_rows.shape[1:]
    partitions = lax.axis_size("mesh")
    groups = lax.axis_size("state")
    across = partitions // 2
    wide = slots * halo
    half_nodes = wide

    odd = lax.axis_index("mesh") % 2
    group = lax.axis_index("state")
    pairs_far = [(i, (i + across) % partitions) for i in range(partitions)]
    pairs_in = [(i, i ^ 1) for i in range(partitions)]
    pairs_out = [
        (i, (i + 1) % partitions if i % 2 else (i - 1) % partitions) for i in range(partitions)
    ]

    lists = send_rows[0]
    outer = jnp.where(odd == 1, lists[0], lists[1])
    inner = jnp.where(odd == 1, lists[1], lists[0])
    sent = jnp.concatenate([lists[2], lists[3], outer, inner])
    ids = jnp.arange(nodes, dtype=jnp.int32)
    hits = (sent[:, None] == ids[None, :]).astype(F32)
    edge = jnp.max(hits, axis=0).astype(jnp.int32)
    count = jnp.sum(jnp.where(ids[:, None] <= ids[None, :], edge[:, None], 0), axis=0)
    place = jnp.where(edge == 1, count - 1, jnp.sum(edge) + ids - count)
    shuffle = place[None, :] == ids[:, None]
    origin = jnp.sum(jnp.where(shuffle, ids[None, :], 0), axis=1)
    shuffle = shuffle.astype(F32)
    lane = jnp.arange(halo, dtype=jnp.int32)
    ghost_ids = nodes + jnp.concatenate(
        [3 * halo + lane, 2 * halo + lane, (1 - odd) * halo + lane, odd * halo + lane]
    )
    pick = (sent[:, None] == origin[None, :half_nodes]).astype(F32)

    turned = mm(shuffle, subspace, ((1,), (1,)))
    first_rows = turned[:half_nodes]
    other_rows = turned[half_nodes:]

    def from_group(rows, step):
        return lax.ppermute(rows, "state", [(i, (i + step) % groups) for i in range(groups)])

    edge_in = [from_group(first_rows, step) for step in range(1, groups)]
    rest_in = [from_group(other_rows, step) for step in range(1, groups)]

    def ritz_part(step):
        return lax.dynamic_slice_in_dim(ritz, ((group - step) % groups) * depth, depth, 1)

    columns = jnp.concatenate([origin, ghost_ids])
    spread = (connect.reshape(-1)[:, None] == columns[None, :]).astype(F32)
    blocks = lax.dot_general(
        element_ham,
        spread.reshape(elems, size, nodes + wide),
        (((2,), (1,)), ((0,), (0,))),
        precision=HIGH,
        preferred_element_type=F32,
    )
    ham = mm(spread, blocks.reshape(elems * size, nodes + wide), ((0,), (0,)))

    def exchange(packed):
        far = lax.ppermute(packed[: 2 * halo], "mesh", pairs_far)
        out = lax.ppermute(packed[2 * halo : 3 * halo], "mesh", pairs_out)
        near = lax.ppermute(packed[3 * halo :], "mesh", pairs_in)
        return jnp.concatenate([far, out, near], 0)

    own_start = mm(turned, ritz_part(0), ((1,), (1,)))
    start_edge = own_start[:half_nodes]
    for step in range(1, groups):
        start_edge = start_edge + mm(edge_in[step - 1], ritz_part(step), ((1,), (1,)))
    ghosts = exchange(mm(pick, start_edge))
    start_rest = own_start[half_nodes:]
    for step in range(1, groups):
        start_rest = start_rest + mm(rest_in[step - 1], ritz_part(step), ((1,), (1,)))

    half = 1.5
    centre = 2.5
    sigma_one = half / (-1.0 - centre)
    sigma_two = 1.0 / (2.0 / sigma_one - sigma_one)
    scale_one = sigma_one / half
    scale_two = 2.0 * sigma_two / half

    extended = jnp.concatenate([start_edge, start_rest, ghosts], 0)
    start = extended[:nodes]
    returned = exchange(mm(ham[nodes:], extended))
    base = scale_one * (mm(ham[:nodes], extended) - centre * start)
    packed = mm(pick, base[:half_nodes]) + mm(scale_one * mm(pick, pick, ((1,), (1,))), returned)
    ghosts = exchange(packed)
    first = jnp.concatenate(
        [
            base[:half_nodes] + scale_one * mm(pick, returned, ((0,), (0,))),
            base[half_nodes:],
        ],
        0,
    )
    own_part = mm(ham[:, :nodes], first)
    returned = exchange(own_part[nodes:] + mm(ham[nodes:, nodes:], ghosts))
    second = (
        scale_two * (own_part[:nodes] + mm(ham[:nodes, nodes:], ghosts) - centre * first)
        - sigma_one * sigma_two * start
    )
    return mm(second, shuffle, ((0,), (0,))) + mm(returned, scale_two * hits, ((0,), (0,)))


def solution(mesh):
    in_specs = (
        P("state", "mesh"),
        P("state", None),
        P("mesh", None, None),
        P("mesh", None),
        P("mesh", None, None),
    )
    out_specs = P("state", "mesh")
    return jax.shard_map(
        per_device, mesh=mesh, in_specs=in_specs, out_specs=out_specs, check_vma=False
    )
```

```python
import jax
import jax.numpy as jnp
from jax import lax
from jax.sharding import PartitionSpec as P

F32 = jnp.float32
HIGH = lax.Precision.HIGH


def mm(a, b, dims=((1,), (0,))):
    return lax.dot_general(a, b, (dims, ((), ())), precision=HIGH, preferred_element_type=F32)


def per_device(subspace, ritz, element_ham, connect, send_rows):
    depth, nodes = subspace.shape
    elems, size = connect.shape
    slots, halo = send_rows.shape[1:]
    partitions = lax.axis_size("mesh")
    groups = lax.axis_size("state")
    across = partitions // 2
    wide = slots * halo
    edge_nodes = wide

    odd = lax.axis_index("mesh") % 2
    group = lax.axis_index("state")
    pairs_far = [(i, (i + across) % partitions) for i in range(partitions)]
    pairs_in = [(i, i ^ 1) for i in range(partitions)]
    pairs_out = [
        (i, (i + 1) % partitions if i % 2 else (i - 1) % partitions) for i in range(partitions)
    ]

    lists = send_rows[0]
    outer = jnp.where(odd == 1, lists[0], lists[1])
    inner = jnp.where(odd == 1, lists[1], lists[0])
    sent = jnp.concatenate([lists[2], lists[3], outer, inner])
    ids = jnp.arange(nodes, dtype=jnp.int32)
    hits = (sent[:, None] == ids[None, :]).astype(F32)
    edge = jnp.max(hits, axis=0).astype(jnp.int32)
    count = jnp.sum(jnp.where(ids[:, None] <= ids[None, :], edge[:, None], 0), axis=0)
    place = jnp.where(edge == 1, count - 1, jnp.sum(edge) + ids - count)
    shuffle = place[None, :] == ids[:, None]
    origin = jnp.sum(jnp.where(shuffle, ids[None, :], 0), axis=1)
    shuffle = shuffle.astype(F32)
    lane = jnp.arange(halo, dtype=jnp.int32)
    ghost_ids = nodes + jnp.concatenate(
        [3 * halo + lane, 2 * halo + lane, (1 - odd) * halo + lane, odd * halo + lane]
    )
    pick = (sent[:, None] == origin[None, :edge_nodes]).astype(F32)

    def from_group(rows, step):
        return lax.ppermute(rows, "state", [(i, (i + step) % groups) for i in range(groups)])

    head = depth // 4
    steps = range(1, groups)
    head_in = [from_group(subspace[:head], step) for step in steps]
    turned = mm(shuffle, subspace, ((1,), (1,)))
    edge_in = [from_group(turned[:edge_nodes, head:], step) for step in steps]
    rest_in = [from_group(turned[edge_nodes:, head:], step) for step in steps]

    def ritz_part(step):
        return lax.dynamic_slice_in_dim(ritz, ((group - step) % groups) * depth, depth, 1)

    columns = jnp.concatenate([origin, ghost_ids])
    spread = (connect.reshape(-1)[:, None] == columns[None, :]).astype(F32)
    blocks = lax.dot_general(
        element_ham,
        spread.reshape(elems, size, nodes + wide),
        (((2,), (1,)), ((0,), (0,))),
        precision=HIGH,
        preferred_element_type=F32,
    )
    ham = mm(spread, blocks.reshape(elems * size, nodes + wide), ((0,), (0,)))

    def far(rows):
        return lax.ppermute(rows, "mesh", pairs_far)

    def ring(rows):
        out = lax.ppermute(rows[:halo], "mesh", pairs_out)
        near = lax.ppermute(rows[halo:], "mesh", pairs_in)
        return jnp.concatenate([out, near], 0)

    duo = 2 * halo
    pick_far, pick_ring = pick[:duo], pick[duo:]
    far_rows = slice(nodes, nodes + duo)
    ring_rows = slice(nodes + duo, nodes + wide)

    own_start = mm(turned, ritz_part(0), ((1,), (1,)))
    for step in steps:
        turned_head = mm(shuffle, head_in[step - 1], ((1,), (1,)))
        own_start = own_start + mm(turned_head, ritz_part(step)[:, :head], ((1,), (1,)))
    start_edge = own_start[:edge_nodes]
    for step in steps:
        start_edge = start_edge + mm(edge_in[step - 1], ritz_part(step)[:, head:], ((1,), (1,)))
    packed = mm(pick, start_edge)
    overlap = mm(pick_far, pick_far, ((1,), (1,)))
    message = far(jnp.concatenate([packed[:duo], overlap, ham[far_rows, far_rows]], 1))
    block_rows = ritz.shape[0]
    ghosts = jnp.concatenate([message[:, :block_rows], ring(packed[duo:])], 0)
    overlap_in = message[:, block_rows : block_rows + duo]
    couple_in = message[:, block_rows + duo :]
    start_rest = own_start[edge_nodes:]
    for step in steps:
        start_rest = start_rest + mm(rest_in[step - 1], ritz_part(step)[:, head:], ((1,), (1,)))

    half = 1.5
    centre = 2.5
    sigma_one = half / (-1.0 - centre)
    sigma_two = 1.0 / (2.0 / sigma_one - sigma_one)
    scale_one = sigma_one / half
    scale_two = 2.0 * sigma_two / half

    extended = jnp.concatenate([start_edge, start_rest, ghosts], 0)
    start = extended[:nodes]
    sent_back = mm(ham[nodes:], extended)
    back_far = far(sent_back[:duo])
    back_ring = ring(sent_back[duo:])
    base = scale_one * (mm(ham[:nodes], extended) - centre * start)
    base_edge = base[:edge_nodes]
    fetched_far = far(
        mm(pick_far, base_edge)
        + mm(scale_one * mm(pick_far, pick_ring, ((1,), (1,))), back_ring)
    )
    back = jnp.concatenate([back_far, back_ring], 0)
    fetched_ring = ring(
        mm(pick_ring, base_edge) + mm(scale_one * mm(pick_ring, pick, ((1,), (1,))), back)
    )
    first_edge = base_edge + scale_one * mm(pick, back, ((0,), (0,)))
    first = jnp.concatenate([first_edge, base[edge_nodes:]], 0)

    own_part = mm(ham[:, :nodes], first)
    ring_part = mm(ham[:, ring_rows], fetched_ring)
    returned_far = far(own_part[far_rows] + ring_part[far_rows])
    ghosts_far = fetched_far + mm(scale_one * overlap_in, sent_back[:duo])
    known = mm(couple_in, mm(pick_far, first_edge))
    far_part = mm(ham[:, far_rows], ghosts_far)
    returned_ring = ring(own_part[ring_rows] + ring_part[ring_rows] + far_part[ring_rows])
    second = (
        scale_two * (own_part[:nodes] + ring_part[:nodes] + far_part[:nodes] - centre * first)
        - sigma_one * sigma_two * start
    )
    weights = scale_two * hits
    result = mm(second, shuffle, ((0,), (0,))) + mm(
        jnp.concatenate([known, returned_ring], 0), weights, ((0,), (0,))
    )
    return result + mm(returned_far, weights[:duo], ((0,), (0,)))


def solution(mesh):
    in_specs = (
        P("state", "mesh"),
        P("state", None),
        P("mesh", None, None),
        P("mesh", None),
        P("mesh", None, None),
    )
    out_specs = P("state", "mesh")
    return jax.shard_map(
        per_device, mesh=mesh, in_specs=in_specs, out_specs=out_specs, check_vma=False
    )
```

```python
import jax
import jax.numpy as jnp
from jax import lax
from jax.experimental import pallas as pl
from jax.experimental.pallas import tpu as pltpu
from jax.sharding import PartitionSpec as P

F32 = jnp.float32
BF16 = jnp.bfloat16
I32 = jnp.int32
NN = ((1,), (0,))
NT = ((1,), (1,))

HALF = 1.5
CENTRE = 2.5
SIGMA_ONE = HALF / (-1.0 - CENTRE)
SIGMA_TWO = 1.0 / (2.0 / SIGMA_ONE - SIGMA_ONE)
SCALE_ONE = SIGMA_ONE / HALF
SCALE_TWO = 2.0 * SIGMA_TWO / HALF


def dot(a, b, dims=NN):
    return lax.dot_general(a, b, (dims, ((), ())), preferred_element_type=F32)


def split(x):
    top = x.astype(BF16)
    return top, (x - top.astype(F32)).astype(BF16)


def mul(a, b, dims=NN):
    return dot(a[0], b[0], dims) + (dot(a[0], b[1], dims) + dot(a[1], b[0], dims))


def sift(a, x):
    top, low = split(x)
    return dot(a, top) + dot(a, low)


def call(body, outs, *args, **rest):
    return pl.pallas_call(
        body,
        out_shape=[jax.ShapeDtypeStruct(*out) for out in outs],
        compiler_params=pltpu.CompilerParams(vmem_limit_bytes=16 << 20),
        cost_estimate=pl.CostEstimate(flops=1000, bytes_accessed=1000, transcendentals=0),
        **rest,
    )(*args)


def column(row, width):
    down = lax.broadcasted_iota(I32, (width, width), 0)
    along = lax.broadcasted_iota(I32, (width, width), 1)
    return jnp.sum(jnp.where(down == along, row, 0), axis=1, keepdims=True)


def renumber(lists, subspace, turned_edge, turned_rest, shuffle_out, origin_out):
    slots, halo = lists.shape[1:]
    nodes = subspace.shape[1]
    edge_nodes = slots * halo
    ids = lax.broadcasted_iota(I32, (halo, nodes), 1)
    seen = jnp.zeros((halo, nodes), F32)
    for slot in range(slots):
        sent = column(lists[0, slot : slot + 1, :], halo)
        seen = jnp.maximum(seen, jnp.where(sent == ids, 1.0, 0.0))
    edge = jnp.max(seen, axis=0, keepdims=True)
    down = lax.broadcasted_iota(I32, (nodes, nodes), 0)
    along = lax.broadcasted_iota(I32, (nodes, nodes), 1)
    upto = jnp.where(down <= along, 1.0, 0.0).astype(BF16)
    count = dot(jnp.broadcast_to(edge, (8, nodes)).astype(BF16), upto)[:1].astype(I32)
    total = jnp.sum(edge, axis=1, keepdims=True).astype(I32)
    place = jnp.where(edge > 0.5, count - 1, total + along[:1] - count)
    match = place == down
    shuffle = jnp.where(match, 1.0, 0.0).astype(BF16)
    shuffle_out[...] = shuffle
    origin_out[...] = jnp.sum(jnp.where(match, along, 0), axis=1, keepdims=True)
    top, low = split(subspace[...])
    turned = dot(shuffle, top, NT) + dot(shuffle, low, NT)
    turned_edge[...] = turned[:edge_nodes]
    turned_rest[...] = turned[edge_nodes:]


def assemble(
    odd, lists, connect, element_ham, shuffle, origin, top_out, low_out, pick_out, both_out, hits_out, pair_out
):
    elems, size = connect.shape
    slots, halo = lists.shape[1:]
    nodes = origin.shape[0]
    wide = slots * halo
    duo = 2 * halo
    swap = odd[0] == 1
    columns = [column(lists[0, slot : slot + 1, :], halo) for slot in range(slots)]
    outer = jnp.where(swap, columns[0], columns[1])
    inner = jnp.where(swap, columns[1], columns[0])
    sent = jnp.concatenate([columns[2], columns[3], outer, inner], 0)
    hits = jnp.where(sent == lax.broadcasted_iota(I32, (wide, nodes), 1), 1.0, 0.0).astype(BF16)
    hits_out[...] = hits
    pick = dot(hits, shuffle[:wide, :], NT).astype(BF16)
    pick_out[...] = pick
    both = dot(pick, pick, NT)
    both_out[...] = both.astype(BF16)

    lane = lax.broadcasted_iota(I32, (halo, 1), 0)
    flag = odd[0]
    ghost = jnp.concatenate(
        [3 * halo + lane, 2 * halo + lane, (1 - flag) * halo + lane, flag * halo + lane], 0
    )
    numbers = jnp.concatenate([origin[...], nodes + ghost], 0)
    ham = jnp.zeros((nodes + wide, nodes + wide), F32)
    for elem in range(elems):
        spread = jnp.where(numbers == connect[elem : elem + 1, :], 1.0, 0.0).astype(BF16)
        top, low = split(element_ham[elem])
        rows = dot(top, spread, NT) + dot(low, spread, NT)
        ham = ham + sift(spread, rows)
    top, low = split(ham)
    top_out[...] = top
    low_out[...] = low
    far = slice(nodes, nodes + duo)
    pair_out[...] = jnp.concatenate([both[:duo, :duo], ham[far, far]], 1)


def rotate_own(group, turned_edge, turned_rest, ritz, start_out, top_out, low_out):
    step = pl.program_id(0)
    top, low = split(ritz[...])

    @pl.when(step == 0)
    def _():
        edge_nodes = turned_edge.shape[0]
        start_out[:edge_nodes, :] = mul(split(turned_edge[...]), (top, low), NT)
        start_out[edge_nodes:, :] = mul(split(turned_rest[...]), (top, low), NT)

    @pl.when(step > 0)
    def _():
        top_out[...] = top.T
        low_out[...] = low.T


def rotate_edge(rows, start_own, top, low, pick, pair, start_out, far_out, out_out, near_out):
    edge_nodes = rows.shape[0]
    wide, block = pick.shape[0], start_own.shape[1]
    quarter = wide // 4
    start = start_own[:edge_nodes, :] + mul(split(rows[...]), (top[...], low[...]))
    start_out[...] = start
    packed = sift(pick[...], start)
    far_out[:, :block] = packed[: 2 * quarter]
    far_out[:, block:] = pair[...]
    out_out[...] = packed[2 * quarter : 3 * quarter]
    near_out[...] = packed[3 * quarter :]


def rotate_rest(
    rows, start_own, start_edge, top, low, far_in, out_in, near_in, ham_top, ham_low,
    ext_out, far_out, out_out, near_out,
):
    edge_nodes, block = start_edge.shape
    nodes = start_own.shape[0]
    halo = out_in.shape[0]
    rest = start_own[edge_nodes:, :] + mul(split(rows[...]), (top[...], low[...]))
    ext = jnp.concatenate(
        [start_edge[...], rest, far_in[:, :block], out_in[...], near_in[...]], 0
    )
    ext_out[...] = ext
    back = mul((ham_top[nodes:, :], ham_low[nodes:, :]), split(ext))
    far_out[...] = back[: 2 * halo]
    out_out[...] = back[2 * halo : 3 * halo]
    near_out[...] = back[3 * halo :]


def first_base(ext, ham_top, ham_low, pick, far_in, back_far, base_out, packed_out, adjust_out):
    nodes = ham_top.shape[0] - pick.shape[0]
    edge_nodes = pick.shape[1]
    block = ext.shape[1]
    duo = far_in.shape[0]
    own = (ham_top[:nodes, :], ham_low[:nodes, :])
    base = SCALE_ONE * (mul(own, split(ext[...])) - CENTRE * ext[:nodes, :])
    base_out[...] = base
    packed_out[...] = sift(pick[...], base[:edge_nodes])
    overlap = far_in[:, block : block + duo].astype(BF16)
    adjust_out[...] = SCALE_ONE * sift(overlap, back_far[...])


def fetch_far(packed, both, out_in, near_in, far_out):
    duo = 2 * out_in.shape[0]
    back = jnp.concatenate([out_in[...], near_in[...]], 0)
    far_out[...] = packed[:duo, :] + SCALE_ONE * sift(both[:duo, duo:], back)


def fetch_ring(packed, both, far_in, out_in, near_in, out_out, near_out):
    halo = out_in.shape[0]
    back = jnp.concatenate([far_in[...], out_in[...], near_in[...]], 0)
    rows = packed[2 * halo :, :] + SCALE_ONE * sift(both[2 * halo :, :], back)
    out_out[...] = rows[:halo]
    near_out[...] = rows[halo:]


def first_own(
    base, pick, far_in, out_in, near_in, ham_top, ham_low, pair_in, first_out, part_out, known_out
):
    edge_nodes = pick.shape[1]
    nodes = base.shape[0]
    block = base.shape[1]
    duo = far_in.shape[0]
    back = jnp.concatenate([far_in[...], out_in[...], near_in[...]], 0)
    edge = base[:edge_nodes, :] + SCALE_ONE * sift(pick[...].T, back)
    first = jnp.concatenate([edge, base[edge_nodes:, :]], 0)
    first_out[...] = first
    part_out[...] = mul((ham_top[:, :nodes], ham_low[:, :nodes]), split(first))
    couple = split(pair_in[:, block + duo :])
    known_out[...] = mul(couple, split(sift(pick[:duo, :], edge)))


def return_far(part, ham_top, ham_low, out_in, near_in, far_out):
    halo = out_in.shape[0]
    nodes = part.shape[0] - 4 * halo
    far = slice(nodes, nodes + 2 * halo)
    ring = slice(nodes + 2 * halo, nodes + 4 * halo)
    ghosts = split(jnp.concatenate([out_in[...], near_in[...]], 0))
    far_out[...] = part[far, :] + mul((ham_top[far, ring], ham_low[far, ring]), ghosts)


def return_ring(
    part, ham_top, ham_low, far_in, adjust, out_in, near_in, ghosts_out, out_out, near_out
):
    halo = out_in.shape[0]
    nodes = part.shape[0] - 4 * halo
    ring = slice(nodes + 2 * halo, nodes + 4 * halo)
    ghosts = jnp.concatenate([far_in[...] + adjust[...], out_in[...], near_in[...]], 0)
    ghosts_out[...] = ghosts
    rows = part[ring, :] + mul((ham_top[ring, nodes:], ham_low[ring, nodes:]), split(ghosts))
    out_out[...] = rows[:halo]
    near_out[...] = rows[halo:]


def second_base(part, ghosts, ham_top, ham_low, first, ext, known, shuffle, hits, result_out):
    nodes = first.shape[0]
    duo = known.shape[0]
    ham = (ham_top[:nodes, nodes:], ham_low[:nodes, nodes:])
    second = part[:nodes, :] + mul(ham, split(ghosts[...])) - CENTRE * first[...]
    second = SCALE_TWO * second - SIGMA_ONE * SIGMA_TWO * ext[:nodes, :]
    top, low = split(second.T)
    result = dot(top, shuffle[...]) + dot(low, shuffle[...])
    top, low = split(SCALE_TWO * known[...].T)
    result_out[...] = result + (dot(top, hits[:duo, :]) + dot(low, hits[:duo, :]))


def finish(result, hits, far_in, out_in, near_in, out):
    back = jnp.concatenate([far_in[...], out_in[...], near_in[...]], 0)
    top, low = split(SCALE_TWO * back.T)
    out[...] = result[...] + (dot(top, hits[...]) + dot(low, hits[...]))


def per_device(subspace, ritz, element_ham, connect, send_rows):
    depth, nodes = subspace.shape
    block = ritz.shape[0]
    slots, halo = send_rows.shape[1:]
    partitions = lax.axis_size("mesh")
    groups = lax.axis_size("state")
    across = partitions // 2
    wide = slots * halo
    duo = 2 * halo
    full = nodes + wide

    odd = (lax.axis_index("mesh") % 2).astype(I32).reshape(1)
    group = lax.axis_index("state").astype(I32).reshape(1)
    pairs_far = [(i, (i + across) % partitions) for i in range(partitions)]
    pairs_in = [(i, i ^ 1) for i in range(partitions)]
    pairs_out = [
        (i, (i + 1) % partitions if i % 2 else (i - 1) % partitions) for i in range(partitions)
    ]

    def far(rows):
        return lax.ppermute(rows, "mesh", pairs_far)

    def out(rows):
        return lax.ppermute(rows, "mesh", pairs_out)

    def near(rows):
        return lax.ppermute(rows, "mesh", pairs_in)

    def gather(rows):
        parts = [
            lax.ppermute(rows, "state", [(i, (i + step) % groups) for i in range(groups)])
            for step in range(1, groups)
        ]
        return parts[0] if len(parts) == 1 else jnp.concatenate(parts, 1)

    def rows_of(count):
        return ((count, block), F32)

    halo_out = [rows_of(duo), rows_of(halo), rows_of(halo)]
    smem = pl.BlockSpec(memory_space=pltpu.SMEM)
    vmem = pl.BlockSpec(memory_space=pltpu.VMEM)

    turned_edge, turned_rest, shuffle, origin = call(
        renumber,
        [((wide, depth), F32), ((nodes - wide, depth), F32), ((nodes, nodes), BF16), ((nodes, 1), I32)],
        send_rows,
        subspace,
    )
    edge_in = gather(turned_edge)
    rest_in = gather(turned_rest)
    ham_top, ham_low, pick, both, hits, pair = call(
        assemble,
        [
            ((full, full), BF16),
            ((full, full), BF16),
            ((wide, wide), BF16),
            ((wide, wide), BF16),
            ((wide, nodes), BF16),
            ((duo, 2 * duo), F32),
        ],
        odd,
        send_rows,
        connect,
        element_ham,
        shuffle,
        origin,
        in_specs=[smem] + [vmem] * 5,
    )
    others = groups - 1
    start_own, ritz_top, ritz_low = pl.pallas_call(
        rotate_own,
        out_shape=[
            jax.ShapeDtypeStruct((nodes, block), F32),
            jax.ShapeDtypeStruct((others * depth, block), BF16),
            jax.ShapeDtypeStruct((others * depth, block), BF16),
        ],
        grid_spec=pltpu.PrefetchScalarGridSpec(
            num_scalar_prefetch=1,
            grid=(groups,),
            in_specs=[
                pl.BlockSpec((wide, depth), lambda i, g: (0, 0)),
                pl.BlockSpec((nodes - wide, depth), lambda i, g: (0, 0)),
                pl.BlockSpec((block, depth), lambda i, g: (0, lax.rem(g[0] + groups - i, groups))),
            ],
            out_specs=[
                pl.BlockSpec((nodes, block), lambda i, g: (0, 0)),
                pl.BlockSpec((depth, block), lambda i, g: (jnp.maximum(i - 1, 0), 0)),
                pl.BlockSpec((depth, block), lambda i, g: (jnp.maximum(i - 1, 0), 0)),
            ],
        ),
        compiler_params=pltpu.CompilerParams(vmem_limit_bytes=32 << 20),
        cost_estimate=pl.CostEstimate(flops=1000, bytes_accessed=1000, transcendentals=0),
    )(group, turned_edge, turned_rest, ritz)

    start_edge, far_rows, out_rows, near_rows = call(
        rotate_edge,
        [rows_of(wide), ((duo, block + 2 * duo), F32), rows_of(halo), rows_of(halo)],
        edge_in, start_own, ritz_top, ritz_low, pick, pair,
    )
    pair_in, out_in, near_in = far(far_rows), out(out_rows), near(near_rows)

    ext, back_far, back_out, back_near = call(
        rotate_rest,
        [rows_of(full)] + halo_out,
        rest_in, start_own, start_edge, ritz_top, ritz_low, pair_in, out_in, near_in, ham_top, ham_low,
    )
    far_in, out_in, near_in = far(back_far), out(back_out), near(back_near)
    base, packed, adjust = call(
        first_base,
        [rows_of(nodes), rows_of(wide), rows_of(duo)],
        ext, ham_top, ham_low, pick, pair_in, back_far,
    )
    (far_rows,) = call(fetch_far, [rows_of(duo)], packed, both, out_in, near_in)
    fetched_far = far(far_rows)
    out_rows, near_rows = call(
        fetch_ring, halo_out[1:], packed, both, far_in, out_in, near_in
    )
    fetched_out, fetched_near = out(out_rows), near(near_rows)
    first, part, known = call(
        first_own,
        [rows_of(nodes), rows_of(full), rows_of(duo)],
        base, pick, far_in, out_in, near_in, ham_top, ham_low, pair_in,
    )

    (far_rows,) = call(
        return_far, [rows_of(duo)], part, ham_top, ham_low, fetched_out, fetched_near
    )
    returned_far = far(far_rows)
    ghosts, out_rows, near_rows = call(
        return_ring,
        [rows_of(wide)] + halo_out[1:],
        part, ham_top, ham_low, fetched_far, adjust, fetched_out, fetched_near,
    )
    returned_out, returned_near = out(out_rows), near(near_rows)
    (result,) = call(
        second_base,
        [((block, nodes), F32)],
        part, ghosts, ham_top, ham_low, first, ext, known, shuffle, hits,
    )
    (result,) = call(
        finish, [((block, nodes), F32)], result, hits, returned_far, returned_out, returned_near
    )
    return result


def solution(mesh):
    in_specs = (
        P("state", "mesh"),
        P("state", None),
        P("mesh", None, None),
        P("mesh", None),
        P("mesh", None, None),
    )
    out_specs = P("state", "mesh")
    return jax.shard_map(
        per_device, mesh=mesh, in_specs=in_specs, out_specs=out_specs, check_vma=False
    )
```

```python
import jax
import jax.numpy as jnp
from jax import lax
from jax.experimental import pallas as pl
from jax.experimental.pallas import tpu as pltpu
from jax.sharding import PartitionSpec as P

F32 = jnp.float32
BF16 = jnp.bfloat16
I32 = jnp.int32
NN = ((1,), (0,))
NT = ((1,), (1,))

HALF = 1.5
CENTRE = 2.5
SIGMA_ONE = HALF / (-1.0 - CENTRE)
SIGMA_TWO = 1.0 / (2.0 / SIGMA_ONE - SIGMA_ONE)
SCALE_ONE = SIGMA_ONE / HALF
SCALE_TWO = 2.0 * SIGMA_TWO / HALF


def dot(a, b, dims=NN):
    return lax.dot_general(a, b, (dims, ((), ())), preferred_element_type=F32)


def split(x):
    top = x.astype(BF16)
    return top, (x - top.astype(F32)).astype(BF16)


def mul(a, b, dims=NN):
    return dot(a[0], b[0], dims) + (dot(a[0], b[1], dims) + dot(a[1], b[0], dims))


def sift(a, x):
    top, low = split(x)
    return dot(a, top) + dot(a, low)


def call(body, outs, *args, limit=16, **rest):
    return pl.pallas_call(
        body,
        out_shape=[jax.ShapeDtypeStruct(*out) for out in outs],
        compiler_params=pltpu.CompilerParams(vmem_limit_bytes=limit << 20),
        cost_estimate=pl.CostEstimate(flops=1000, bytes_accessed=1000, transcendentals=0),
        **rest,
    )(*args)


def column(row, width):
    down = lax.broadcasted_iota(I32, (width, width), 0)
    along = lax.broadcasted_iota(I32, (width, width), 1)
    return jnp.sum(jnp.where(down == along, row, 0), axis=1, keepdims=True)


def renumber(lists_in, subspace_in, edge_out, rest_out, shuffle_out, origin_out, lists, subspace, sems):
    slots, halo = lists.shape[1:]
    depth, nodes = subspace.shape
    wide = slots * halo
    parts = sems.shape[0] - 1
    span = depth // parts
    index_copy = pltpu.make_async_copy(lists_in, lists, sems.at[parts])
    index_copy.start()
    copies = []
    for part in range(parts):
        rows = pl.ds(part * span, span)
        copies.append(
            pltpu.make_async_copy(subspace_in.at[rows], subspace.at[rows], sems.at[part])
        )
        copies[-1].start()
    index_copy.wait()
    ids = lax.broadcasted_iota(I32, (halo, nodes), 1)
    seen = jnp.zeros((halo, nodes), F32)
    for slot in range(slots):
        sent = column(lists[0, slot : slot + 1, :], halo)
        seen = jnp.maximum(seen, jnp.where(sent == ids, 1.0, 0.0))
    edge = jnp.max(seen, axis=0, keepdims=True)
    down = lax.broadcasted_iota(I32, (nodes, nodes), 0)
    along = lax.broadcasted_iota(I32, (nodes, nodes), 1)
    upto = jnp.where(down <= along, 1.0, 0.0).astype(BF16)
    count = dot(jnp.broadcast_to(edge, (8, nodes)).astype(BF16), upto)[:1].astype(I32)
    total = jnp.sum(edge, axis=1, keepdims=True).astype(I32)
    place = jnp.where(edge > 0.5, count - 1, total + along[:1] - count)
    match = place == down
    shuffle = jnp.where(match, 1.0, 0.0).astype(BF16)
    shuffle_out[...] = shuffle
    origin_out[...] = jnp.sum(jnp.where(match, along, 0), axis=1, keepdims=True)
    for part in range(parts):
        rows = slice(part * span, (part + 1) * span)
        copies[part].wait()
        top, low = split(subspace[rows, :])
        turned = dot(top, shuffle, NT) + dot(low, shuffle, NT)
        edge_out[rows, :] = turned[:, :wide]
        rest_out[rows, :] = turned[:, wide:]


def assemble(
    odd, lists, connect, blocks, shuffle, origin, top_out, low_out, pick_out, both_out, hits_out, pair_out,
    spread, rows_top, rows_low,
):
    elems, size = connect.shape
    slots, halo = lists.shape[1:]
    nodes = origin.shape[0]
    wide = slots * halo
    duo = 2 * halo
    swap = odd[0] == 1
    columns = [column(lists[0, slot : slot + 1, :], halo) for slot in range(slots)]
    outer = jnp.where(swap, columns[0], columns[1])
    inner = jnp.where(swap, columns[1], columns[0])
    sent = jnp.concatenate([columns[2], columns[3], outer, inner], 0)
    hits = jnp.where(sent == lax.broadcasted_iota(I32, (wide, nodes), 1), 1.0, 0.0).astype(BF16)
    hits_out[...] = hits
    pick = dot(hits, shuffle[:wide, :], NT).astype(BF16)
    pick_out[...] = pick
    both = dot(pick, pick, NT)
    both_out[...] = both.astype(BF16)

    lane = lax.broadcasted_iota(I32, (halo, 1), 0)
    flag = odd[0]
    ghost = jnp.concatenate(
        [3 * halo + lane, 2 * halo + lane, (1 - flag) * halo + lane, flag * halo + lane], 0
    )
    numbers = jnp.concatenate([origin[...], nodes + ghost], 0)
    pitch = spread.shape[1] // elems
    for elem in range(elems):
        cols = slice(elem * pitch, (elem + 1) * pitch)
        wanted = jnp.pad(connect[elem : elem + 1, :], ((0, 0), (0, pitch - size)), constant_values=-1)
        chosen = jnp.where(numbers == wanted, 1.0, 0.0).astype(BF16)
        spread[:, cols] = chosen
        block = blocks[pl.ds(elem, size, stride=elems), :]
        top, low = split(jnp.pad(block, ((0, pitch - size), (0, pitch - size))))
        top, low = split(dot(top, chosen, NT) + dot(low, chosen, NT))
        rows_top[cols, :] = top
        rows_low[cols, :] = low
    ham = dot(spread[...], rows_top[...]) + dot(spread[...], rows_low[...])
    top, low = split(ham)
    top_out[...] = top
    low_out[...] = low
    far = slice(nodes, nodes + duo)
    pair_out[...] = jnp.concatenate([both[:duo, :duo], ham[far, far]], 1)


def rotate_own(group, edge, rest, ritz_in, start_out, top_out, low_out, ritz, sems):
    block, depth = ritz.shape[1:]
    groups = ritz.shape[0]
    parts = sems.shape[1]
    span = block // parts
    copies = []
    for step in range(groups):
        first = lax.rem(group[0] + groups - step, groups) * depth
        cols = pl.ds(pl.multiple_of(first, depth), depth)
        for part in range(parts):
            rows = pl.ds(part * span, span)
            copies.append(
                pltpu.make_async_copy(
                    ritz_in.at[rows, cols], ritz.at[step, rows], sems.at[step, part]
                )
            )
            copies[-1].start()
    own = split(jnp.concatenate([edge[...], rest[...]], 1))
    for step in range(groups):
        for part in range(parts):
            rows = slice(part * span, (part + 1) * span)
            copies[step * parts + part].wait()
            top, low = split(ritz[step, rows, :])
            if step == 0:
                start_out[rows, :] = mul((top, low), own)
            else:
                cols = slice((step - 1) * depth, step * depth)
                top_out[rows, cols] = top
                low_out[rows, cols] = low


def rotate(top, low, columns):
    width = columns.shape[1]
    high, rest = split(columns)
    wide = dot(top, jnp.concatenate([high, rest], 1))
    return wide[:, :width] + (wide[:, width:] + dot(low, high))


def rotate_edge(columns, start_own, top, low, pick, pair, start_out, far_out, out_out, near_out):
    edge_nodes = columns.shape[1]
    wide, block = pick.shape[0], start_own.shape[0]
    quarter = wide // 4
    start = (start_own[:, :edge_nodes] + rotate(top[...], low[...], columns[...])).T
    start_out[...] = start
    packed = sift(pick[...], start)
    far_out[:, :block] = packed[: 2 * quarter]
    far_out[:, block:] = pair[...]
    out_out[...] = packed[2 * quarter : 3 * quarter]
    near_out[...] = packed[3 * quarter :]


def first_part(start_edge, far_in, out_in, near_in, ham_top, ham_low, part_out):
    edge_nodes, block = start_edge.shape
    nodes = ham_top.shape[0] - 4 * out_in.shape[0]
    ghosts = jnp.concatenate([far_in[:, :block], out_in[...], near_in[...]], 0)
    part_out[...] = mul(
        (ham_top[:, :edge_nodes], ham_low[:, :edge_nodes]), split(start_edge[...])
    ) + mul((ham_top[:, nodes:], ham_low[:, nodes:]), split(ghosts))


def rotate_rest(
    columns, start_own, top, low, part, ham_top, ham_low, rest_out, far_out, out_out, near_out
):
    nodes = start_own.shape[1]
    edge_nodes = nodes - columns.shape[1]
    halo = out_out.shape[0]
    rest = (start_own[:, edge_nodes:] + rotate(top[...], low[...], columns[...])).T
    rest_out[...] = rest
    cols = slice(edge_nodes, nodes)
    back = part[nodes:, :] + mul((ham_top[nodes:, cols], ham_low[nodes:, cols]), split(rest))
    far_out[...] = back[: 2 * halo]
    out_out[...] = back[2 * halo : 3 * halo]
    near_out[...] = back[3 * halo :]


def first_base(
    start_edge, start_rest, part, ham_top, ham_low, pick, far_in, back_far,
    start_out, base_out, packed_out, adjust_out,
):
    nodes = ham_top.shape[0] - pick.shape[0]
    edge_nodes, block = start_edge.shape
    duo = far_in.shape[0]
    cols = slice(edge_nodes, nodes)
    start = jnp.concatenate([start_edge[...], start_rest[...]], 0)
    start_out[...] = start
    own = part[:nodes, :] + mul(
        (ham_top[:nodes, cols], ham_low[:nodes, cols]), split(start_rest[...])
    )
    base = SCALE_ONE * (own - CENTRE * start)
    base_out[...] = base
    packed_out[...] = sift(pick[...], base[:edge_nodes])
    overlap = far_in[:, block : block + duo].astype(BF16)
    adjust_out[...] = SCALE_ONE * sift(overlap, back_far[...])


def fetch_far(packed, both, out_in, near_in, far_out):
    duo = 2 * out_in.shape[0]
    back = jnp.concatenate([out_in[...], near_in[...]], 0)
    far_out[...] = packed[:duo, :] + SCALE_ONE * sift(both[:duo, duo:], back)


def fetch_ring(packed, both, far_in, out_in, near_in, out_out, near_out):
    halo = out_in.shape[0]
    back = jnp.concatenate([far_in[...], out_in[...], near_in[...]], 0)
    rows = packed[2 * halo :, :] + SCALE_ONE * sift(both[2 * halo :, :], back)
    out_out[...] = rows[:halo]
    near_out[...] = rows[halo:]


def first_own(
    base, pick, far_in, out_in, near_in, ham_top, ham_low, pair_in, first_out, part_out, known_out
):
    edge_nodes = pick.shape[1]
    nodes = base.shape[0]
    block = base.shape[1]
    duo = far_in.shape[0]
    back = jnp.concatenate([far_in[...], out_in[...], near_in[...]], 0)
    edge = base[:edge_nodes, :] + SCALE_ONE * sift(pick[...].T, back)
    first = jnp.concatenate([edge, base[edge_nodes:, :]], 0)
    first_out[...] = first
    part_out[...] = mul((ham_top[:, :nodes], ham_low[:, :nodes]), split(first))
    couple = split(pair_in[:, block + duo :])
    known_out[...] = mul(couple, split(sift(pick[:duo, :], edge)))


def return_far(part, ham_top, ham_low, out_in, near_in, far_out):
    halo = out_in.shape[0]
    nodes = part.shape[0] - 4 * halo
    far = slice(nodes, nodes + 2 * halo)
    ring = slice(nodes + 2 * halo, nodes + 4 * halo)
    ghosts = split(jnp.concatenate([out_in[...], near_in[...]], 0))
    far_out[...] = part[far, :] + mul((ham_top[far, ring], ham_low[far, ring]), ghosts)


def return_ring(
    part, ham_top, ham_low, far_in, adjust, out_in, near_in, ghosts_out, out_out, near_out
):
    halo = out_in.shape[0]
    nodes = part.shape[0] - 4 * halo
    ring = slice(nodes + 2 * halo, nodes + 4 * halo)
    ghosts = jnp.concatenate([far_in[...] + adjust[...], out_in[...], near_in[...]], 0)
    ghosts_out[...] = ghosts
    rows = part[ring, :] + mul((ham_top[ring, nodes:], ham_low[ring, nodes:]), split(ghosts))
    out_out[...] = rows[:halo]
    near_out[...] = rows[halo:]


def second_base(part, ghosts, ham_top, ham_low, first, start, known, shuffle, hits, result_out):
    nodes = first.shape[0]
    duo = known.shape[0]
    ham = (ham_top[:nodes, nodes:], ham_low[:nodes, nodes:])
    second = part[:nodes, :] + mul(ham, split(ghosts[...])) - CENTRE * first[...]
    second = SCALE_TWO * second - SIGMA_ONE * SIGMA_TWO * start[...]
    top, low = split(second.T)
    result = dot(top, shuffle[...]) + dot(low, shuffle[...])
    top, low = split(SCALE_TWO * known[...].T)
    result_out[...] = result + (dot(top, hits[:duo, :]) + dot(low, hits[:duo, :]))


def finish(result, hits, far_in, out_in, near_in, out):
    back = jnp.concatenate([far_in[...], out_in[...], near_in[...]], 0)
    top, low = split(SCALE_TWO * back.T)
    out[...] = result[...] + (dot(top, hits[...]) + dot(low, hits[...]))


def per_device(subspace, ritz, element_ham, connect, send_rows):
    depth, nodes = subspace.shape
    block = ritz.shape[0]
    slots, halo = send_rows.shape[1:]
    partitions = lax.axis_size("mesh")
    groups = lax.axis_size("state")
    across = partitions // 2
    wide = slots * halo
    duo = 2 * halo
    full = nodes + wide

    odd = (lax.axis_index("mesh") % 2).astype(I32).reshape(1)
    group = lax.axis_index("state").astype(I32).reshape(1)
    pairs_far = [(i, (i + across) % partitions) for i in range(partitions)]
    pairs_in = [(i, i ^ 1) for i in range(partitions)]
    pairs_out = [
        (i, (i + 1) % partitions if i % 2 else (i - 1) % partitions) for i in range(partitions)
    ]

    def far(rows):
        return lax.ppermute(rows, "mesh", pairs_far)

    def out(rows):
        return lax.ppermute(rows, "mesh", pairs_out)

    def near(rows):
        return lax.ppermute(rows, "mesh", pairs_in)

    def gather(rows):
        parts = [
            lax.ppermute(rows, "state", [(i, (i + step) % groups) for i in range(groups)])
            for step in range(1, groups)
        ]
        return parts[0] if len(parts) == 1 else jnp.concatenate(parts, 0)

    def rows_of(count):
        return ((count, block), F32)

    halo_out = [rows_of(duo), rows_of(halo), rows_of(halo)]
    smem = pl.BlockSpec(memory_space=pltpu.SMEM)
    vmem = pl.BlockSpec(memory_space=pltpu.VMEM)
    hbm = pl.BlockSpec(memory_space=pltpu.HBM)

    edge, rest, shuffle, origin = call(
        renumber,
        [((depth, wide), F32), ((depth, nodes - wide), F32), ((nodes, nodes), BF16), ((nodes, 1), I32)],
        send_rows, subspace,
        in_specs=[hbm, hbm],
        scratch_shapes=[
            pltpu.VMEM(send_rows.shape, I32),
            pltpu.VMEM(subspace.shape, F32),
            pltpu.SemaphoreType.DMA((5,)),
        ],
    )
    edge_in = gather(edge)
    rest_in = gather(rest)
    elems, size = connect.shape
    pitch = -(-size // 128) * 128
    blocks = jnp.transpose(element_ham, (1, 0, 2)).reshape(size * elems, size)
    ham_top, ham_low, pick, both, hits, pair = call(
        assemble,
        [
            ((full, full), BF16),
            ((full, full), BF16),
            ((wide, wide), BF16),
            ((wide, wide), BF16),
            ((wide, nodes), BF16),
            ((duo, 2 * duo), F32),
        ],
        odd, send_rows, connect, blocks, shuffle, origin,
        in_specs=[smem] + [vmem] * 5,
        scratch_shapes=[
            pltpu.VMEM((full, elems * pitch), BF16),
            pltpu.VMEM((elems * pitch, full), BF16),
            pltpu.VMEM((elems * pitch, full), BF16),
        ],
    )
    others = groups - 1
    start_own, ritz_top, ritz_low = call(
        rotate_own,
        [
            ((block, nodes), F32),
            ((block, others * depth), BF16),
            ((block, others * depth), BF16),
        ],
        group, edge, rest, ritz,
        limit=24,
        in_specs=[smem, vmem, vmem, hbm],
        scratch_shapes=[
            pltpu.VMEM((groups, block, depth), F32),
            pltpu.SemaphoreType.DMA((groups, 2)),
        ],
    )

    start_edge, far_rows, out_rows, near_rows = call(
        rotate_edge,
        [rows_of(wide), ((duo, block + 2 * duo), F32), rows_of(halo), rows_of(halo)],
        edge_in, start_own, ritz_top, ritz_low, pick, pair,
    )
    pair_in, out_in, near_in = far(far_rows), out(out_rows), near(near_rows)
    (part,) = call(
        first_part, [rows_of(full)], start_edge, pair_in, out_in, near_in, ham_top, ham_low
    )

    start_rest, back_far, back_out, back_near = call(
        rotate_rest,
        [rows_of(nodes - wide)] + halo_out,
        rest_in, start_own, ritz_top, ritz_low, part, ham_top, ham_low,
    )
    far_in, out_in, near_in = far(back_far), out(back_out), near(back_near)
    start, base, packed, adjust = call(
        first_base,
        [rows_of(nodes), rows_of(nodes), rows_of(wide), rows_of(duo)],
        start_edge, start_rest, part, ham_top, ham_low, pick, pair_in, back_far,
    )
    (far_rows,) = call(fetch_far, [rows_of(duo)], packed, both, out_in, near_in)
    fetched_far = far(far_rows)
    out_rows, near_rows = call(
        fetch_ring, halo_out[1:], packed, both, far_in, out_in, near_in
    )
    fetched_out, fetched_near = out(out_rows), near(near_rows)
    first, part, known = call(
        first_own,
        [rows_of(nodes), rows_of(full), rows_of(duo)],
        base, pick, far_in, out_in, near_in, ham_top, ham_low, pair_in,
    )

    (far_rows,) = call(
        return_far, [rows_of(duo)], part, ham_top, ham_low, fetched_out, fetched_near
    )
    returned_far = far(far_rows)
    ghosts, out_rows, near_rows = call(
        return_ring,
        [rows_of(wide)] + halo_out[1:],
        part, ham_top, ham_low, fetched_far, adjust, fetched_out, fetched_near,
    )
    returned_out, returned_near = out(out_rows), near(near_rows)
    (result,) = call(
        second_base,
        [((block, nodes), F32)],
        part, ghosts, ham_top, ham_low, first, start, known, shuffle, hits,
    )
    (result,) = call(
        finish, [((block, nodes), F32)], result, hits, returned_far, returned_out, returned_near
    )
    return result


def solution(mesh):
    in_specs = (
        P("state", "mesh"),
        P("state", None),
        P("mesh", None, None),
        P("mesh", None),
        P("mesh", None, None),
    )
    out_specs = P("state", "mesh")
    return jax.shard_map(
        per_device, mesh=mesh, in_specs=in_specs, out_specs=out_specs, check_vma=False
    )
```

```python
import jax
import jax.numpy as jnp
from jax import lax
from jax.experimental import pallas as pl
from jax.experimental.pallas import tpu as pltpu
from jax.sharding import PartitionSpec as P

F32 = jnp.float32
BF16 = jnp.bfloat16
I32 = jnp.int32
NN = ((1,), (0,))
NT = ((1,), (1,))

HALF = 1.5
CENTRE = 2.5
SIGMA_ONE = HALF / (-1.0 - CENTRE)
SIGMA_TWO = 1.0 / (2.0 / SIGMA_ONE - SIGMA_ONE)
SCALE_ONE = SIGMA_ONE / HALF
SCALE_TWO = 2.0 * SIGMA_TWO / HALF


def dot(a, b, dims=NN):
    return lax.dot_general(a, b, (dims, ((), ())), preferred_element_type=F32)


def split(x):
    top = x.astype(BF16)
    return top, (x - top.astype(F32)).astype(BF16)


def mul(a, b, dims=NN):
    return dot(a[0], b[0], dims) + (dot(a[0], b[1], dims) + dot(a[1], b[0], dims))


def sift(a, x):
    top, low = split(x)
    return dot(a, top) + dot(a, low)


def call(body, outs, *args, limit=8, **rest):
    return pl.pallas_call(
        body,
        out_shape=[jax.ShapeDtypeStruct(*out) for out in outs],
        compiler_params=pltpu.CompilerParams(vmem_limit_bytes=limit << 20),
        cost_estimate=pl.CostEstimate(flops=1000, bytes_accessed=1000, transcendentals=0),
        **rest,
    )(*args)


def in_hbm(x):
    return pltpu.with_memory_space_constraint(x, pltpu.HBM)


def column(row, width):
    down = lax.broadcasted_iota(I32, (width, width), 0)
    along = lax.broadcasted_iota(I32, (width, width), 1)
    return jnp.sum(jnp.where(down == along, row, 0), axis=1, keepdims=True)


def renumber(lists_in, subspace_in, edge_out, rest_out, shuffle_out, origin_out, lists, subspace, sems):
    slots, halo = lists.shape[1:]
    depth, nodes = subspace.shape
    wide = slots * halo
    parts = sems.shape[0] - 1
    span = depth // parts
    index_copy = pltpu.make_async_copy(lists_in, lists, sems.at[parts])
    index_copy.start()
    copies = []
    for part in range(parts):
        rows = pl.ds(part * span, span)
        copies.append(
            pltpu.make_async_copy(subspace_in.at[rows], subspace.at[rows], sems.at[part])
        )
        copies[-1].start()
    index_copy.wait()
    ids = lax.broadcasted_iota(I32, (halo, nodes), 1)
    seen = jnp.zeros((halo, nodes), F32)
    for slot in range(slots):
        sent = column(lists[0, slot : slot + 1, :], halo)
        seen = jnp.maximum(seen, jnp.where(sent == ids, 1.0, 0.0))
    edge = jnp.max(seen, axis=0, keepdims=True)
    down = lax.broadcasted_iota(I32, (nodes, nodes), 0)
    along = lax.broadcasted_iota(I32, (nodes, nodes), 1)
    upto = jnp.where(down <= along, 1.0, 0.0).astype(BF16)
    count = dot(jnp.broadcast_to(edge, (8, nodes)).astype(BF16), upto)[:1].astype(I32)
    total = jnp.sum(edge, axis=1, keepdims=True).astype(I32)
    place = jnp.where(edge > 0.5, count - 1, total + along[:1] - count)
    match = place == down
    shuffle = jnp.where(match, 1.0, 0.0).astype(BF16)
    shuffle_out[...] = shuffle
    origin_out[...] = jnp.sum(jnp.where(match, along, 0), axis=1, keepdims=True)
    for part in range(parts):
        rows = slice(part * span, (part + 1) * span)
        copies[part].wait()
        top, low = split(subspace[rows, :])
        turned = dot(top, shuffle, NT) + dot(low, shuffle, NT)
        edge_out[rows, :] = turned[:, :wide]
        rest_out[rows, :] = turned[:, wide:]


def assemble(
    odd, lists, connect, blocks_in, shuffle, origin, top_out, low_out, pick_out, both_out, hits_out, pair_out,
    blocks, sem, spread, rows_top, rows_low,
):
    copy = pltpu.make_async_copy(blocks_in, blocks, sem)
    copy.start()
    elems, size = connect.shape
    slots, halo = lists.shape[1:]
    nodes = origin.shape[0]
    wide = slots * halo
    duo = 2 * halo
    swap = odd[0] == 1
    columns = [column(lists[0, slot : slot + 1, :], halo) for slot in range(slots)]
    outer = jnp.where(swap, columns[0], columns[1])
    inner = jnp.where(swap, columns[1], columns[0])
    sent = jnp.concatenate([columns[2], columns[3], outer, inner], 0)
    hits = jnp.where(sent == lax.broadcasted_iota(I32, (wide, nodes), 1), 1.0, 0.0).astype(BF16)
    hits_out[...] = hits
    pick = dot(hits, shuffle[:wide, :], NT).astype(BF16)
    pick_out[...] = pick
    both = dot(pick, pick, NT)
    both_out[...] = both.astype(BF16)

    lane = lax.broadcasted_iota(I32, (halo, 1), 0)
    flag = odd[0]
    ghost = jnp.concatenate(
        [3 * halo + lane, 2 * halo + lane, (1 - flag) * halo + lane, flag * halo + lane], 0
    )
    numbers = jnp.concatenate([origin[...], nodes + ghost], 0)
    pitch = spread.shape[1] // elems
    copy.wait()
    for elem in range(elems):
        cols = slice(elem * pitch, (elem + 1) * pitch)
        wanted = jnp.pad(connect[elem : elem + 1, :], ((0, 0), (0, pitch - size)), constant_values=-1)
        chosen = jnp.where(numbers == wanted, 1.0, 0.0).astype(BF16)
        spread[:, cols] = chosen
        block = blocks[pl.ds(elem, size, stride=elems), :]
        top, low = split(jnp.pad(block, ((0, pitch - size), (0, pitch - size))))
        top, low = split(dot(top, chosen, NT) + dot(low, chosen, NT))
        rows_top[cols, :] = top
        rows_low[cols, :] = low
    ham = dot(spread[...], rows_top[...]) + dot(spread[...], rows_low[...])
    top, low = split(ham)
    top_out[...] = top
    low_out[...] = low
    far = slice(nodes, nodes + duo)
    pair_out[...] = jnp.concatenate([both[:duo, :duo], ham[far, far]], 1)


def rotate_own(group, edge, rest, ritz_in, start_out, top_out, low_out, ritz, sems):
    block, depth = ritz.shape[1:]
    groups = ritz.shape[0]
    parts = sems.shape[1]
    span = block // parts
    copies = []
    for step in range(groups):
        first = lax.rem(group[0] + groups - step, groups) * depth
        cols = pl.ds(pl.multiple_of(first, depth), depth)
        for part in range(parts):
            rows = pl.ds(part * span, span)
            copies.append(
                pltpu.make_async_copy(
                    ritz_in.at[rows, cols], ritz.at[step, rows], sems.at[step, part]
                )
            )
            copies[-1].start()
    own = split(jnp.concatenate([edge[...], rest[...]], 1))
    for step in range(groups):
        for part in range(parts):
            rows = slice(part * span, (part + 1) * span)
            copies[step * parts + part].wait()
            top, low = split(ritz[step, rows, :])
            if step == 0:
                start_out[rows, :] = mul((top, low), own)
            else:
                cols = slice((step - 1) * depth, step * depth)
                top_out[rows, cols] = top
                low_out[rows, cols] = low


def rotate(top, low, columns):
    width = columns.shape[1]
    high, rest = split(columns)
    wide = dot(top, jnp.concatenate([high, rest], 1))
    return wide[:, :width] + (wide[:, width:] + dot(low, high))


def rotate_edge(columns, start_own, top, low, pick, pair, start_out, far_out, out_out, near_out):
    edge_nodes = columns.shape[1]
    wide, block = pick.shape[0], start_own.shape[0]
    quarter = wide // 4
    start = (start_own[:, :edge_nodes] + rotate(top[...], low[...], columns[...])).T
    start_out[...] = start
    packed = sift(pick[...], start)
    far_out[:, :block] = packed[: 2 * quarter]
    far_out[:, block:] = pair[...]
    out_out[...] = packed[2 * quarter : 3 * quarter]
    near_out[...] = packed[3 * quarter :]


def first_part(start_edge, far_in, out_in, near_in, ham_top, ham_low, part_out):
    edge_nodes, block = start_edge.shape
    nodes = ham_top.shape[0] - 4 * out_in.shape[0]
    ghosts = jnp.concatenate([far_in[:, :block], out_in[...], near_in[...]], 0)
    part_out[...] = mul(
        (ham_top[:, :edge_nodes], ham_low[:, :edge_nodes]), split(start_edge[...])
    ) + mul((ham_top[:, nodes:], ham_low[:, nodes:]), split(ghosts))


def rotate_rest(
    columns, start_own, top, low, part, ham_top, ham_low, rest_out, far_out, out_out, near_out
):
    nodes = start_own.shape[1]
    edge_nodes = nodes - columns.shape[1]
    halo = out_out.shape[0]
    rest = (start_own[:, edge_nodes:] + rotate(top[...], low[...], columns[...])).T
    rest_out[...] = rest
    cols = slice(edge_nodes, nodes)
    back = part[nodes:, :] + mul((ham_top[nodes:, cols], ham_low[nodes:, cols]), split(rest))
    far_out[...] = back[: 2 * halo]
    out_out[...] = back[2 * halo : 3 * halo]
    near_out[...] = back[3 * halo :]


def first_base(
    start_edge, start_rest, part, ham_top, ham_low, pick, far_in, back_far,
    start_out, base_out, packed_out, adjust_out,
):
    nodes = ham_top.shape[0] - pick.shape[0]
    edge_nodes, block = start_edge.shape
    duo = far_in.shape[0]
    cols = slice(edge_nodes, nodes)
    start = jnp.concatenate([start_edge[...], start_rest[...]], 0)
    start_out[...] = start
    own = part[:nodes, :] + mul(
        (ham_top[:nodes, cols], ham_low[:nodes, cols]), split(start_rest[...])
    )
    base = SCALE_ONE * (own - CENTRE * start)
    base_out[...] = base
    packed_out[...] = sift(pick[...], base[:edge_nodes])
    overlap = far_in[:, block : block + duo].astype(BF16)
    adjust_out[...] = SCALE_ONE * sift(overlap, back_far[...])


def fetch_far(packed, both, out_in, near_in, far_out):
    duo = 2 * out_in.shape[0]
    back = jnp.concatenate([out_in[...], near_in[...]], 0)
    far_out[...] = packed[:duo, :] + SCALE_ONE * sift(both[:duo, duo:], back)


def fetch_ring(packed, both, far_in, out_in, near_in, out_out, near_out):
    halo = out_in.shape[0]
    back = jnp.concatenate([far_in[...], out_in[...], near_in[...]], 0)
    rows = packed[2 * halo :, :] + SCALE_ONE * sift(both[2 * halo :, :], back)
    out_out[...] = rows[:halo]
    near_out[...] = rows[halo:]


def first_own(
    base, pick, far_in, out_in, near_in, ham_top, ham_low, pair_in, first_out, part_out, known_out
):
    edge_nodes = pick.shape[1]
    nodes = base.shape[0]
    block = base.shape[1]
    duo = far_in.shape[0]
    back = jnp.concatenate([far_in[...], out_in[...], near_in[...]], 0)
    edge = base[:edge_nodes, :] + SCALE_ONE * sift(pick[...].T, back)
    first = jnp.concatenate([edge, base[edge_nodes:, :]], 0)
    first_out[...] = first
    part_out[...] = mul((ham_top[:, :nodes], ham_low[:, :nodes]), split(first))
    couple = split(pair_in[:, block + duo :])
    known_out[...] = mul(couple, split(sift(pick[:duo, :], edge)))


def return_far(part, ham_top, ham_low, out_in, near_in, far_out):
    halo = out_in.shape[0]
    nodes = part.shape[0] - 4 * halo
    far = slice(nodes, nodes + 2 * halo)
    ring = slice(nodes + 2 * halo, nodes + 4 * halo)
    ghosts = split(jnp.concatenate([out_in[...], near_in[...]], 0))
    far_out[...] = part[far, :] + mul((ham_top[far, ring], ham_low[far, ring]), ghosts)


def return_ring(
    part, ham_top, ham_low, far_in, adjust, out_in, near_in, ghosts_out, out_out, near_out
):
    halo = out_in.shape[0]
    nodes = part.shape[0] - 4 * halo
    ring = slice(nodes + 2 * halo, nodes + 4 * halo)
    ghosts = jnp.concatenate([far_in[...] + adjust[...], out_in[...], near_in[...]], 0)
    ghosts_out[...] = ghosts
    rows = part[ring, :] + mul((ham_top[ring, nodes:], ham_low[ring, nodes:]), split(ghosts))
    out_out[...] = rows[:halo]
    near_out[...] = rows[halo:]


def second_base(part, ghosts, ham_top, ham_low, first, start, known, shuffle, hits, result_out):
    nodes = first.shape[0]
    duo = known.shape[0]
    ham = (ham_top[:nodes, nodes:], ham_low[:nodes, nodes:])
    second = part[:nodes, :] + mul(ham, split(ghosts[...])) - CENTRE * first[...]
    second = SCALE_TWO * second - SIGMA_ONE * SIGMA_TWO * start[...]
    top, low = split(second.T)
    result = dot(top, shuffle[...]) + dot(low, shuffle[...])
    top, low = split(SCALE_TWO * known[...].T)
    result_out[...] = result + (dot(top, hits[:duo, :]) + dot(low, hits[:duo, :]))


def finish(result, hits, far_in, out_in, near_in, out):
    back = jnp.concatenate([far_in[...], out_in[...], near_in[...]], 0)
    top, low = split(SCALE_TWO * back.T)
    out[...] = result[...] + (dot(top, hits[...]) + dot(low, hits[...]))


def per_device(subspace, ritz, element_ham, connect, send_rows):
    depth, nodes = subspace.shape
    block = ritz.shape[0]
    slots, halo = send_rows.shape[1:]
    partitions = lax.axis_size("mesh")
    groups = lax.axis_size("state")
    across = partitions // 2
    wide = slots * halo
    duo = 2 * halo
    full = nodes + wide

    odd = (lax.axis_index("mesh") % 2).astype(I32).reshape(1)
    group = lax.axis_index("state").astype(I32).reshape(1)
    pairs_far = [(i, (i + across) % partitions) for i in range(partitions)]
    pairs_in = [(i, i ^ 1) for i in range(partitions)]
    pairs_out = [
        (i, (i + 1) % partitions if i % 2 else (i - 1) % partitions) for i in range(partitions)
    ]

    def far(rows):
        return lax.ppermute(rows, "mesh", pairs_far)

    def out(rows):
        return lax.ppermute(rows, "mesh", pairs_out)

    def near(rows):
        return lax.ppermute(rows, "mesh", pairs_in)

    def gather(rows):
        parts = [
            lax.ppermute(rows, "state", [(i, (i + step) % groups) for i in range(groups)])
            for step in range(1, groups)
        ]
        return parts[0] if len(parts) == 1 else jnp.concatenate(parts, 0)

    def rows_of(count):
        return ((count, block), F32)

    halo_out = [rows_of(duo), rows_of(halo), rows_of(halo)]
    smem = pl.BlockSpec(memory_space=pltpu.SMEM)
    vmem = pl.BlockSpec(memory_space=pltpu.VMEM)
    hbm = pl.BlockSpec(memory_space=pltpu.HBM)

    edge, rest, shuffle, origin = call(
        renumber,
        [((depth, wide), F32), ((depth, nodes - wide), F32), ((nodes, nodes), BF16), ((nodes, 1), I32)],
        in_hbm(send_rows), in_hbm(subspace),
        in_specs=[hbm, hbm],
        scratch_shapes=[
            pltpu.VMEM(send_rows.shape, I32),
            pltpu.VMEM(subspace.shape, F32),
            pltpu.SemaphoreType.DMA((5,)),
        ],
    )
    edge_in = gather(edge)
    rest_in = gather(rest)
    elems, size = connect.shape
    pitch = -(-size // 128) * 128
    blocks = jnp.transpose(element_ham, (1, 0, 2)).reshape(size * elems, size)
    ham_top, ham_low, pick, both, hits, pair = call(
        assemble,
        [
            ((full, full), BF16),
            ((full, full), BF16),
            ((wide, wide), BF16),
            ((wide, wide), BF16),
            ((wide, nodes), BF16),
            ((duo, 2 * duo), F32),
        ],
        odd, send_rows, connect, in_hbm(blocks), shuffle, origin,
        limit=12,
        in_specs=[smem, vmem, vmem, hbm, vmem, vmem],
        scratch_shapes=[
            pltpu.VMEM(blocks.shape, F32),
            pltpu.SemaphoreType.DMA,
            pltpu.VMEM((full, elems * pitch), BF16),
            pltpu.VMEM((elems * pitch, full), BF16),
            pltpu.VMEM((elems * pitch, full), BF16),
        ],
    )
    others = groups - 1
    start_own, ritz_top, ritz_low = call(
        rotate_own,
        [
            ((block, nodes), F32),
            ((block, others * depth), BF16),
            ((block, others * depth), BF16),
        ],
        group, edge, rest, in_hbm(ritz),
        limit=12,
        in_specs=[smem, vmem, vmem, hbm],
        scratch_shapes=[
            pltpu.VMEM((groups, block, depth), F32),
            pltpu.SemaphoreType.DMA((groups, 2)),
        ],
    )

    start_edge, far_rows, out_rows, near_rows = call(
        rotate_edge,
        [rows_of(wide), ((duo, block + 2 * duo), F32), rows_of(halo), rows_of(halo)],
        edge_in, start_own, ritz_top, ritz_low, pick, pair,
    )
    pair_in, out_in, near_in = far(far_rows), out(out_rows), near(near_rows)
    (part,) = call(
        first_part, [rows_of(full)], start_edge, pair_in, out_in, near_in, ham_top, ham_low
    )

    start_rest, back_far, back_out, back_near = call(
        rotate_rest,
        [rows_of(nodes - wide)] + halo_out,
        rest_in, start_own, ritz_top, ritz_low, part, ham_top, ham_low,
    )
    far_in, out_in, near_in = far(back_far), out(back_out), near(back_near)
    start, base, packed, adjust = call(
        first_base,
        [rows_of(nodes), rows_of(nodes), rows_of(wide), rows_of(duo)],
        start_edge, start_rest, part, ham_top, ham_low, pick, pair_in, back_far,
    )
    (far_rows,) = call(fetch_far, [rows_of(duo)], packed, both, out_in, near_in)
    fetched_far = far(far_rows)
    out_rows, near_rows = call(
        fetch_ring, halo_out[1:], packed, both, far_in, out_in, near_in
    )
    fetched_out, fetched_near = out(out_rows), near(near_rows)
    first, part, known = call(
        first_own,
        [rows_of(nodes), rows_of(full), rows_of(duo)],
        base, pick, far_in, out_in, near_in, ham_top, ham_low, pair_in,
    )

    (far_rows,) = call(
        return_far, [rows_of(duo)], part, ham_top, ham_low, fetched_out, fetched_near
    )
    returned_far = far(far_rows)
    ghosts, out_rows, near_rows = call(
        return_ring,
        [rows_of(wide)] + halo_out[1:],
        part, ham_top, ham_low, fetched_far, adjust, fetched_out, fetched_near,
    )
    returned_out, returned_near = out(out_rows), near(near_rows)
    (result,) = call(
        second_base,
        [((block, nodes), F32)],
        part, ghosts, ham_top, ham_low, first, start, known, shuffle, hits,
    )
    (result,) = call(
        finish, [((block, nodes), F32)], result, hits, returned_far, returned_out, returned_near
    )
    return result


def solution(mesh):
    in_specs = (
        P("state", "mesh"),
        P("state", None),
        P("mesh", None, None),
        P("mesh", None),
        P("mesh", None, None),
    )
    out_specs = P("state", "mesh")
    return jax.shard_map(
        per_device, mesh=mesh, in_specs=in_specs, out_specs=out_specs, check_vma=False
    )
```

```python
import functools

import jax
import jax.numpy as jnp
from jax import lax
from jax.experimental import pallas as pl
from jax.experimental.pallas import tpu as pltpu
from jax.sharding import PartitionSpec as P

F32 = jnp.float32
BF16 = jnp.bfloat16
I32 = jnp.int32
NN = ((1,), (0,))
NT = ((1,), (1,))

HALF = 1.5
CENTRE = 2.5
SIGMA_ONE = HALF / (-1.0 - CENTRE)
SIGMA_TWO = 1.0 / (2.0 / SIGMA_ONE - SIGMA_ONE)
SCALE_ONE = SIGMA_ONE / HALF
SCALE_TWO = 2.0 * SIGMA_TWO / HALF


def dot(a, b, dims=NN):
    return lax.dot_general(a, b, (dims, ((), ())), preferred_element_type=F32)


def split(x):
    top = x.astype(BF16)
    return top, (x - top.astype(F32)).astype(BF16)


def mul(a, b, dims=NN):
    return dot(a[0], b[0], dims) + (dot(a[0], b[1], dims) + dot(a[1], b[0], dims))


def sift(a, x):
    top, low = split(x)
    return dot(a, top) + dot(a, low)


def call(body, outs, *args, limit=8, kept=False, **rest):
    return pl.pallas_call(
        body,
        out_shape=[pltpu.VMEM(*out) if kept else jax.ShapeDtypeStruct(*out) for out in outs],
        compiler_params=pltpu.CompilerParams(vmem_limit_bytes=limit << 20),
        cost_estimate=pl.CostEstimate(flops=1000, bytes_accessed=1000, transcendentals=0),
        **rest,
    )(*args)


def in_hbm(x):
    return pltpu.with_memory_space_constraint(x, pltpu.HBM)


def in_vmem(x):
    return pltpu.with_memory_space_constraint(x, pltpu.VMEM)


def column(row, width):
    down = lax.broadcasted_iota(I32, (width, width), 0)
    along = lax.broadcasted_iota(I32, (width, width), 1)
    return jnp.sum(jnp.where(down == along, row, 0), axis=1, keepdims=True)


def renumber(
    lists_in, subspace_in, far_out, ring_out, low_out, high_out, shuffle_out, origin_out, lists, subspace, sems
):
    slots, halo = lists.shape[1:]
    depth, nodes = subspace.shape
    duo = 2 * halo
    span = depth // 2
    index_copy = pltpu.make_async_copy(lists_in, lists, sems.at[0])
    index_copy.start()
    copy = pltpu.make_async_copy(subspace_in, subspace, sems.at[1])
    copy.start()
    index_copy.wait()
    ids = lax.broadcasted_iota(I32, (halo, nodes), 1)
    seen = []
    for slot in range(slots):
        sent = column(lists[0, slot : slot + 1, :], halo)
        seen.append(jnp.where(sent == ids, 1.0, 0.0))
    far = jnp.max(jnp.maximum(seen[2], seen[3]), axis=0, keepdims=True)
    ring = jnp.max(jnp.maximum(seen[0], seen[1]), axis=0, keepdims=True) * (1.0 - far)
    down = lax.broadcasted_iota(I32, (nodes, nodes), 0)
    along = lax.broadcasted_iota(I32, (nodes, nodes), 1)
    upto = jnp.where(down <= along, 1.0, 0.0).astype(BF16)
    flags = jnp.concatenate([far, ring, jnp.zeros((6, nodes), F32)], 0)
    counts = dot(flags.astype(BF16), upto).astype(I32)
    far_count, ring_count = counts[0:1], counts[1:2]
    totals = jnp.sum(flags, axis=1, keepdims=True).astype(I32)
    far_total, ring_total = totals[0:1], totals[1:2]
    place = jnp.where(
        far > 0.5,
        far_count - 1,
        jnp.where(
            ring > 0.5,
            far_total + ring_count - 1,
            far_total + ring_total + along[:1] - far_count - ring_count,
        ),
    )
    match = place == down
    shuffle = jnp.where(match, 1.0, 0.0).astype(BF16)
    shuffle_out[...] = shuffle
    origin_out[...] = jnp.sum(jnp.where(match, along, 0), axis=1, keepdims=True)
    copy.wait()
    halves = []
    for part, rest_out in enumerate((low_out, high_out)):
        top, low = split(subspace[part * span : (part + 1) * span, :])
        turned = dot(top, shuffle, NT) + dot(low, shuffle, NT)
        rest_out[...] = turned[:, 2 * duo :]
        halves.append(turned)
    far_out[...] = jnp.concatenate([half[:, :duo] for half in halves], 1)
    ring_out[...] = jnp.concatenate([half[:, duo : 2 * duo] for half in halves], 1)


def assemble(
    odd, lists, connect, blocks_in, shuffle, origin, top_out, low_out, pick_out, both_out, hits_out, pair_out,
    blocks, sem, spread, rows_top, rows_low,
):
    copy = pltpu.make_async_copy(blocks_in, blocks, sem)
    copy.start()
    elems, size = connect.shape
    slots, halo = lists.shape[1:]
    nodes = origin.shape[0]
    wide = slots * halo
    duo = 2 * halo
    swap = odd[0] == 1
    columns = [column(lists[0, slot : slot + 1, :], halo) for slot in range(slots)]
    outer = jnp.where(swap, columns[0], columns[1])
    inner = jnp.where(swap, columns[1], columns[0])
    sent = jnp.concatenate([columns[2], columns[3], outer, inner], 0)
    hits = jnp.where(sent == lax.broadcasted_iota(I32, (wide, nodes), 1), 1.0, 0.0).astype(BF16)
    hits_out[...] = hits
    pick = dot(hits, shuffle[:wide, :], NT).astype(BF16)
    pick_out[...] = pick
    both = dot(pick, pick, NT)
    both_out[...] = both.astype(BF16)

    lane = lax.broadcasted_iota(I32, (halo, 1), 0)
    flag = odd[0]
    ghost = jnp.concatenate(
        [3 * halo + lane, 2 * halo + lane, (1 - flag) * halo + lane, flag * halo + lane], 0
    )
    numbers = jnp.concatenate([origin[...], nodes + ghost], 0)
    pitch = spread.shape[1] // elems
    copy.wait()
    for elem in range(elems):
        cols = slice(elem * pitch, (elem + 1) * pitch)
        wanted = jnp.pad(connect[elem : elem + 1, :], ((0, 0), (0, pitch - size)), constant_values=-1)
        chosen = jnp.where(numbers == wanted, 1.0, 0.0).astype(BF16)
        spread[:, cols] = chosen
        block = blocks[pl.ds(elem, size, stride=elems), :]
        top, low = split(jnp.pad(block, ((0, pitch - size), (0, pitch - size))))
        top, low = split(dot(top, chosen, NT) + dot(low, chosen, NT))
        rows_top[cols, :] = top
        rows_low[cols, :] = low
    ham = dot(spread[...], rows_top[...]) + dot(spread[...], rows_low[...])
    top, low = split(ham)
    top_out[...] = top
    low_out[...] = low
    far = slice(nodes, nodes + duo)
    pair_out[...] = jnp.concatenate([both[:duo, :duo], ham[far, far]], 1)


def rotate_own(group, far, ring, low_rest, high_rest, ritz_in, start_out, top_out, low_out, ritz, sems):
    block, depth = ritz.shape[1:]
    groups = ritz.shape[0]
    parts = sems.shape[1]
    span = block // parts
    copies = []
    for step in range(groups):
        first = lax.rem(group[0] + groups - step, groups) * depth
        cols = pl.ds(pl.multiple_of(first, depth), depth)
        for part in range(parts):
            rows = pl.ds(part * span, span)
            copies.append(
                pltpu.make_async_copy(
                    ritz_in.at[rows, cols], ritz.at[step, rows], sems.at[step, part]
                )
            )
            copies[-1].start()
    width = far.shape[1] // 2
    columns = [jnp.concatenate([x[:, :width], x[:, width:]], 0) for x in (far, ring)]
    rest = jnp.concatenate([low_rest[...], high_rest[...]], 0)
    own = split(jnp.concatenate(columns + [rest], 1))
    for step in range(groups):
        for part in range(parts):
            rows = slice(part * span, (part + 1) * span)
            copies[step * parts + part].wait()
            top, low = split(ritz[step, rows, :])
            if step == 0:
                start_out[rows, :] = mul((top, low), own)
            else:
                cols = slice((step - 1) * depth, step * depth)
                top_out[rows, cols] = top
                low_out[rows, cols] = low


def rotate(top, low, columns):
    width = columns.shape[1]
    high, rest = split(columns)
    wide = dot(top, jnp.concatenate([high, rest], 1))
    return wide[:, :width] + (wide[:, width:] + dot(low, high))


def pieces(x, groups, part, axis):
    span = x.shape[axis] // (2 * (groups - 1))
    starts = [(2 * step + part) * span for step in range(groups - 1)]
    if axis == 0:
        return [x[start : start + span, :] for start in starts]
    return [x[:, start : start + span] for start in starts]


def rotate_sides(columns, top, low, groups):
    width = columns.shape[1] // 2
    span = columns.shape[0] // (groups - 1)
    whole = jnp.concatenate(
        [
            columns[step * span : (step + 1) * span, part * width : (part + 1) * width]
            for step in range(groups - 1)
            for part in range(2)
        ],
        0,
    )
    return rotate(top[...], low[...], whole)


def rotate_half(columns, top, low, groups, part):
    return rotate(
        jnp.concatenate(pieces(top, groups, part, 1), 1),
        jnp.concatenate(pieces(low, groups, part, 1), 1),
        columns[...],
    )


def rotate_far(groups, columns, start_own, top, low, pick, start_out, far_out):
    duo = far_out.shape[0]
    start = (start_own[:, :duo] + rotate_sides(columns, top, low, groups)).T
    start_out[...] = start
    far_out[...] = sift(pick[:duo, :duo], start)


def rotate_ring(groups, columns, start_own, start_far, top, low, pick, start_out, out_out, near_out):
    halo = out_out.shape[0]
    duo = 2 * halo
    start = (start_own[:, duo : 2 * duo] + rotate_sides(columns, top, low, groups)).T
    start = jnp.concatenate([start_far[...], start], 0)
    start_out[...] = start
    packed = sift(pick[duo:, :], start)
    out_out[...] = packed[:halo]
    near_out[...] = packed[halo:]


def rotate_low(groups, columns, start_own, top, low, rest_out):
    edge_nodes = start_own.shape[1] - columns.shape[1]
    rest_out[...] = start_own[:, edge_nodes:] + rotate_half(columns, top, low, groups, 0)


def first_part(start_edge, far_in, out_in, near_in, ham_top, ham_low, pair_in, part_out, overlap_out, couple_out):
    edge_nodes = start_edge.shape[0]
    nodes = ham_top.shape[0] - 4 * out_in.shape[0]
    duo = far_in.shape[0]
    ghosts = jnp.concatenate([far_in[...], out_in[...], near_in[...]], 0)
    part_out[...] = mul(
        (ham_top[:, :edge_nodes], ham_low[:, :edge_nodes]), split(start_edge[...])
    ) + mul((ham_top[:, nodes:], ham_low[:, nodes:]), split(ghosts))
    overlap_out[...] = SCALE_ONE * pair_in[:, :duo]
    couple_out[...] = pair_in[:, duo:]


def rotate_rest(
    groups, columns, rest_low, top, low, part, ham_top, ham_low, rest_out, far_out, out_out, near_out
):
    rest = (rest_low[...] + rotate_half(columns, top, low, groups, 1)).T
    rest_out[...] = rest
    halo = out_out.shape[0]
    edge_nodes, width = part.shape[0] - 4 * halo - rest.shape[0], rest.shape[0]
    nodes = edge_nodes + width
    cols = slice(edge_nodes, nodes)
    back = part[nodes:, :] + mul((ham_top[nodes:, cols], ham_low[nodes:, cols]), split(rest))
    far_out[...] = back[: 2 * halo]
    out_out[...] = back[2 * halo : 3 * halo]
    near_out[...] = back[3 * halo :]


def first_base(
    start_edge, start_rest, part, ham_top, ham_low, pick, overlap, back_far,
    start_out, base_out, packed_out, adjust_out,
):
    nodes = ham_top.shape[0] - pick.shape[0]
    edge_nodes = start_edge.shape[0]
    cols = slice(edge_nodes, nodes)
    start = jnp.concatenate([start_edge[...], start_rest[...]], 0)
    start_out[...] = start
    own = part[:nodes, :] + mul(
        (ham_top[:nodes, cols], ham_low[:nodes, cols]), split(start_rest[...])
    )
    base = SCALE_ONE * (own - CENTRE * start)
    base_out[...] = base
    packed_out[...] = sift(pick[...], base[:edge_nodes])
    adjust_out[...] = mul(split(overlap[...]), split(back_far[...]))


def fetch_far(packed, both, out_in, near_in, far_out):
    duo = 2 * out_in.shape[0]
    back = jnp.concatenate([out_in[...], near_in[...]], 0)
    far_out[...] = packed[:duo, :] + SCALE_ONE * sift(both[:duo, duo:], back)


def fetch_ring(packed, both, far_in, out_in, near_in, out_out, near_out):
    halo = out_in.shape[0]
    back = jnp.concatenate([far_in[...], out_in[...], near_in[...]], 0)
    rows = packed[2 * halo :, :] + SCALE_ONE * sift(both[2 * halo :, :], back)
    out_out[...] = rows[:halo]
    near_out[...] = rows[halo:]


def first_own(
    base, pick, far_in, out_in, near_in, ham_top, ham_low, couple, first_out, part_out, known_out
):
    edge_nodes = pick.shape[1]
    nodes = base.shape[0]
    duo = far_in.shape[0]
    back = jnp.concatenate([far_in[...], out_in[...], near_in[...]], 0)
    edge = base[:edge_nodes, :] + SCALE_ONE * sift(pick[...].T, back)
    first = jnp.concatenate([edge, base[edge_nodes:, :]], 0)
    first_out[...] = first
    part_out[...] = mul((ham_top[:, :nodes], ham_low[:, :nodes]), split(first))
    known_out[...] = mul(split(couple[...]), split(sift(pick[:duo, :], edge)))


def return_far(part, ham_top, ham_low, out_in, near_in, far_out):
    halo = out_in.shape[0]
    nodes = part.shape[0] - 4 * halo
    far = slice(nodes, nodes + 2 * halo)
    ring = slice(nodes + 2 * halo, nodes + 4 * halo)
    ghosts = split(jnp.concatenate([out_in[...], near_in[...]], 0))
    far_out[...] = part[far, :] + mul((ham_top[far, ring], ham_low[far, ring]), ghosts)


def return_ring(
    part, ham_top, ham_low, far_in, adjust, out_in, near_in, ghosts_out, out_out, near_out
):
    halo = out_in.shape[0]
    nodes = part.shape[0] - 4 * halo
    ring = slice(nodes + 2 * halo, nodes + 4 * halo)
    ghosts = jnp.concatenate([far_in[...] + adjust[...], out_in[...], near_in[...]], 0)
    ghosts_out[...] = ghosts
    rows = part[ring, :] + mul((ham_top[ring, nodes:], ham_low[ring, nodes:]), split(ghosts))
    out_out[...] = rows[:halo]
    near_out[...] = rows[halo:]


def second_base(part, ghosts, ham_top, ham_low, first, start, known, shuffle, hits, result_out):
    nodes = first.shape[0]
    duo = known.shape[0]
    ham = (ham_top[:nodes, nodes:], ham_low[:nodes, nodes:])
    second = part[:nodes, :] + mul(ham, split(ghosts[...])) - CENTRE * first[...]
    second = SCALE_TWO * second - SIGMA_ONE * SIGMA_TWO * start[...]
    top, low = split(second.T)
    result = dot(top, shuffle[...]) + dot(low, shuffle[...])
    top, low = split(SCALE_TWO * known[...].T)
    result_out[...] = result + (dot(top, hits[:duo, :]) + dot(low, hits[:duo, :]))


def finish(result, hits, far_in, out_in, near_in, out):
    back = jnp.concatenate([far_in[...], out_in[...], near_in[...]], 0)
    top, low = split(SCALE_TWO * back.T)
    out[...] = result[...] + (dot(top, hits[...]) + dot(low, hits[...]))


def per_device(subspace, ritz, element_ham, connect, send_rows):
    depth, nodes = subspace.shape
    block = ritz.shape[0]
    slots, halo = send_rows.shape[1:]
    partitions = lax.axis_size("mesh")
    groups = lax.axis_size("state")
    across = partitions // 2
    wide = slots * halo
    duo = 2 * halo
    full = nodes + wide

    odd = (lax.axis_index("mesh") % 2).astype(I32).reshape(1)
    group = lax.axis_index("state").astype(I32).reshape(1)
    pairs_far = [(i, (i + across) % partitions) for i in range(partitions)]
    pairs_in = [(i, i ^ 1) for i in range(partitions)]
    pairs_out = [
        (i, (i + 1) % partitions if i % 2 else (i - 1) % partitions) for i in range(partitions)
    ]

    def far(rows):
        return lax.ppermute(rows, "mesh", pairs_far)

    def out(rows):
        return lax.ppermute(rows, "mesh", pairs_out)

    def near(rows):
        return lax.ppermute(rows, "mesh", pairs_in)

    def gather(rows):
        parts = [
            lax.ppermute(rows, "state", [(i, (i + step) % groups) for i in range(groups)])
            for step in range(1, groups)
        ]
        return parts[0] if len(parts) == 1 else jnp.concatenate(parts, 0)

    def rows_of(count):
        return ((count, block), F32)

    halo_out = [rows_of(duo), rows_of(halo), rows_of(halo)]
    smem = pl.BlockSpec(memory_space=pltpu.SMEM)
    vmem = pl.BlockSpec(memory_space=pltpu.VMEM)
    hbm = pl.BlockSpec(memory_space=pltpu.HBM)

    far_cols, ring_cols, low_cols, high_cols, shuffle, origin = call(
        renumber,
        [
            ((depth // 2, 2 * duo), F32),
            ((depth // 2, 2 * duo), F32),
            ((depth // 2, nodes - wide), F32),
            ((depth // 2, nodes - wide), F32),
            ((nodes, nodes), BF16),
            ((nodes, 1), I32),
        ],
        in_hbm(send_rows), in_hbm(subspace),
        kept=True,
        in_specs=[hbm, hbm],
        scratch_shapes=[
            pltpu.VMEM(send_rows.shape, I32),
            pltpu.VMEM(subspace.shape, F32),
            pltpu.SemaphoreType.DMA((2,)),
        ],
    )
    far_cols_in = gather(far_cols)
    ring_cols_in = gather(ring_cols)
    low_cols_in = gather(low_cols)
    high_cols_in = gather(high_cols)
    elems, size = connect.shape
    pitch = -(-size // 128) * 128
    blocks = jnp.transpose(element_ham, (1, 0, 2)).reshape(size * elems, size)
    ham_top, ham_low, pick, both, hits, pair = call(
        assemble,
        [
            ((full, full), BF16),
            ((full, full), BF16),
            ((wide, wide), BF16),
            ((wide, wide), BF16),
            ((wide, nodes), BF16),
            ((duo, 2 * duo), F32),
        ],
        odd, send_rows, connect, in_hbm(blocks), shuffle, origin,
        limit=12,
        in_specs=[smem, vmem, vmem, hbm, vmem, vmem],
        scratch_shapes=[
            pltpu.VMEM(blocks.shape, F32),
            pltpu.SemaphoreType.DMA,
            pltpu.VMEM((full, elems * pitch), BF16),
            pltpu.VMEM((elems * pitch, full), BF16),
            pltpu.VMEM((elems * pitch, full), BF16),
        ],
    )
    pair_in = far(pair)
    others = groups - 1
    start_own, ritz_top, ritz_low = call(
        rotate_own,
        [
            ((block, nodes), F32),
            ((block, others * depth), BF16),
            ((block, others * depth), BF16),
        ],
        group, far_cols, ring_cols, low_cols, high_cols, in_hbm(ritz),
        limit=12,
        in_specs=[smem, vmem, vmem, vmem, vmem, hbm],
        scratch_shapes=[
            pltpu.VMEM((groups, block, depth), F32),
            pltpu.SemaphoreType.DMA((groups, 2)),
        ],
    )

    start_far, far_rows = call(
        functools.partial(rotate_far, groups),
        [rows_of(duo), rows_of(duo)],
        in_vmem(far_cols_in), start_own, ritz_top, ritz_low, pick,
    )
    far_in = far(far_rows)
    start_edge, out_rows, near_rows = call(
        functools.partial(rotate_ring, groups),
        [rows_of(wide), rows_of(halo), rows_of(halo)],
        in_vmem(ring_cols_in), start_own, start_far, ritz_top, ritz_low, pick,
    )
    out_in, near_in = out(out_rows), near(near_rows)
    part, overlap, couple = call(
        first_part,
        [rows_of(full), ((duo, duo), F32), ((duo, duo), F32)],
        start_edge, far_in, out_in, near_in, ham_top, ham_low, pair_in,
    )
    (rest_low,) = call(
        functools.partial(rotate_low, groups),
        [((block, nodes - wide), F32)],
        in_vmem(low_cols_in), start_own, ritz_top, ritz_low,
    )

    start_rest, back_far, back_out, back_near = call(
        functools.partial(rotate_rest, groups),
        [rows_of(nodes - wide)] + halo_out,
        in_vmem(high_cols_in), rest_low, ritz_top, ritz_low, part, ham_top, ham_low,
    )
    far_in, out_in, near_in = far(back_far), out(back_out), near(back_near)
    start, base, packed, adjust = call(
        first_base,
        [rows_of(nodes), rows_of(nodes), rows_of(wide), rows_of(duo)],
        start_edge, start_rest, part, ham_top, ham_low, pick, overlap, back_far,
    )
    (far_rows,) = call(fetch_far, [rows_of(duo)], packed, both, out_in, near_in)
    fetched_far = far(far_rows)
    out_rows, near_rows = call(
        fetch_ring, halo_out[1:], packed, both, far_in, out_in, near_in
    )
    fetched_out, fetched_near = out(out_rows), near(near_rows)
    first, part, known = call(
        first_own,
        [rows_of(nodes), rows_of(full), rows_of(duo)],
        base, pick, far_in, out_in, near_in, ham_top, ham_low, couple,
    )

    (far_rows,) = call(
        return_far, [rows_of(duo)], part, ham_top, ham_low, fetched_out, fetched_near
    )
    returned_far = far(far_rows)
    ghosts, out_rows, near_rows = call(
        return_ring,
        [rows_of(wide)] + halo_out[1:],
        part, ham_top, ham_low, fetched_far, adjust, fetched_out, fetched_near,
    )
    returned_out, returned_near = out(out_rows), near(near_rows)
    (result,) = call(
        second_base,
        [((block, nodes), F32)],
        part, ghosts, ham_top, ham_low, first, start, known, shuffle, hits,
    )
    (result,) = call(
        finish, [((block, nodes), F32)], result, hits, returned_far, returned_out, returned_near
    )
    return result


def solution(mesh):
    in_specs = (
        P("state", "mesh"),
        P("state", None),
        P("mesh", None, None),
        P("mesh", None),
        P("mesh", None, None),
    )
    out_specs = P("state", "mesh")
    return jax.shard_map(
        per_device, mesh=mesh, in_specs=in_specs, out_specs=out_specs, check_vma=False
    )
```

```python
import functools

import jax
import jax.numpy as jnp
from jax import lax
from jax.experimental import pallas as pl
from jax.experimental.pallas import tpu as pltpu
from jax.sharding import PartitionSpec as P

F32 = jnp.float32
BF16 = jnp.bfloat16
I32 = jnp.int32
NN = ((1,), (0,))
NT = ((1,), (1,))

HALF = 1.5
CENTRE = 2.5
SIGMA_ONE = HALF / (-1.0 - CENTRE)
SIGMA_TWO = 1.0 / (2.0 / SIGMA_ONE - SIGMA_ONE)
SCALE_ONE = SIGMA_ONE / HALF
SCALE_TWO = 2.0 * SIGMA_TWO / HALF


def dot(a, b, dims=NN):
    return lax.dot_general(a, b, (dims, ((), ())), preferred_element_type=F32)


def split(x):
    top = x.astype(BF16)
    return top, (x - top.astype(F32)).astype(BF16)


def mul(a, b, dims=NN):
    return dot(a[0], b[0], dims) + (dot(a[0], b[1], dims) + dot(a[1], b[0], dims))


def sift(a, x):
    top, low = split(x)
    return dot(a, top) + dot(a, low)


def call(body, outs, *args, limit=8, kept=False, **rest):
    return pl.pallas_call(
        body,
        out_shape=[pltpu.VMEM(*out) if kept else jax.ShapeDtypeStruct(*out) for out in outs],
        compiler_params=pltpu.CompilerParams(vmem_limit_bytes=limit << 20),
        cost_estimate=pl.CostEstimate(flops=1000, bytes_accessed=1000, transcendentals=0),
        **rest,
    )(*args)


def in_hbm(x):
    return pltpu.with_memory_space_constraint(x, pltpu.HBM)


def in_vmem(x):
    return pltpu.with_memory_space_constraint(x, pltpu.VMEM)


def column(row, width):
    down = lax.broadcasted_iota(I32, (width, width), 0)
    along = lax.broadcasted_iota(I32, (width, width), 1)
    return jnp.sum(jnp.where(down == along, row, 0), axis=1, keepdims=True)


def renumber(
    lists_in, subspace_in, far_out, ring_out, low_out, high_out, shuffle_out, lists, subspace, sems
):
    slots, halo = lists.shape[1:]
    depth, nodes = subspace.shape
    duo = 2 * halo
    span = depth // 2
    index_copy = pltpu.make_async_copy(lists_in, lists, sems.at[0])
    index_copy.start()
    copy = pltpu.make_async_copy(subspace_in, subspace, sems.at[1])
    copy.start()
    index_copy.wait()
    ids = lax.broadcasted_iota(I32, (halo, nodes), 1)
    seen = []
    for slot in range(slots):
        sent = column(lists[0, slot : slot + 1, :], halo)
        seen.append(jnp.where(sent == ids, 1.0, 0.0))
    far = jnp.max(jnp.maximum(seen[2], seen[3]), axis=0, keepdims=True)
    ring = jnp.max(jnp.maximum(seen[0], seen[1]), axis=0, keepdims=True) * (1.0 - far)
    down = lax.broadcasted_iota(I32, (nodes, nodes), 0)
    along = lax.broadcasted_iota(I32, (nodes, nodes), 1)
    upto = jnp.where(down <= along, 1.0, 0.0).astype(BF16)
    flags = jnp.concatenate([far, ring, jnp.zeros((6, nodes), F32)], 0)
    counts = dot(flags.astype(BF16), upto).astype(I32)
    far_count, ring_count = counts[0:1], counts[1:2]
    totals = jnp.sum(flags, axis=1, keepdims=True).astype(I32)
    far_total, ring_total = totals[0:1], totals[1:2]
    place = jnp.where(
        far > 0.5,
        far_count - 1,
        jnp.where(
            ring > 0.5,
            far_total + ring_count - 1,
            far_total + ring_total + along[:1] - far_count - ring_count,
        ),
    )
    match = place == down
    shuffle = jnp.where(match, 1.0, 0.0).astype(BF16)
    shuffle_out[...] = shuffle
    copy.wait()
    halves = []
    for part, rest_out in enumerate((low_out, high_out)):
        rows = slice(part * span, (part + 1) * span)
        top, low = split(subspace[rows, :])
        turned = dot(top, shuffle, NT) + dot(low, shuffle, NT)
        rest_out[...] = turned[:, 2 * duo :]
        halves.append(turned)
    far_out[...] = jnp.concatenate([half[:, :duo] for half in halves], 1)
    ring_out[...] = jnp.concatenate([half[:, duo : 2 * duo] for half in halves], 1)


def list_hits(sent, nodes):
    ids = lax.broadcasted_iota(I32, (sent.shape[0], nodes), 1)
    return jnp.where(sent == ids, 1.0, 0.0).astype(BF16)


def assemble(
    odd, lists, connect, blocks_in, shuffle, _, top_out, low_out, pick_out, both_out, hits_out, pair_out,
    blocks, sem, spread, rows_top, rows_low,
):
    copy = pltpu.make_async_copy(blocks_in, blocks, sem)
    copy.start()
    elems, size = connect.shape
    slots, halo = lists.shape[1:]
    nodes = shuffle.shape[0]
    wide = slots * halo
    duo = 2 * halo
    swap = odd[0] == 1
    columns = [column(lists[0, slot : slot + 1, :], halo) for slot in range(slots)]
    outer = jnp.where(swap, columns[0], columns[1])
    inner = jnp.where(swap, columns[1], columns[0])
    sent = jnp.concatenate([columns[2], columns[3], outer, inner], 0)
    hits = list_hits(sent, nodes)
    hits_out[...] = hits
    pick = dot(hits, shuffle[:wide, :], NT).astype(BF16)
    pick_out[...] = pick
    both = dot(pick, pick, NT)
    both_out[...] = both.astype(BF16)

    lane = lax.broadcasted_iota(I32, (halo, 1), 0)
    flag = odd[0]
    ghost = jnp.concatenate(
        [3 * halo + lane, 2 * halo + lane, (1 - flag) * halo + lane, flag * halo + lane], 0
    )
    along = lax.broadcasted_iota(I32, (nodes, nodes), 1).astype(F32)
    origin = jnp.sum(along * shuffle[...].astype(F32), axis=1, keepdims=True).astype(I32)
    numbers = jnp.concatenate([origin, nodes + ghost], 0)
    pitch = spread.shape[1] // elems
    copy.wait()
    for elem in range(elems):
        cols = slice(elem * pitch, (elem + 1) * pitch)
        wanted = jnp.pad(connect[elem : elem + 1, :], ((0, 0), (0, pitch - size)), constant_values=-1)
        chosen = jnp.where(numbers == wanted, 1.0, 0.0).astype(BF16)
        spread[:, cols] = chosen
        block = blocks[pl.ds(elem, size, stride=elems), :]
        top, low = split(jnp.pad(block, ((0, pitch - size), (0, pitch - size))))
        top, low = split(dot(top, chosen, NT) + dot(low, chosen, NT))
        rows_top[cols, :] = top
        rows_low[cols, :] = low
    ham = dot(spread[...], rows_top[...]) + dot(spread[...], rows_low[...])
    top, low = split(ham)
    top_out[...] = top
    low_out[...] = low
    far = slice(nodes, nodes + duo)
    pair_out[...] = jnp.concatenate([both[:duo, :duo], ham[far, far]], 1)


def rotate_own(group, far, ring, low_rest, high_rest, ritz_in, start_out, top_out, low_out, ritz, sems):
    block, depth = ritz.shape[1:]
    groups = ritz.shape[0]
    parts = sems.shape[1]
    span = block // parts
    copies = []
    for step in range(groups):
        first = lax.rem(group[0] + groups - step, groups) * depth
        cols = pl.ds(pl.multiple_of(first, depth), depth)
        for part in range(parts):
            rows = pl.ds(part * span, span)
            copies.append(
                pltpu.make_async_copy(
                    ritz_in.at[rows, cols], ritz.at[step, rows], sems.at[step, part]
                )
            )
            copies[-1].start()
    width = far.shape[1] // 2
    columns = [jnp.concatenate([x[:, :width], x[:, width:]], 0) for x in (far, ring)]
    rest = jnp.concatenate([low_rest[...], high_rest[...]], 0)
    own = split(jnp.concatenate(columns + [rest], 1))
    for step in range(groups):
        for part in range(parts):
            rows = slice(part * span, (part + 1) * span)
            copies[step * parts + part].wait()
            top, low = split(ritz[step, rows, :])
            if step == 0:
                start_out[rows, :] = mul((top, low), own)
            else:
                cols = slice((step - 1) * depth, step * depth)
                top_out[rows, cols] = top
                low_out[rows, cols] = low


def rotate(top, low, columns):
    width = columns.shape[1]
    high, rest = split(columns)
    wide = dot(top, jnp.concatenate([high, rest], 1))
    return wide[:, :width] + (wide[:, width:] + dot(low, high))


def pieces(x, groups, part, axis):
    span = x.shape[axis] // (2 * (groups - 1))
    starts = [(2 * step + part) * span for step in range(groups - 1)]
    if axis == 0:
        return [x[start : start + span, :] for start in starts]
    return [x[:, start : start + span] for start in starts]


def rotate_sides(columns, top, low, groups):
    width = columns.shape[1] // 2
    span = columns.shape[0] // (groups - 1)
    whole = jnp.concatenate(
        [
            columns[step * span : (step + 1) * span, part * width : (part + 1) * width]
            for step in range(groups - 1)
            for part in range(2)
        ],
        0,
    )
    return rotate(top[...], low[...], whole)


def rotate_half(columns, top, low, groups, part):
    return rotate(
        jnp.concatenate(pieces(top, groups, part, 1), 1),
        jnp.concatenate(pieces(low, groups, part, 1), 1),
        columns[...],
    )


def rotate_far(groups, columns, start_own, top, low, lists, shuffle, start_out, far_out):
    duo = far_out.shape[0]
    halo = duo // 2
    sent = [column(lists[0, slot : slot + 1, :], halo) for slot in (2, 3)]
    hits = list_hits(jnp.concatenate(sent, 0), shuffle.shape[0])
    pick = dot(hits, shuffle[:duo, :], NT).astype(BF16)
    start = (start_own[:, :duo] + rotate_sides(columns, top, low, groups)).T
    start_out[...] = start
    far_out[...] = sift(pick, start)


def rotate_ring(groups, columns, start_own, start_far, top, low, pick, start_out, out_out, near_out):
    halo = out_out.shape[0]
    duo = 2 * halo
    start = (start_own[:, duo : 2 * duo] + rotate_sides(columns, top, low, groups)).T
    start = jnp.concatenate([start_far[...], start], 0)
    start_out[...] = start
    packed = sift(pick[duo:, :], start)
    out_out[...] = packed[:halo]
    near_out[...] = packed[halo:]


def rotate_low(groups, columns, start_own, top, low, rest_out):
    edge_nodes = start_own.shape[1] - columns.shape[1]
    rest_out[...] = start_own[:, edge_nodes:] + rotate_half(columns, top, low, groups, 0)


def first_part(start_edge, far_in, out_in, near_in, ham_top, ham_low, pair_in, part_out, overlap_out, couple_out):
    edge_nodes = start_edge.shape[0]
    nodes = ham_top.shape[0] - 4 * out_in.shape[0]
    duo = far_in.shape[0]
    ghosts = jnp.concatenate([far_in[...], out_in[...], near_in[...]], 0)
    part_out[...] = mul(
        (ham_top[:, :edge_nodes], ham_low[:, :edge_nodes]), split(start_edge[...])
    ) + mul((ham_top[:, nodes:], ham_low[:, nodes:]), split(ghosts))
    overlap_out[...] = SCALE_ONE * pair_in[:, :duo]
    couple_out[...] = pair_in[:, duo:]


def rotate_rest(
    groups, columns, rest_low, top, low, part, ham_top, ham_low, rest_out, far_out, out_out, near_out
):
    rest = (rest_low[...] + rotate_half(columns, top, low, groups, 1)).T
    rest_out[...] = rest
    halo = out_out.shape[0]
    edge_nodes, width = part.shape[0] - 4 * halo - rest.shape[0], rest.shape[0]
    nodes = edge_nodes + width
    cols = slice(edge_nodes, nodes)
    back = part[nodes:, :] + mul((ham_top[nodes:, cols], ham_low[nodes:, cols]), split(rest))
    far_out[...] = back[: 2 * halo]
    out_out[...] = back[2 * halo : 3 * halo]
    near_out[...] = back[3 * halo :]


def first_base(
    start_edge, start_rest, part, ham_top, ham_low, pick, overlap, back_far,
    start_out, base_out, packed_out, adjust_out,
):
    nodes = ham_top.shape[0] - pick.shape[0]
    edge_nodes = start_edge.shape[0]
    cols = slice(edge_nodes, nodes)
    start = jnp.concatenate([start_edge[...], start_rest[...]], 0)
    start_out[...] = start
    own = part[:nodes, :] + mul(
        (ham_top[:nodes, cols], ham_low[:nodes, cols]), split(start_rest[...])
    )
    base = SCALE_ONE * (own - CENTRE * start)
    base_out[...] = base
    packed_out[...] = sift(pick[...], base[:edge_nodes])
    adjust_out[...] = mul(split(overlap[...]), split(back_far[...]))


def fetch_far(packed, both, out_in, near_in, far_out):
    duo = 2 * out_in.shape[0]
    back = jnp.concatenate([out_in[...], near_in[...]], 0)
    far_out[...] = packed[:duo, :] + SCALE_ONE * sift(both[:duo, duo:], back)


def fetch_ring(packed, both, far_in, out_in, near_in, out_out, near_out):
    halo = out_in.shape[0]
    back = jnp.concatenate([far_in[...], out_in[...], near_in[...]], 0)
    rows = packed[2 * halo :, :] + SCALE_ONE * sift(both[2 * halo :, :], back)
    out_out[...] = rows[:halo]
    near_out[...] = rows[halo:]


def first_own(
    base, pick, far_in, out_in, near_in, ham_top, ham_low, couple, first_out, part_out, known_out
):
    edge_nodes = pick.shape[1]
    nodes = base.shape[0]
    duo = far_in.shape[0]
    back = jnp.concatenate([far_in[...], out_in[...], near_in[...]], 0)
    edge = base[:edge_nodes, :] + SCALE_ONE * sift(pick[...].T, back)
    first = jnp.concatenate([edge, base[edge_nodes:, :]], 0)
    first_out[...] = first
    part_out[...] = mul((ham_top[:, :nodes], ham_low[:, :nodes]), split(first))
    known_out[...] = mul(split(couple[...]), split(sift(pick[:duo, :], edge)))


def return_far(part, ham_top, ham_low, out_in, near_in, far_out):
    halo = out_in.shape[0]
    nodes = part.shape[0] - 4 * halo
    far = slice(nodes, nodes + 2 * halo)
    ring = slice(nodes + 2 * halo, nodes + 4 * halo)
    ghosts = split(jnp.concatenate([out_in[...], near_in[...]], 0))
    far_out[...] = part[far, :] + mul((ham_top[far, ring], ham_low[far, ring]), ghosts)


def return_ring(
    part, ham_top, ham_low, far_in, adjust, out_in, near_in, ghosts_out, out_out, near_out
):
    halo = out_in.shape[0]
    nodes = part.shape[0] - 4 * halo
    ring = slice(nodes + 2 * halo, nodes + 4 * halo)
    ghosts = jnp.concatenate([far_in[...] + adjust[...], out_in[...], near_in[...]], 0)
    ghosts_out[...] = ghosts
    rows = part[ring, :] + mul((ham_top[ring, nodes:], ham_low[ring, nodes:]), split(ghosts))
    out_out[...] = rows[:halo]
    near_out[...] = rows[halo:]


def second_base(part, ghosts, ham_top, ham_low, first, start, known, shuffle, hits, result_out):
    nodes = first.shape[0]
    duo = known.shape[0]
    ham = (ham_top[:nodes, nodes:], ham_low[:nodes, nodes:])
    second = part[:nodes, :] + mul(ham, split(ghosts[...])) - CENTRE * first[...]
    second = SCALE_TWO * second - SIGMA_ONE * SIGMA_TWO * start[...]
    top, low = split(second.T)
    result = dot(top, shuffle[...]) + dot(low, shuffle[...])
    top, low = split(SCALE_TWO * known[...].T)
    result_out[...] = result + (dot(top, hits[:duo, :]) + dot(low, hits[:duo, :]))


def finish(result, hits, far_in, out_in, near_in, out):
    back = jnp.concatenate([far_in[...], out_in[...], near_in[...]], 0)
    top, low = split(SCALE_TWO * back.T)
    out[...] = result[...] + (dot(top, hits[...]) + dot(low, hits[...]))


def per_device(subspace, ritz, element_ham, connect, send_rows):
    depth, nodes = subspace.shape
    block = ritz.shape[0]
    slots, halo = send_rows.shape[1:]
    partitions = lax.axis_size("mesh")
    groups = lax.axis_size("state")
    across = partitions // 2
    wide = slots * halo
    duo = 2 * halo
    full = nodes + wide

    odd = (lax.axis_index("mesh") % 2).astype(I32).reshape(1)
    group = lax.axis_index("state").astype(I32).reshape(1)
    pairs_far = [(i, (i + across) % partitions) for i in range(partitions)]
    pairs_in = [(i, i ^ 1) for i in range(partitions)]
    pairs_out = [
        (i, (i + 1) % partitions if i % 2 else (i - 1) % partitions) for i in range(partitions)
    ]

    def far(rows):
        return lax.ppermute(rows, "mesh", pairs_far)

    def out(rows):
        return lax.ppermute(rows, "mesh", pairs_out)

    def near(rows):
        return lax.ppermute(rows, "mesh", pairs_in)

    def gather(rows):
        parts = [
            lax.ppermute(rows, "state", [(i, (i + step) % groups) for i in range(groups)])
            for step in range(1, groups)
        ]
        return parts[0] if len(parts) == 1 else jnp.concatenate(parts, 0)

    def rows_of(count):
        return ((count, block), F32)

    halo_out = [rows_of(duo), rows_of(halo), rows_of(halo)]
    smem = pl.BlockSpec(memory_space=pltpu.SMEM)
    vmem = pl.BlockSpec(memory_space=pltpu.VMEM)
    hbm = pl.BlockSpec(memory_space=pltpu.HBM)

    far_cols, ring_cols, low_cols, high_cols, shuffle = call(
        renumber,
        [
            ((depth // 2, 2 * duo), F32),
            ((depth // 2, 2 * duo), F32),
            ((depth // 2, nodes - wide), F32),
            ((depth // 2, nodes - wide), F32),
            ((nodes, nodes), BF16),
        ],
        in_hbm(send_rows), in_hbm(subspace),
        kept=True,
        in_specs=[hbm, hbm],
        scratch_shapes=[
            pltpu.VMEM(send_rows.shape, I32),
            pltpu.VMEM(subspace.shape, F32),
            pltpu.SemaphoreType.DMA((2,)),
        ],
    )
    far_cols_in = gather(far_cols)
    ring_cols_in = gather(ring_cols)
    low_cols_in = gather(low_cols)
    high_cols_in = gather(high_cols)
    others = groups - 1
    start_own, ritz_top, ritz_low = call(
        rotate_own,
        [
            ((block, nodes), F32),
            ((block, others * depth), BF16),
            ((block, others * depth), BF16),
        ],
        group, far_cols, ring_cols, low_cols, high_cols, in_hbm(ritz),
        limit=12,
        in_specs=[smem, vmem, vmem, vmem, vmem, hbm],
        scratch_shapes=[
            pltpu.VMEM((groups, block, depth), F32),
            pltpu.SemaphoreType.DMA((groups, 2)),
        ],
    )

    start_far, far_rows = call(
        functools.partial(rotate_far, groups),
        [rows_of(duo), rows_of(duo)],
        in_vmem(far_cols_in), start_own, ritz_top, ritz_low, send_rows, shuffle,
    )
    far_in = far(far_rows)
    elems, size = connect.shape
    pitch = -(-size // 128) * 128
    blocks = jnp.transpose(element_ham, (1, 0, 2)).reshape(size * elems, size)
    ham_top, ham_low, pick, both, hits, pair = call(
        assemble,
        [
            ((full, full), BF16),
            ((full, full), BF16),
            ((wide, wide), BF16),
            ((wide, wide), BF16),
            ((wide, nodes), BF16),
            ((duo, 2 * duo), F32),
        ],
        odd, send_rows, connect, in_hbm(blocks), shuffle, start_far,
        limit=12,
        in_specs=[smem, vmem, vmem, hbm, vmem, vmem],
        scratch_shapes=[
            pltpu.VMEM(blocks.shape, F32),
            pltpu.SemaphoreType.DMA,
            pltpu.VMEM((full, elems * pitch), BF16),
            pltpu.VMEM((elems * pitch, full), BF16),
            pltpu.VMEM((elems * pitch, full), BF16),
        ],
    )
    pair_in = far(pair)
    start_edge, out_rows, near_rows = call(
        functools.partial(rotate_ring, groups),
        [rows_of(wide), rows_of(halo), rows_of(halo)],
        in_vmem(ring_cols_in), start_own, start_far, ritz_top, ritz_low, pick,
    )
    out_in, near_in = out(out_rows), near(near_rows)
    part, overlap, couple = call(
        first_part,
        [rows_of(full), ((duo, duo), F32), ((duo, duo), F32)],
        start_edge, far_in, out_in, near_in, ham_top, ham_low, pair_in,
    )
    (rest_low,) = call(
        functools.partial(rotate_low, groups),
        [((block, nodes - wide), F32)],
        in_vmem(low_cols_in), start_own, ritz_top, ritz_low,
    )

    start_rest, back_far, back_out, back_near = call(
        functools.partial(rotate_rest, groups),
        [rows_of(nodes - wide)] + halo_out,
        in_vmem(high_cols_in), rest_low, ritz_top, ritz_low, part, ham_top, ham_low,
    )
    far_in, out_in, near_in = far(back_far), out(back_out), near(back_near)
    start, base, packed, adjust = call(
        first_base,
        [rows_of(nodes), rows_of(nodes), rows_of(wide), rows_of(duo)],
        start_edge, start_rest, part, ham_top, ham_low, pick, overlap, back_far,
    )
    (far_rows,) = call(fetch_far, [rows_of(duo)], packed, both, out_in, near_in)
    fetched_far = far(far_rows)
    out_rows, near_rows = call(
        fetch_ring, halo_out[1:], packed, both, far_in, out_in, near_in
    )
    fetched_out, fetched_near = out(out_rows), near(near_rows)
    first, part, known = call(
        first_own,
        [rows_of(nodes), rows_of(full), rows_of(duo)],
        base, pick, far_in, out_in, near_in, ham_top, ham_low, couple,
    )

    (far_rows,) = call(
        return_far, [rows_of(duo)], part, ham_top, ham_low, fetched_out, fetched_near
    )
    returned_far = far(far_rows)
    ghosts, out_rows, near_rows = call(
        return_ring,
        [rows_of(wide)] + halo_out[1:],
        part, ham_top, ham_low, fetched_far, adjust, fetched_out, fetched_near,
    )
    returned_out, returned_near = out(out_rows), near(near_rows)
    (result,) = call(
        second_base,
        [((block, nodes), F32)],
        part, ghosts, ham_top, ham_low, first, start, known, shuffle, hits,
    )
    (result,) = call(
        finish, [((block, nodes), F32)], result, hits, returned_far, returned_out, returned_near
    )
    return result


def solution(mesh):
    in_specs = (
        P("state", "mesh"),
        P("state", None),
        P("mesh", None, None),
        P("mesh", None),
        P("mesh", None, None),
    )
    out_specs = P("state", "mesh")
    return jax.shard_map(
        per_device, mesh=mesh, in_specs=in_specs, out_specs=out_specs, check_vma=False
    )
```

```python
import functools

import jax
import jax.numpy as jnp
from jax import lax
from jax.experimental import pallas as pl
from jax.experimental.pallas import tpu as pltpu
from jax.sharding import PartitionSpec as P

F32 = jnp.float32
BF16 = jnp.bfloat16
I32 = jnp.int32
NN = ((1,), (0,))
NT = ((1,), (1,))

HALF = 1.5
CENTRE = 2.5
SIGMA_ONE = HALF / (-1.0 - CENTRE)
SIGMA_TWO = 1.0 / (2.0 / SIGMA_ONE - SIGMA_ONE)
SCALE_ONE = SIGMA_ONE / HALF
SCALE_TWO = 2.0 * SIGMA_TWO / HALF


def dot(a, b, dims=NN):
    return lax.dot_general(a, b, (dims, ((), ())), preferred_element_type=F32)


def split(x):
    top = x.astype(BF16)
    return top, (x - top.astype(F32)).astype(BF16)


def mul(a, b, dims=NN):
    return dot(a[0], b[0], dims) + (dot(a[0], b[1], dims) + dot(a[1], b[0], dims))


def sift(a, x):
    top, low = split(x)
    return dot(a, top) + dot(a, low)


def call(body, outs, *args, limit=8, kept=False, **rest):
    return pl.pallas_call(
        body,
        out_shape=[pltpu.VMEM(*out) if kept else jax.ShapeDtypeStruct(*out) for out in outs],
        compiler_params=pltpu.CompilerParams(vmem_limit_bytes=limit << 20),
        cost_estimate=pl.CostEstimate(flops=1000, bytes_accessed=1000, transcendentals=0),
        **rest,
    )(*args)


def in_hbm(x):
    return pltpu.with_memory_space_constraint(x, pltpu.HBM)


def in_vmem(x):
    return pltpu.with_memory_space_constraint(x, pltpu.VMEM)


def column(row, width):
    down = lax.broadcasted_iota(I32, (width, width), 0)
    along = lax.broadcasted_iota(I32, (width, width), 1)
    return jnp.sum(jnp.where(down == along, row, 0), axis=1, keepdims=True)


def renumber(
    lists_in, subspace_in, far_out, ring_out, low_out, high_out, shuffle_out, lists, subspace, sems
):
    slots, halo = lists.shape[1:]
    depth, nodes = subspace.shape
    duo = 2 * halo
    span = depth // 2
    index_copy = pltpu.make_async_copy(lists_in, lists, sems.at[0])
    index_copy.start()
    copy = pltpu.make_async_copy(subspace_in, subspace, sems.at[1])
    copy.start()
    index_copy.wait()
    ids = lax.broadcasted_iota(I32, (halo, nodes), 1)
    seen = []
    for slot in range(slots):
        sent = column(lists[0, slot : slot + 1, :], halo)
        seen.append(jnp.where(sent == ids, 1.0, 0.0))
    far = jnp.max(jnp.maximum(seen[2], seen[3]), axis=0, keepdims=True)
    ring = jnp.max(jnp.maximum(seen[0], seen[1]), axis=0, keepdims=True) * (1.0 - far)
    down = lax.broadcasted_iota(I32, (nodes, nodes), 0)
    along = lax.broadcasted_iota(I32, (nodes, nodes), 1)
    upto = jnp.where(down <= along, 1.0, 0.0).astype(BF16)
    flags = jnp.concatenate([far, ring, jnp.zeros((6, nodes), F32)], 0)
    counts = dot(flags.astype(BF16), upto).astype(I32)
    far_count, ring_count = counts[0:1], counts[1:2]
    totals = jnp.sum(flags, axis=1, keepdims=True).astype(I32)
    far_total, ring_total = totals[0:1], totals[1:2]
    place = jnp.where(
        far > 0.5,
        far_count - 1,
        jnp.where(
            ring > 0.5,
            far_total + ring_count - 1,
            far_total + ring_total + along[:1] - far_count - ring_count,
        ),
    )
    match = place == down
    shuffle = jnp.where(match, 1.0, 0.0).astype(BF16)
    shuffle_out[...] = shuffle
    copy.wait()
    halves = []
    for part, rest_out in enumerate((low_out, high_out)):
        rows = slice(part * span, (part + 1) * span)
        top, low = split(subspace[rows, :])
        turned = dot(top, shuffle, NT) + dot(low, shuffle, NT)
        rest_out[...] = turned[:, 2 * duo :]
        halves.append(turned)
    far_out[...] = jnp.concatenate([half[:, :duo] for half in halves], 1)
    ring_out[...] = jnp.concatenate([half[:, duo : 2 * duo] for half in halves], 1)


def list_hits(sent, nodes):
    ids = lax.broadcasted_iota(I32, (sent.shape[0], nodes), 1)
    return jnp.where(sent == ids, 1.0, 0.0).astype(BF16)


def assemble(
    odd, lists, connect, blocks_in, shuffle, _, top_out, low_out, pick_out, both_out, hits_out, pair_out,
    blocks, sem, spread, rows_top, rows_low,
):
    copy = pltpu.make_async_copy(blocks_in, blocks, sem)
    copy.start()
    elems, size = connect.shape
    slots, halo = lists.shape[1:]
    nodes = shuffle.shape[0]
    wide = slots * halo
    duo = 2 * halo
    swap = odd[0] == 1
    columns = [column(lists[0, slot : slot + 1, :], halo) for slot in range(slots)]
    outer = jnp.where(swap, columns[0], columns[1])
    inner = jnp.where(swap, columns[1], columns[0])
    sent = jnp.concatenate([columns[2], columns[3], outer, inner], 0)
    hits = list_hits(sent, nodes)
    hits_out[...] = hits
    pick = dot(hits, shuffle[:wide, :], NT).astype(BF16)
    pick_out[...] = pick
    both = dot(pick, pick, NT)
    both_out[...] = both.astype(BF16)

    lane = lax.broadcasted_iota(I32, (halo, 1), 0)
    flag = odd[0]
    ghost = jnp.concatenate(
        [3 * halo + lane, 2 * halo + lane, (1 - flag) * halo + lane, flag * halo + lane], 0
    )
    along = lax.broadcasted_iota(I32, (nodes, nodes), 1).astype(F32)
    origin = jnp.sum(along * shuffle[...].astype(F32), axis=1, keepdims=True).astype(I32)
    numbers = jnp.concatenate([origin, nodes + ghost], 0)
    pitch = spread.shape[1] // elems
    copy.wait()
    for elem in range(elems):
        cols = slice(elem * pitch, (elem + 1) * pitch)
        wanted = jnp.pad(connect[elem : elem + 1, :], ((0, 0), (0, pitch - size)), constant_values=-1)
        chosen = jnp.where(numbers == wanted, 1.0, 0.0).astype(BF16)
        spread[:, cols] = chosen
        block = blocks[pl.ds(elem, size, stride=elems), :]
        top, low = split(jnp.pad(block, ((0, pitch - size), (0, pitch - size))))
        top, low = split(dot(top, chosen, NT) + dot(low, chosen, NT))
        rows_top[cols, :] = top
        rows_low[cols, :] = low
    ham = dot(spread[...], rows_top[...]) + dot(spread[...], rows_low[...])
    top, low = split(ham)
    top_out[...] = top
    low_out[...] = low
    far = slice(nodes, nodes + duo)
    pair_out[...] = jnp.concatenate([both[:duo, :duo], ham[far, far]], 1)


def rotate_own(group, far, ring, low_rest, high_rest, ritz_in, start_out, top_out, low_out, ritz, sems):
    block, depth = ritz.shape[1:]
    groups = ritz.shape[0]
    parts = sems.shape[1]
    span = block // parts
    copies = []
    for step in range(groups):
        first = lax.rem(group[0] + groups - step, groups) * depth
        cols = pl.ds(pl.multiple_of(first, depth), depth)
        for part in range(parts):
            rows = pl.ds(part * span, span)
            copies.append(
                pltpu.make_async_copy(
                    ritz_in.at[rows, cols], ritz.at[step, rows], sems.at[step, part]
                )
            )
            copies[-1].start()
    width = far.shape[1] // 2
    columns = [jnp.concatenate([x[:, :width], x[:, width:]], 0) for x in (far, ring)]
    rest = jnp.concatenate([low_rest[...], high_rest[...]], 0)
    own = split(jnp.concatenate(columns + [rest], 1))
    for step in range(groups):
        for part in range(parts):
            rows = slice(part * span, (part + 1) * span)
            copies[step * parts + part].wait()
            top, low = split(ritz[step, rows, :])
            if step == 0:
                start_out[rows, :] = mul((top, low), own)
            else:
                cols = slice((step - 1) * depth, step * depth)
                top_out[rows, cols] = top
                low_out[rows, cols] = low


def rotate(top, low, columns):
    width = columns.shape[1]
    high, rest = split(columns)
    wide = dot(top, jnp.concatenate([high, rest], 1))
    return wide[:, :width] + (wide[:, width:] + dot(low, high))


def pieces(x, groups, part, axis):
    span = x.shape[axis] // (2 * (groups - 1))
    starts = [(2 * step + part) * span for step in range(groups - 1)]
    if axis == 0:
        return [x[start : start + span, :] for start in starts]
    return [x[:, start : start + span] for start in starts]


def rotate_sides(columns, top, low, groups):
    width = columns.shape[1] // 2
    span = columns.shape[0] // (groups - 1)
    whole = jnp.concatenate(
        [
            columns[step * span : (step + 1) * span, part * width : (part + 1) * width]
            for step in range(groups - 1)
            for part in range(2)
        ],
        0,
    )
    return rotate(top[...], low[...], whole)


def rotate_half(columns, top, low, groups, part):
    return rotate(
        jnp.concatenate(pieces(top, groups, part, 1), 1),
        jnp.concatenate(pieces(low, groups, part, 1), 1),
        columns[...],
    )


def rotate_far(groups, columns, start_own, top, low, lists, shuffle, start_out, far_out):
    duo = far_out.shape[0]
    halo = duo // 2
    sent = [column(lists[0, slot : slot + 1, :], halo) for slot in (2, 3)]
    hits = list_hits(jnp.concatenate(sent, 0), shuffle.shape[0])
    pick = dot(hits, shuffle[:duo, :], NT).astype(BF16)
    start = (start_own[:, :duo] + rotate_sides(columns, top, low, groups)).T
    start_out[...] = start
    far_out[...] = sift(pick, start)


def rotate_ring(groups, columns, start_own, start_far, top, low, pick, start_out, out_out, near_out):
    halo = out_out.shape[0]
    duo = 2 * halo
    start = (start_own[:, duo : 2 * duo] + rotate_sides(columns, top, low, groups)).T
    start = jnp.concatenate([start_far[...], start], 0)
    start_out[...] = start
    packed = sift(pick[duo:, :], start)
    out_out[...] = packed[:halo]
    near_out[...] = packed[halo:]


def rotate_low(groups, columns, start_own, top, low, rest_out):
    edge_nodes = start_own.shape[1] - columns.shape[1]
    rest_out[...] = start_own[:, edge_nodes:] + rotate_half(columns, top, low, groups, 0)


def first_part(start_edge, far_in, out_in, near_in, ham_top, ham_low, part_out):
    edge_nodes = start_edge.shape[0]
    nodes = ham_top.shape[0] - 4 * out_in.shape[0]
    ghosts = jnp.concatenate([far_in[...], out_in[...], near_in[...]], 0)
    part_out[...] = mul(
        (ham_top[:, :edge_nodes], ham_low[:, :edge_nodes]), split(start_edge[...])
    ) + mul((ham_top[:, nodes:], ham_low[:, nodes:]), split(ghosts))


def rotate_rest(
    groups, columns, rest_low, top, low, part, ham_top, ham_low, rest_out, far_out, out_out, near_out
):
    rest = (rest_low[...] + rotate_half(columns, top, low, groups, 1)).T
    rest_out[...] = rest
    halo = out_out.shape[0]
    edge_nodes, width = part.shape[0] - 4 * halo - rest.shape[0], rest.shape[0]
    nodes = edge_nodes + width
    cols = slice(edge_nodes, nodes)
    back = part[nodes:, :] + mul((ham_top[nodes:, cols], ham_low[nodes:, cols]), split(rest))
    far_out[...] = back[: 2 * halo]
    out_out[...] = back[2 * halo : 3 * halo]
    near_out[...] = back[3 * halo :]


def first_base(
    start_edge, start_rest, part, ham_top, ham_low, pick, start_out, base_out, packed_out
):
    nodes = ham_top.shape[0] - pick.shape[0]
    edge_nodes = start_edge.shape[0]
    cols = slice(edge_nodes, nodes)
    start = jnp.concatenate([start_edge[...], start_rest[...]], 0)
    start_out[...] = start
    own = part[:nodes, :] + mul(
        (ham_top[:nodes, cols], ham_low[:nodes, cols]), split(start_rest[...])
    )
    base = SCALE_ONE * (own - CENTRE * start)
    base_out[...] = base
    packed_out[...] = sift(pick[...], base[:edge_nodes])


def fetch_far(packed, both, pair, out_in, near_in, far_out):
    duo = 2 * out_in.shape[0]
    block = packed.shape[1]
    back = jnp.concatenate([out_in[...], near_in[...]], 0)
    far_out[:, block:] = pair[...]
    far_out[:, :block] = packed[:duo, :] + SCALE_ONE * sift(both[:duo, duo:], back)


def fetch_ring(packed, both, far_in, out_in, near_in, out_out, near_out):
    halo = out_in.shape[0]
    back = jnp.concatenate([far_in[...], out_in[...], near_in[...]], 0)
    rows = packed[2 * halo :, :] + SCALE_ONE * sift(both[2 * halo :, :], back)
    out_out[...] = rows[:halo]
    near_out[...] = rows[halo:]


def first_own(
    base, pick, far_in, out_in, near_in, ham_top, ham_low, first_out, part_out, picked_out
):
    edge_nodes = pick.shape[1]
    nodes = base.shape[0]
    duo = far_in.shape[0]
    back = jnp.concatenate([far_in[...], out_in[...], near_in[...]], 0)
    edge = base[:edge_nodes, :] + SCALE_ONE * sift(pick[...].T, back)
    first = jnp.concatenate([edge, base[edge_nodes:, :]], 0)
    first_out[...] = first
    part_out[...] = mul((ham_top[:, :nodes], ham_low[:, :nodes]), split(first))
    picked_out[...] = sift(pick[:duo, :], edge)


def return_far(part, ham_top, ham_low, out_in, near_in, far_out):
    halo = out_in.shape[0]
    nodes = part.shape[0] - 4 * halo
    far = slice(nodes, nodes + 2 * halo)
    ring = slice(nodes + 2 * halo, nodes + 4 * halo)
    ghosts = split(jnp.concatenate([out_in[...], near_in[...]], 0))
    far_out[...] = part[far, :] + mul((ham_top[far, ring], ham_low[far, ring]), ghosts)


def return_ring(
    part, ham_top, ham_low, far_in, back_far, out_in, near_in, ghosts_out, out_out, near_out
):
    halo = out_in.shape[0]
    nodes = part.shape[0] - 4 * halo
    ring = slice(nodes + 2 * halo, nodes + 4 * halo)
    duo, block = back_far.shape
    overlap = far_in[:, block : block + duo].astype(BF16)
    far = far_in[:, :block] + SCALE_ONE * sift(overlap, back_far[...])
    ghosts = jnp.concatenate([far, out_in[...], near_in[...]], 0)
    ghosts_out[...] = ghosts
    rows = part[ring, :] + mul((ham_top[ring, nodes:], ham_low[ring, nodes:]), split(ghosts))
    out_out[...] = rows[:halo]
    near_out[...] = rows[halo:]


def second_base(
    part, ghosts, ham_top, ham_low, first, start, picked, far_in, shuffle, hits, result_out
):
    nodes = first.shape[0]
    duo, block = picked.shape
    known = mul(split(far_in[:, block + duo :]), split(picked[...]))
    ham = (ham_top[:nodes, nodes:], ham_low[:nodes, nodes:])
    second = part[:nodes, :] + mul(ham, split(ghosts[...])) - CENTRE * first[...]
    second = SCALE_TWO * second - SIGMA_ONE * SIGMA_TWO * start[...]
    top, low = split(second.T)
    result = dot(top, shuffle[...]) + dot(low, shuffle[...])
    top, low = split(SCALE_TWO * known.T)
    result_out[...] = result + (dot(top, hits[:duo, :]) + dot(low, hits[:duo, :]))


def finish(result, hits, far_in, out_in, near_in, out):
    back = jnp.concatenate([far_in[...], out_in[...], near_in[...]], 0)
    top, low = split(SCALE_TWO * back.T)
    out[...] = result[...] + (dot(top, hits[...]) + dot(low, hits[...]))


def per_device(subspace, ritz, element_ham, connect, send_rows):
    depth, nodes = subspace.shape
    block = ritz.shape[0]
    slots, halo = send_rows.shape[1:]
    partitions = lax.axis_size("mesh")
    groups = lax.axis_size("state")
    across = partitions // 2
    wide = slots * halo
    duo = 2 * halo
    full = nodes + wide

    odd = (lax.axis_index("mesh") % 2).astype(I32).reshape(1)
    group = lax.axis_index("state").astype(I32).reshape(1)
    pairs_far = [(i, (i + across) % partitions) for i in range(partitions)]
    pairs_in = [(i, i ^ 1) for i in range(partitions)]
    pairs_out = [
        (i, (i + 1) % partitions if i % 2 else (i - 1) % partitions) for i in range(partitions)
    ]

    def far(rows):
        return lax.ppermute(rows, "mesh", pairs_far)

    def out(rows):
        return lax.ppermute(rows, "mesh", pairs_out)

    def near(rows):
        return lax.ppermute(rows, "mesh", pairs_in)

    def gather(rows):
        parts = [
            lax.ppermute(rows, "state", [(i, (i + step) % groups) for i in range(groups)])
            for step in range(1, groups)
        ]
        return parts[0] if len(parts) == 1 else jnp.concatenate(parts, 0)

    def rows_of(count):
        return ((count, block), F32)

    halo_out = [rows_of(duo), rows_of(halo), rows_of(halo)]
    smem = pl.BlockSpec(memory_space=pltpu.SMEM)
    vmem = pl.BlockSpec(memory_space=pltpu.VMEM)
    hbm = pl.BlockSpec(memory_space=pltpu.HBM)

    far_cols, ring_cols, low_cols, high_cols, shuffle = call(
        renumber,
        [
            ((depth // 2, 2 * duo), F32),
            ((depth // 2, 2 * duo), F32),
            ((depth // 2, nodes - wide), F32),
            ((depth // 2, nodes - wide), F32),
            ((nodes, nodes), BF16),
        ],
        in_hbm(send_rows), in_hbm(subspace),
        kept=True,
        in_specs=[hbm, hbm],
        scratch_shapes=[
            pltpu.VMEM(send_rows.shape, I32),
            pltpu.VMEM(subspace.shape, F32),
            pltpu.SemaphoreType.DMA((2,)),
        ],
    )
    far_cols_in = gather(far_cols)
    ring_cols_in = gather(ring_cols)
    low_cols_in = gather(low_cols)
    high_cols_in = gather(high_cols)
    others = groups - 1
    start_own, ritz_top, ritz_low = call(
        rotate_own,
        [
            ((block, nodes), F32),
            ((block, others * depth), BF16),
            ((block, others * depth), BF16),
        ],
        group, far_cols, ring_cols, low_cols, high_cols, in_hbm(ritz),
        limit=12,
        in_specs=[smem, vmem, vmem, vmem, vmem, hbm],
        scratch_shapes=[
            pltpu.VMEM((groups, block, depth), F32),
            pltpu.SemaphoreType.DMA((groups, 2)),
        ],
    )

    start_far, far_rows = call(
        functools.partial(rotate_far, groups),
        [rows_of(duo), rows_of(duo)],
        in_vmem(far_cols_in), start_own, ritz_top, ritz_low, send_rows, shuffle,
    )
    far_in = far(far_rows)
    elems, size = connect.shape
    pitch = -(-size // 128) * 128
    blocks = jnp.transpose(element_ham, (1, 0, 2)).reshape(size * elems, size)
    ham_top, ham_low, pick, both, hits, pair = call(
        assemble,
        [
            ((full, full), BF16),
            ((full, full), BF16),
            ((wide, wide), BF16),
            ((wide, wide), BF16),
            ((wide, nodes), BF16),
            ((duo, 2 * duo), F32),
        ],
        odd, send_rows, connect, in_hbm(blocks), shuffle, start_far,
        limit=12,
        in_specs=[smem, vmem, vmem, hbm, vmem, vmem],
        scratch_shapes=[
            pltpu.VMEM(blocks.shape, F32),
            pltpu.SemaphoreType.DMA,
            pltpu.VMEM((full, elems * pitch), BF16),
            pltpu.VMEM((elems * pitch, full), BF16),
            pltpu.VMEM((elems * pitch, full), BF16),
        ],
    )
    start_edge, out_rows, near_rows = call(
        functools.partial(rotate_ring, groups),
        [rows_of(wide), rows_of(halo), rows_of(halo)],
        in_vmem(ring_cols_in), start_own, start_far, ritz_top, ritz_low, pick,
    )
    out_in, near_in = out(out_rows), near(near_rows)
    (part,) = call(
        first_part, [rows_of(full)], start_edge, far_in, out_in, near_in, ham_top, ham_low
    )
    (rest_low,) = call(
        functools.partial(rotate_low, groups),
        [((block, nodes - wide), F32)],
        in_vmem(low_cols_in), start_own, ritz_top, ritz_low,
    )

    start_rest, back_far, back_out, back_near = call(
        functools.partial(rotate_rest, groups),
        [rows_of(nodes - wide)] + halo_out,
        in_vmem(high_cols_in), rest_low, ritz_top, ritz_low, part, ham_top, ham_low,
    )
    far_in, out_in, near_in = far(back_far), out(back_out), near(back_near)
    start, base, packed = call(
        first_base,
        [rows_of(nodes), rows_of(nodes), rows_of(wide)],
        start_edge, start_rest, part, ham_top, ham_low, pick,
    )
    (far_rows,) = call(
        fetch_far, [((duo, block + 2 * duo), F32)], packed, both, pair, out_in, near_in
    )
    fetched_far = far(far_rows)
    out_rows, near_rows = call(
        fetch_ring, halo_out[1:], packed, both, far_in, out_in, near_in
    )
    fetched_out, fetched_near = out(out_rows), near(near_rows)
    first, part, picked = call(
        first_own,
        [rows_of(nodes), rows_of(full), rows_of(duo)],
        base, pick, far_in, out_in, near_in, ham_top, ham_low,
    )

    (far_rows,) = call(
        return_far, [rows_of(duo)], part, ham_top, ham_low, fetched_out, fetched_near
    )
    returned_far = far(far_rows)
    ghosts, out_rows, near_rows = call(
        return_ring,
        [rows_of(wide)] + halo_out[1:],
        part, ham_top, ham_low, fetched_far, back_far, fetched_out, fetched_near,
    )
    returned_out, returned_near = out(out_rows), near(near_rows)
    (result,) = call(
        second_base,
        [((block, nodes), F32)],
        part, ghosts, ham_top, ham_low, first, start, picked, fetched_far, shuffle, hits,
    )
    (result,) = call(
        finish, [((block, nodes), F32)], result, hits, returned_far, returned_out, returned_near
    )
    return result


def solution(mesh):
    in_specs = (
        P("state", "mesh"),
        P("state", None),
        P("mesh", None, None),
        P("mesh", None),
        P("mesh", None, None),
    )
    out_specs = P("state", "mesh")
    return jax.shard_map(
        per_device, mesh=mesh, in_specs=in_specs, out_specs=out_specs, check_vma=False
    )
```

```python
import functools

import jax
import jax.numpy as jnp
from jax import lax
from jax.experimental import pallas as pl
from jax.experimental.pallas import tpu as pltpu
from jax.sharding import PartitionSpec as P

F32 = jnp.float32
BF16 = jnp.bfloat16
I32 = jnp.int32
NN = ((1,), (0,))
NT = ((1,), (1,))

HALF = 1.5
CENTRE = 2.5
SIGMA_ONE = HALF / (-1.0 - CENTRE)
SIGMA_TWO = 1.0 / (2.0 / SIGMA_ONE - SIGMA_ONE)
SCALE_ONE = SIGMA_ONE / HALF
SCALE_TWO = 2.0 * SIGMA_TWO / HALF


def dot(a, b, dims=NN):
    return lax.dot_general(a, b, (dims, ((), ())), preferred_element_type=F32)


def split(x):
    top = x.astype(BF16)
    return top, (x - top.astype(F32)).astype(BF16)


def mul(a, b, dims=NN):
    return dot(a[0], b[0], dims) + (dot(a[0], b[1], dims) + dot(a[1], b[0], dims))


def sift(a, x):
    top, low = split(x)
    return dot(a, top) + dot(a, low)


def call(body, outs, *args, limit=8, kept=False, **rest):
    return pl.pallas_call(
        body,
        out_shape=[pltpu.VMEM(*out) if kept else jax.ShapeDtypeStruct(*out) for out in outs],
        compiler_params=pltpu.CompilerParams(vmem_limit_bytes=limit << 20),
        cost_estimate=pl.CostEstimate(flops=1000, bytes_accessed=1000, transcendentals=0),
        **rest,
    )(*args)


def in_hbm(x):
    return pltpu.with_memory_space_constraint(x, pltpu.HBM)


def in_vmem(x):
    return pltpu.with_memory_space_constraint(x, pltpu.VMEM)


def column(row, width):
    down = lax.broadcasted_iota(I32, (width, width), 0)
    along = lax.broadcasted_iota(I32, (width, width), 1)
    return jnp.sum(jnp.where(down == along, row, 0), axis=1, keepdims=True)


def renumber(
    lists_in, subspace_in, far_out, ring_out, low_out, high_out, shuffle_out, lists, subspace, sems
):
    slots, halo = lists.shape[1:]
    depth, nodes = subspace.shape
    duo = 2 * halo
    span = depth // 2
    index_copy = pltpu.make_async_copy(lists_in, lists, sems.at[0])
    index_copy.start()
    copy = pltpu.make_async_copy(subspace_in, subspace, sems.at[1])
    copy.start()
    index_copy.wait()
    ids = lax.broadcasted_iota(I32, (halo, nodes), 1)
    seen = []
    for slot in range(slots):
        sent = column(lists[0, slot : slot + 1, :], halo)
        seen.append(jnp.where(sent == ids, 1.0, 0.0))
    far = jnp.max(jnp.maximum(seen[2], seen[3]), axis=0, keepdims=True)
    ring = jnp.max(jnp.maximum(seen[0], seen[1]), axis=0, keepdims=True) * (1.0 - far)
    down = lax.broadcasted_iota(I32, (nodes, nodes), 0)
    along = lax.broadcasted_iota(I32, (nodes, nodes), 1)
    upto = jnp.where(down <= along, 1.0, 0.0).astype(BF16)
    flags = jnp.concatenate([far, ring, jnp.zeros((6, nodes), F32)], 0)
    counts = dot(flags.astype(BF16), upto).astype(I32)
    far_count, ring_count = counts[0:1], counts[1:2]
    totals = jnp.sum(flags, axis=1, keepdims=True).astype(I32)
    far_total, ring_total = totals[0:1], totals[1:2]
    place = jnp.where(
        far > 0.5,
        far_count - 1,
        jnp.where(
            ring > 0.5,
            far_total + ring_count - 1,
            far_total + ring_total + along[:1] - far_count - ring_count,
        ),
    )
    match = place == down
    shuffle = jnp.where(match, 1.0, 0.0).astype(BF16)
    shuffle_out[...] = shuffle
    copy.wait()
    halves = []
    for part, rest_out in enumerate((low_out, high_out)):
        top, low = split(subspace[part * span : (part + 1) * span, :])
        turned = dot(top, shuffle, NT) + dot(low, shuffle, NT)
        rest_out[...] = turned[:, 2 * duo :]
        halves.append(turned)
    far_out[...] = jnp.concatenate([half[:, :duo] for half in halves], 1)
    ring_out[...] = jnp.concatenate([half[:, duo : 2 * duo] for half in halves], 1)


def assemble(
    odd, lists, connect, blocks_in, shuffle, top_out, low_out, pick_out, both_out, hits_out, pair_out,
    blocks, sem, spread, rows_both,
):
    copy = pltpu.make_async_copy(blocks_in, blocks, sem)
    copy.start()
    elems, size = connect.shape
    slots, halo = lists.shape[1:]
    nodes = shuffle.shape[0]
    wide = slots * halo
    duo = 2 * halo
    swap = odd[0] == 1
    columns = [column(lists[0, slot : slot + 1, :], halo) for slot in range(slots)]
    outer = jnp.where(swap, columns[0], columns[1])
    inner = jnp.where(swap, columns[1], columns[0])
    sent = jnp.concatenate([columns[2], columns[3], outer, inner], 0)
    hits = jnp.where(sent == lax.broadcasted_iota(I32, (wide, nodes), 1), 1.0, 0.0).astype(BF16)
    hits_out[...] = hits
    pick = dot(hits, shuffle[:wide, :], NT).astype(BF16)
    pick_out[...] = pick
    both = dot(pick, pick, NT)
    both_out[...] = both.astype(BF16)

    lane = lax.broadcasted_iota(I32, (halo, 1), 0)
    flag = odd[0]
    ghost = jnp.concatenate(
        [3 * halo + lane, 2 * halo + lane, (1 - flag) * halo + lane, flag * halo + lane], 0
    )
    along = lax.broadcasted_iota(I32, (nodes, nodes), 1).astype(F32)
    origin = jnp.sum(along * shuffle[...].astype(F32), axis=1, keepdims=True).astype(I32)
    pitch = spread.shape[1] // elems
    full = nodes + wide
    numbers = jnp.broadcast_to(jnp.concatenate([origin, nodes + ghost], 0), (full, pitch))
    copy.wait()
    for elem in range(elems):
        cols = slice(elem * pitch, (elem + 1) * pitch)
        wanted = jnp.pad(connect[elem : elem + 1, :], ((0, 0), (0, pitch - size)), constant_values=-1)
        chosen = jnp.where(numbers == wanted, 1.0, 0.0).astype(BF16)
        spread[:, cols] = chosen
        block = blocks[pl.ds(elem, size, stride=elems), :]
        top, low = split(jnp.pad(block, ((0, pitch - size), (0, pitch - size))))
        rows = dot(jnp.concatenate([top, low], 0), chosen, NT)
        top, low = split(rows[:pitch] + rows[pitch:])
        rows_both[cols, :full] = top
        rows_both[cols, full:] = low
    ham = dot(spread[...], rows_both[...])
    ham = ham[:, :full] + ham[:, full:]
    top, low = split(ham)
    top_out[...] = top
    low_out[...] = low
    far = slice(nodes, nodes + duo)
    pair_out[...] = jnp.concatenate([both[:duo, :duo], ham[far, far]], 1)


def rotate_own(group, far, ring, low_rest, high_rest, ritz_in, start_out, top_out, low_out, ritz, sems):
    block, depth = ritz.shape[1:]
    groups = ritz.shape[0]
    parts = sems.shape[1]
    span = block // parts
    copies = []
    for step in range(groups):
        first = lax.rem(group[0] + groups - step, groups) * depth
        cols = pl.ds(pl.multiple_of(first, depth), depth)
        for part in range(parts):
            rows = pl.ds(part * span, span)
            copies.append(
                pltpu.make_async_copy(
                    ritz_in.at[rows, cols], ritz.at[step, rows], sems.at[step, part]
                )
            )
            copies[-1].start()
    width = far.shape[1] // 2
    columns = [jnp.concatenate([x[:, :width], x[:, width:]], 0) for x in (far, ring)]
    rest = jnp.concatenate([low_rest[...], high_rest[...]], 0)
    own = split(jnp.concatenate(columns + [rest], 1))
    for step in range(groups):
        for part in range(parts):
            rows = slice(part * span, (part + 1) * span)
            copies[step * parts + part].wait()
            top, low = split(ritz[step, rows, :])
            if step == 0:
                start_out[rows, :] = mul((top, low), own)
            else:
                cols = slice((step - 1) * depth, step * depth)
                top_out[rows, cols] = top
                low_out[rows, cols] = low


def rotate(top, low, columns):
    width = columns.shape[1]
    high, rest = split(columns)
    wide = dot(top, jnp.concatenate([high, rest], 1))
    return wide[:, :width] + (wide[:, width:] + dot(low, high))


def pieces(x, groups, part, axis):
    span = x.shape[axis] // (2 * (groups - 1))
    starts = [(2 * step + part) * span for step in range(groups - 1)]
    if axis == 0:
        return [x[start : start + span, :] for start in starts]
    return [x[:, start : start + span] for start in starts]


def rotate_sides(columns, top, low, groups):
    width = columns.shape[1] // 2
    span = columns.shape[0] // (groups - 1)
    whole = jnp.concatenate(
        [
            columns[step * span : (step + 1) * span, part * width : (part + 1) * width]
            for step in range(groups - 1)
            for part in range(2)
        ],
        0,
    )
    return rotate(top[...], low[...], whole)


def rotate_half(columns, top, low, groups, part):
    return rotate(
        jnp.concatenate(pieces(top, groups, part, 1), 1),
        jnp.concatenate(pieces(low, groups, part, 1), 1),
        columns[...],
    )


def rotate_far(groups, columns, start_own, top, low, pick, pair, start_out, far_out):
    duo, block = start_out.shape
    start = (start_own[:, :duo] + rotate_sides(columns, top, low, groups)).T
    start_out[...] = start
    far_out[:, :block] = sift(pick[:duo, :duo], start)
    far_out[:, block:] = pair[...]


def rotate_ring(groups, columns, start_own, start_far, top, low, pick, start_out, out_out, near_out):
    halo = out_out.shape[0]
    duo = 2 * halo
    start = (start_own[:, duo : 2 * duo] + rotate_sides(columns, top, low, groups)).T
    start = jnp.concatenate([start_far[...], start], 0)
    start_out[...] = start
    packed = sift(pick[duo:, :], start)
    out_out[...] = packed[:halo]
    near_out[...] = packed[halo:]


def rotate_low(groups, columns, start_own, top, low, rest_out):
    edge_nodes = start_own.shape[1] - columns.shape[1]
    rest_out[...] = start_own[:, edge_nodes:] + rotate_half(columns, top, low, groups, 0)


def first_part(start_edge, far_in, out_in, near_in, ham_top, ham_low, part_out, overlap_out, couple_out):
    edge_nodes = start_edge.shape[0]
    nodes = ham_top.shape[0] - 4 * out_in.shape[0]
    duo = far_in.shape[0]
    block = start_edge.shape[1]
    ghosts = jnp.concatenate([far_in[:, :block], out_in[...], near_in[...]], 0)
    part_out[...] = mul(
        (ham_top[:, :edge_nodes], ham_low[:, :edge_nodes]), split(start_edge[...])
    ) + mul((ham_top[:, nodes:], ham_low[:, nodes:]), split(ghosts))
    overlap_out[...] = SCALE_ONE * far_in[:, block : block + duo]
    couple_out[...] = far_in[:, block + duo :]


def rotate_rest(
    groups, columns, rest_low, top, low, part, ham_top, ham_low, rest_out, far_out, out_out, near_out
):
    rest = (rest_low[...] + rotate_half(columns, top, low, groups, 1)).T
    rest_out[...] = rest
    halo = out_out.shape[0]
    edge_nodes, width = part.shape[0] - 4 * halo - rest.shape[0], rest.shape[0]
    nodes = edge_nodes + width
    cols = slice(edge_nodes, nodes)
    back = part[nodes:, :] + mul((ham_top[nodes:, cols], ham_low[nodes:, cols]), split(rest))
    far_out[...] = back[: 2 * halo]
    out_out[...] = back[2 * halo : 3 * halo]
    near_out[...] = back[3 * halo :]


def first_base(
    start_edge, start_rest, part, ham_top, ham_low, pick, overlap, back_far,
    start_out, base_out, packed_out, adjust_out,
):
    nodes = ham_top.shape[0] - pick.shape[0]
    edge_nodes = start_edge.shape[0]
    cols = slice(edge_nodes, nodes)
    start = jnp.concatenate([start_edge[...], start_rest[...]], 0)
    start_out[...] = start
    own = part[:nodes, :] + mul(
        (ham_top[:nodes, cols], ham_low[:nodes, cols]), split(start_rest[...])
    )
    base = SCALE_ONE * (own - CENTRE * start)
    base_out[...] = base
    packed_out[...] = sift(pick[...], base[:edge_nodes])
    adjust_out[...] = mul(split(overlap[...]), split(back_far[...]))


def fetch_far(packed, both, out_in, near_in, far_out):
    duo = 2 * out_in.shape[0]
    back = jnp.concatenate([out_in[...], near_in[...]], 0)
    far_out[...] = packed[:duo, :] + SCALE_ONE * sift(both[:duo, duo:], back)


def fetch_ring(packed, both, far_in, out_in, near_in, out_out, near_out):
    halo = out_in.shape[0]
    back = jnp.concatenate([far_in[...], out_in[...], near_in[...]], 0)
    rows = packed[2 * halo :, :] + SCALE_ONE * sift(both[2 * halo :, :], back)
    out_out[...] = rows[:halo]
    near_out[...] = rows[halo:]


def first_own(
    base, pick, far_in, out_in, near_in, ham_top, ham_low, couple, first_out, part_out, known_out
):
    edge_nodes = pick.shape[1]
    nodes = base.shape[0]
    duo = far_in.shape[0]
    back = jnp.concatenate([far_in[...], out_in[...], near_in[...]], 0)
    edge = base[:edge_nodes, :] + SCALE_ONE * sift(pick[...].T, back)
    first = jnp.concatenate([edge, base[edge_nodes:, :]], 0)
    first_out[...] = first
    part_out[...] = mul((ham_top[:, :nodes], ham_low[:, :nodes]), split(first))
    known_out[...] = mul(split(couple[...]), split(sift(pick[:duo, :], edge)))


def return_far(part, ham_top, ham_low, out_in, near_in, far_out):
    halo = out_in.shape[0]
    nodes = part.shape[0] - 4 * halo
    far = slice(nodes, nodes + 2 * halo)
    ring = slice(nodes + 2 * halo, nodes + 4 * halo)
    ghosts = split(jnp.concatenate([out_in[...], near_in[...]], 0))
    far_out[...] = part[far, :] + mul((ham_top[far, ring], ham_low[far, ring]), ghosts)


def return_ring(
    part, ham_top, ham_low, far_in, adjust, out_in, near_in, ghosts_out, out_out, near_out
):
    halo = out_in.shape[0]
    nodes = part.shape[0] - 4 * halo
    ring = slice(nodes + 2 * halo, nodes + 4 * halo)
    ghosts = jnp.concatenate([far_in[...] + adjust[...], out_in[...], near_in[...]], 0)
    ghosts_out[...] = ghosts
    rows = part[ring, :] + mul((ham_top[ring, nodes:], ham_low[ring, nodes:]), split(ghosts))
    out_out[...] = rows[:halo]
    near_out[...] = rows[halo:]


def second_base(part, ghosts, ham_top, ham_low, first, start, known, shuffle, hits, result_out):
    nodes = first.shape[0]
    duo = known.shape[0]
    ham = (ham_top[:nodes, nodes:], ham_low[:nodes, nodes:])
    second = part[:nodes, :] + mul(ham, split(ghosts[...])) - CENTRE * first[...]
    second = SCALE_TWO * second - SIGMA_ONE * SIGMA_TWO * start[...]
    top, low = split(second.T)
    result = dot(top, shuffle[...]) + dot(low, shuffle[...])
    top, low = split(SCALE_TWO * known[...].T)
    result_out[...] = result + (dot(top, hits[:duo, :]) + dot(low, hits[:duo, :]))


def finish(result, hits, far_in, out_in, near_in, out):
    back = jnp.concatenate([far_in[...], out_in[...], near_in[...]], 0)
    top, low = split(SCALE_TWO * back.T)
    out[...] = result[...] + (dot(top, hits[...]) + dot(low, hits[...]))


def per_device(subspace, ritz, element_ham, connect, send_rows):
    depth, nodes = subspace.shape
    block = ritz.shape[0]
    slots, halo = send_rows.shape[1:]
    partitions = lax.axis_size("mesh")
    groups = lax.axis_size("state")
    across = partitions // 2
    wide = slots * halo
    duo = 2 * halo
    full = nodes + wide

    odd = (lax.axis_index("mesh") % 2).astype(I32).reshape(1)
    group = lax.axis_index("state").astype(I32).reshape(1)
    pairs_far = [(i, (i + across) % partitions) for i in range(partitions)]
    pairs_in = [(i, i ^ 1) for i in range(partitions)]
    pairs_out = [
        (i, (i + 1) % partitions if i % 2 else (i - 1) % partitions) for i in range(partitions)
    ]

    def far(rows):
        return lax.ppermute(rows, "mesh", pairs_far)

    def out(rows):
        return lax.ppermute(rows, "mesh", pairs_out)

    def near(rows):
        return lax.ppermute(rows, "mesh", pairs_in)

    def gather(rows):
        parts = [
            lax.ppermute(rows, "state", [(i, (i + step) % groups) for i in range(groups)])
            for step in range(1, groups)
        ]
        return parts[0] if len(parts) == 1 else jnp.concatenate(parts, 0)

    def rows_of(count):
        return ((count, block), F32)

    halo_out = [rows_of(duo), rows_of(halo), rows_of(halo)]
    smem = pl.BlockSpec(memory_space=pltpu.SMEM)
    vmem = pl.BlockSpec(memory_space=pltpu.VMEM)
    hbm = pl.BlockSpec(memory_space=pltpu.HBM)

    far_cols, ring_cols, low_cols, high_cols, shuffle = call(
        renumber,
        [
            ((depth // 2, 2 * duo), F32),
            ((depth // 2, 2 * duo), F32),
            ((depth // 2, nodes - wide), F32),
            ((depth // 2, nodes - wide), F32),
            ((nodes, nodes), BF16),
        ],
        in_hbm(send_rows), in_hbm(subspace),
        kept=True,
        in_specs=[hbm, hbm],
        scratch_shapes=[
            pltpu.VMEM(send_rows.shape, I32),
            pltpu.VMEM(subspace.shape, F32),
            pltpu.SemaphoreType.DMA((2,)),
        ],
    )
    far_cols_in = gather(far_cols)
    ring_cols_in = gather(ring_cols)
    low_cols_in = gather(low_cols)
    high_cols_in = gather(high_cols)
    elems, size = connect.shape
    pitch = -(-size // 128) * 128
    blocks = jnp.transpose(element_ham, (1, 0, 2)).reshape(size * elems, size)
    ham_top, ham_low, pick, both, hits, pair = call(
        assemble,
        [
            ((full, full), BF16),
            ((full, full), BF16),
            ((wide, wide), BF16),
            ((wide, wide), BF16),
            ((wide, nodes), BF16),
            ((duo, 2 * duo), F32),
        ],
        odd, send_rows, connect, in_hbm(blocks), shuffle,
        limit=12,
        in_specs=[smem, vmem, vmem, hbm, vmem],
        scratch_shapes=[
            pltpu.VMEM(blocks.shape, F32),
            pltpu.SemaphoreType.DMA,
            pltpu.VMEM((full, elems * pitch), BF16),
            pltpu.VMEM((elems * pitch, 2 * full), BF16),
        ],
    )
    others = groups - 1
    start_own, ritz_top, ritz_low = call(
        rotate_own,
        [
            ((block, nodes), F32),
            ((block, others * depth), BF16),
            ((block, others * depth), BF16),
        ],
        group, far_cols, ring_cols, low_cols, high_cols, in_hbm(ritz),
        limit=12,
        in_specs=[smem, vmem, vmem, vmem, vmem, hbm],
        scratch_shapes=[
            pltpu.VMEM((groups, block, depth), F32),
            pltpu.SemaphoreType.DMA((groups, 2)),
        ],
    )

    start_far, far_rows = call(
        functools.partial(rotate_far, groups),
        [rows_of(duo), ((duo, block + 2 * duo), F32)],
        in_vmem(far_cols_in), start_own, ritz_top, ritz_low, pick, pair,
    )
    far_in = far(far_rows)
    start_edge, out_rows, near_rows = call(
        functools.partial(rotate_ring, groups),
        [rows_of(wide), rows_of(halo), rows_of(halo)],
        in_vmem(ring_cols_in), start_own, start_far, ritz_top, ritz_low, pick,
    )
    out_in, near_in = out(out_rows), near(near_rows)
    part, overlap, couple = call(
        first_part,
        [rows_of(full), ((duo, duo), F32), ((duo, duo), F32)],
        start_edge, far_in, out_in, near_in, ham_top, ham_low,
    )
    (rest_low,) = call(
        functools.partial(rotate_low, groups),
        [((block, nodes - wide), F32)],
        in_vmem(low_cols_in), start_own, ritz_top, ritz_low,
    )

    start_rest, back_far, back_out, back_near = call(
        functools.partial(rotate_rest, groups),
        [rows_of(nodes - wide)] + halo_out,
        in_vmem(high_cols_in), rest_low, ritz_top, ritz_low, part, ham_top, ham_low,
    )
    far_in, out_in, near_in = far(back_far), out(back_out), near(back_near)
    start, base, packed, adjust = call(
        first_base,
        [rows_of(nodes), rows_of(nodes), rows_of(wide), rows_of(duo)],
        start_edge, start_rest, part, ham_top, ham_low, pick, overlap, back_far,
    )
    (far_rows,) = call(fetch_far, [rows_of(duo)], packed, both, out_in, near_in)
    fetched_far = far(far_rows)
    out_rows, near_rows = call(
        fetch_ring, halo_out[1:], packed, both, far_in, out_in, near_in
    )
    fetched_out, fetched_near = out(out_rows), near(near_rows)
    first, part, known = call(
        first_own,
        [rows_of(nodes), rows_of(full), rows_of(duo)],
        base, pick, far_in, out_in, near_in, ham_top, ham_low, couple,
    )

    (far_rows,) = call(
        return_far, [rows_of(duo)], part, ham_top, ham_low, fetched_out, fetched_near
    )
    returned_far = far(far_rows)
    ghosts, out_rows, near_rows = call(
        return_ring,
        [rows_of(wide)] + halo_out[1:],
        part, ham_top, ham_low, fetched_far, adjust, fetched_out, fetched_near,
    )
    returned_out, returned_near = out(out_rows), near(near_rows)
    (result,) = call(
        second_base,
        [((block, nodes), F32)],
        part, ghosts, ham_top, ham_low, first, start, known, shuffle, hits,
    )
    (result,) = call(
        finish, [((block, nodes), F32)], result, hits, returned_far, returned_out, returned_near
    )
    return result


def solution(mesh):
    in_specs = (
        P("state", "mesh"),
        P("state", None),
        P("mesh", None, None),
        P("mesh", None),
        P("mesh", None, None),
    )
    out_specs = P("state", "mesh")
    return jax.shard_map(
        per_device, mesh=mesh, in_specs=in_specs, out_specs=out_specs, check_vma=False
    )
```

```python
import functools

import jax
import jax.numpy as jnp
from jax import lax
from jax.experimental import pallas as pl
from jax.experimental.pallas import tpu as pltpu
from jax.sharding import PartitionSpec as P

F32 = jnp.float32
BF16 = jnp.bfloat16
I32 = jnp.int32
NN = ((1,), (0,))
NT = ((1,), (1,))

HALF = 1.5
CENTRE = 2.5
SIGMA_ONE = HALF / (-1.0 - CENTRE)
SIGMA_TWO = 1.0 / (2.0 / SIGMA_ONE - SIGMA_ONE)
SCALE_ONE = SIGMA_ONE / HALF
SCALE_TWO = 2.0 * SIGMA_TWO / HALF


def dot(a, b, dims=NN):
    return lax.dot_general(a, b, (dims, ((), ())), preferred_element_type=F32)


def split(x):
    top = x.astype(BF16)
    return top, (x - top.astype(F32)).astype(BF16)


def mul(a, b, dims=NN):
    return dot(a[0], b[0], dims) + (dot(a[0], b[1], dims) + dot(a[1], b[0], dims))


def sift(a, x):
    top, low = split(x)
    return dot(a, top) + dot(a, low)


def call(body, outs, *args, limit=8, kept=False, **rest):
    return pl.pallas_call(
        body,
        out_shape=[pltpu.VMEM(*out) if kept else jax.ShapeDtypeStruct(*out) for out in outs],
        compiler_params=pltpu.CompilerParams(vmem_limit_bytes=limit << 20),
        cost_estimate=pl.CostEstimate(flops=1000, bytes_accessed=1000, transcendentals=0),
        **rest,
    )(*args)


def in_hbm(x):
    return pltpu.with_memory_space_constraint(x, pltpu.HBM)


def in_vmem(x):
    return pltpu.with_memory_space_constraint(x, pltpu.VMEM)


def column(row, width):
    down = lax.broadcasted_iota(I32, (width, width), 0)
    along = lax.broadcasted_iota(I32, (width, width), 1)
    return jnp.sum(jnp.where(down == along, row, 0), axis=1, keepdims=True)


def renumber(
    lists_in, subspace_in, far_out, ring_out, low_out, high_out, shuffle_out, lists, subspace, sems
):
    slots, halo = lists.shape[1:]
    depth, nodes = subspace.shape
    duo = 2 * halo
    span = depth // 2
    index_copy = pltpu.make_async_copy(lists_in, lists, sems.at[0])
    index_copy.start()
    copy = pltpu.make_async_copy(subspace_in, subspace, sems.at[1])
    copy.start()
    index_copy.wait()
    ids = lax.broadcasted_iota(I32, (halo, nodes), 1)
    seen = []
    for slot in range(slots):
        sent = column(lists[0, slot : slot + 1, :], halo)
        seen.append(jnp.where(sent == ids, 1.0, 0.0))
    far = jnp.max(jnp.maximum(seen[2], seen[3]), axis=0, keepdims=True)
    ring = jnp.max(jnp.maximum(seen[0], seen[1]), axis=0, keepdims=True) * (1.0 - far)
    down = lax.broadcasted_iota(I32, (nodes, nodes), 0)
    along = lax.broadcasted_iota(I32, (nodes, nodes), 1)
    upto = jnp.where(down <= along, 1.0, 0.0).astype(BF16)
    flags = jnp.concatenate([far, ring, jnp.zeros((6, nodes), F32)], 0)
    counts = dot(flags.astype(BF16), upto).astype(I32)
    far_count, ring_count = counts[0:1], counts[1:2]
    totals = jnp.sum(flags, axis=1, keepdims=True).astype(I32)
    far_total, ring_total = totals[0:1], totals[1:2]
    place = jnp.where(
        far > 0.5,
        far_count - 1,
        jnp.where(
            ring > 0.5,
            far_total + ring_count - 1,
            far_total + ring_total + along[:1] - far_count - ring_count,
        ),
    )
    match = place == down
    shuffle = jnp.where(match, 1.0, 0.0).astype(BF16)
    shuffle_out[...] = shuffle
    copy.wait()
    halves = []
    for part, rest_out in enumerate((low_out, high_out)):
        top, low = split(subspace[part * span : (part + 1) * span, :])
        turned = dot(top, shuffle, NT) + dot(low, shuffle, NT)
        rest_out[...] = turned[:, 2 * duo :]
        halves.append(turned)
    far_out[...] = jnp.concatenate([half[:, :duo] for half in halves], 1)
    ring_out[...] = jnp.concatenate([half[:, duo : 2 * duo] for half in halves], 1)


def assemble(
    odd, lists, connect, blocks_in, shuffle, top_out, low_out, pick_out, both_out, hits_out, pair_out,
    blocks, sem, spread, rows_both,
):
    copy = pltpu.make_async_copy(blocks_in, blocks, sem)
    copy.start()
    elems, size = connect.shape
    slots, halo = lists.shape[1:]
    nodes = shuffle.shape[0]
    wide = slots * halo
    duo = 2 * halo
    swap = odd[0] == 1
    columns = [column(lists[0, slot : slot + 1, :], halo) for slot in range(slots)]
    outer = jnp.where(swap, columns[0], columns[1])
    inner = jnp.where(swap, columns[1], columns[0])
    sent = jnp.concatenate([columns[2], columns[3], outer, inner], 0)
    hits = jnp.where(sent == lax.broadcasted_iota(I32, (wide, nodes), 1), 1.0, 0.0).astype(BF16)
    hits_out[...] = hits
    pick = dot(hits, shuffle[:wide, :], NT).astype(BF16)
    pick_out[...] = pick
    both = dot(pick, pick, NT)
    both_out[...] = both.astype(BF16)

    lane = lax.broadcasted_iota(I32, (halo, 1), 0)
    flag = odd[0]
    ghost = jnp.concatenate(
        [3 * halo + lane, 2 * halo + lane, (1 - flag) * halo + lane, flag * halo + lane], 0
    )
    along = lax.broadcasted_iota(I32, (nodes, nodes), 1).astype(F32)
    origin = jnp.sum(along * shuffle[...].astype(F32), axis=1, keepdims=True).astype(I32)
    pitch = spread.shape[1] // elems
    full = nodes + wide
    numbers = jnp.broadcast_to(jnp.concatenate([origin, nodes + ghost], 0), (full, pitch))
    copy.wait()
    for elem in range(elems):
        cols = slice(elem * pitch, (elem + 1) * pitch)
        wanted = jnp.pad(connect[elem : elem + 1, :], ((0, 0), (0, pitch - size)), constant_values=-1)
        chosen = jnp.where(numbers == wanted, 1.0, 0.0).astype(BF16)
        spread[:, cols] = chosen
        block = blocks[pl.ds(elem, size, stride=elems), :]
        top, low = split(jnp.pad(block, ((0, pitch - size), (0, pitch - size))))
        rows = dot(jnp.concatenate([top, low], 0), chosen, NT)
        top, low = split(rows[:pitch] + rows[pitch:])
        rows_both[cols, :full] = top
        rows_both[cols, full:] = low
    ham = dot(spread[...], rows_both[...])
    ham = ham[:, :full] + ham[:, full:]
    top, low = split(ham)
    top_out[...] = top
    low_out[...] = low
    far = slice(nodes, nodes + duo)
    pair_out[...] = jnp.concatenate([both[:duo, :duo], ham[far, far]], 1)


def rotate_own(group, far, ring, low_rest, high_rest, ritz_in, start_out, top_out, low_out, ritz, sems):
    block, depth = ritz.shape[1:]
    groups = ritz.shape[0]
    parts = sems.shape[1]
    span = block // parts
    copies = []
    for step in range(groups):
        first = lax.rem(group[0] + groups - step, groups) * depth
        cols = pl.ds(pl.multiple_of(first, depth), depth)
        for part in range(parts):
            rows = pl.ds(part * span, span)
            copies.append(
                pltpu.make_async_copy(
                    ritz_in.at[rows, cols], ritz.at[step, rows], sems.at[step, part]
                )
            )
            copies[-1].start()
    width = far.shape[1] // 2
    columns = [jnp.concatenate([x[:, :width], x[:, width:]], 0) for x in (far, ring)]
    rest = jnp.concatenate([low_rest[...], high_rest[...]], 0)
    own = split(jnp.concatenate(columns + [rest], 1))
    for step in range(groups):
        for part in range(parts):
            rows = slice(part * span, (part + 1) * span)
            copies[step * parts + part].wait()
            top, low = split(ritz[step, rows, :])
            if step == 0:
                start_out[rows, :] = mul((top, low), own)
            else:
                cols = slice((step - 1) * depth, step * depth)
                top_out[rows, cols] = top
                low_out[rows, cols] = low


def rotate(top, low, columns):
    width = columns.shape[1]
    high, rest = split(columns)
    wide = dot(top, jnp.concatenate([high, rest], 1))
    return wide[:, :width] + (wide[:, width:] + dot(low, high))


def pieces(x, groups, part, axis):
    span = x.shape[axis] // (2 * (groups - 1))
    starts = [(2 * step + part) * span for step in range(groups - 1)]
    if axis == 0:
        return [x[start : start + span, :] for start in starts]
    return [x[:, start : start + span] for start in starts]


def rotate_sides(columns, top, low, groups):
    width = columns.shape[1] // 2
    span = columns.shape[0] // (groups - 1)
    whole = jnp.concatenate(
        [
            columns[step * span : (step + 1) * span, part * width : (part + 1) * width]
            for step in range(groups - 1)
            for part in range(2)
        ],
        0,
    )
    return rotate(top[...], low[...], whole)


def rotate_half(columns, top, low, groups, part):
    return rotate(
        jnp.concatenate(pieces(top, groups, part, 1), 1),
        jnp.concatenate(pieces(low, groups, part, 1), 1),
        columns[...],
    )


def rotate_far(groups, columns, start_own, top, low, pick, pair, start_out, far_out):
    duo, block = start_out.shape
    start = (start_own[:, :duo] + rotate_sides(columns, top, low, groups)).T
    start_out[...] = start
    far_out[:, :block] = sift(pick[:duo, :duo], start)
    far_out[:, block:] = pair[...]


def rotate_ring(groups, columns, start_own, start_far, top, low, pick, start_out, out_out, near_out):
    halo = out_out.shape[0]
    duo = 2 * halo
    start = (start_own[:, duo : 2 * duo] + rotate_sides(columns, top, low, groups)).T
    start = jnp.concatenate([start_far[...], start], 0)
    start_out[...] = start
    packed = sift(pick[duo:, :], start)
    out_out[...] = packed[:halo]
    near_out[...] = packed[halo:]


def rotate_low(groups, columns, start_own, top, low, rest_out):
    edge_nodes = start_own.shape[1] - columns.shape[1]
    rest_out[...] = start_own[:, edge_nodes:] + rotate_half(columns, top, low, groups, 0)


def first_part(start_edge, far_in, out_in, near_in, ham_top, ham_low, part_out, overlap_out, couple_out):
    edge_nodes = start_edge.shape[0]
    nodes = ham_top.shape[0] - 4 * out_in.shape[0]
    duo = far_in.shape[0]
    block = start_edge.shape[1]
    ghosts = jnp.concatenate([far_in[:, :block], out_in[...], near_in[...]], 0)
    part_out[...] = mul(
        (ham_top[:, :edge_nodes], ham_low[:, :edge_nodes]), split(start_edge[...])
    ) + mul((ham_top[:, nodes:], ham_low[:, nodes:]), split(ghosts))
    overlap_out[...] = SCALE_ONE * far_in[:, block : block + duo]
    couple_out[...] = far_in[:, block + duo :]


def rotate_rest(
    groups, columns, rest_low, top, low, part, ham_top, ham_low, rest_out, far_out, lower_out, upper_out, out_out, near_out
):
    rest = (rest_low[...] + rotate_half(columns, top, low, groups, 1)).T
    rest_out[...] = rest
    halo = out_out.shape[0]
    edge_nodes, width = part.shape[0] - 4 * halo - rest.shape[0], rest.shape[0]
    nodes = edge_nodes + width
    cols = slice(edge_nodes, nodes)
    back = part[nodes:, :] + mul((ham_top[nodes:, cols], ham_low[nodes:, cols]), split(rest))
    far_out[...] = back[: 2 * halo]
    lower_out[...] = back[:halo]
    upper_out[...] = back[halo : 2 * halo]
    out_out[...] = back[2 * halo : 3 * halo]
    near_out[...] = back[3 * halo :]


def first_base(
    start_edge, start_rest, part, ham_top, ham_low, pick, overlap, back_far,
    start_out, base_out, packed_out, adjust_out,
):
    nodes = ham_top.shape[0] - pick.shape[0]
    edge_nodes = start_edge.shape[0]
    cols = slice(edge_nodes, nodes)
    start = jnp.concatenate([start_edge[...], start_rest[...]], 0)
    start_out[...] = start
    own = part[:nodes, :] + mul(
        (ham_top[:nodes, cols], ham_low[:nodes, cols]), split(start_rest[...])
    )
    base = SCALE_ONE * (own - CENTRE * start)
    base_out[...] = base
    packed_out[...] = sift(pick[...], base[:edge_nodes])
    adjust_out[...] = mul(split(overlap[...]), split(back_far[...]))


def fetch_far(packed, both, out_in, near_in, far_out):
    duo = 2 * out_in.shape[0]
    back = jnp.concatenate([out_in[...], near_in[...]], 0)
    far_out[...] = packed[:duo, :] + SCALE_ONE * sift(both[:duo, duo:], back)


def fetch_ring(packed, both, far_in, lower_in, upper_in, out_in, near_in, out_out, near_out):
    halo = out_in.shape[0]
    far = far_in[...] + jnp.concatenate([lower_in[...], upper_in[...]], 0)
    back = jnp.concatenate([far, out_in[...], near_in[...]], 0)
    rows = packed[2 * halo :, :] + SCALE_ONE * sift(both[2 * halo :, :], back)
    out_out[...] = rows[:halo]
    near_out[...] = rows[halo:]


def first_own(
    base, pick, far_in, lower_in, upper_in, out_in, near_in, ham_top, ham_low, couple, first_out, part_out, known_out
):
    edge_nodes = pick.shape[1]
    nodes = base.shape[0]
    duo = far_in.shape[0]
    far = far_in[...] + jnp.concatenate([lower_in[...], upper_in[...]], 0)
    back = jnp.concatenate([far, out_in[...], near_in[...]], 0)
    edge = base[:edge_nodes, :] + SCALE_ONE * sift(pick[...].T, back)
    first = jnp.concatenate([edge, base[edge_nodes:, :]], 0)
    first_out[...] = first
    part_out[...] = mul((ham_top[:, :nodes], ham_low[:, :nodes]), split(first))
    known_out[...] = mul(split(couple[...]), split(sift(pick[:duo, :], edge)))


def return_far(part, ham_top, ham_low, out_in, near_in, far_out):
    halo = out_in.shape[0]
    nodes = part.shape[0] - 4 * halo
    far = slice(nodes, nodes + 2 * halo)
    ring = slice(nodes + 2 * halo, nodes + 4 * halo)
    ghosts = split(jnp.concatenate([out_in[...], near_in[...]], 0))
    far_out[...] = part[far, :] + mul((ham_top[far, ring], ham_low[far, ring]), ghosts)


def return_ring(
    part, ham_top, ham_low, far_in, adjust, out_in, near_in, ghosts_out, out_out, near_out
):
    halo = out_in.shape[0]
    nodes = part.shape[0] - 4 * halo
    ring = slice(nodes + 2 * halo, nodes + 4 * halo)
    ghosts = jnp.concatenate([far_in[...] + adjust[...], out_in[...], near_in[...]], 0)
    ghosts_out[...] = ghosts
    rows = part[ring, :] + mul((ham_top[ring, nodes:], ham_low[ring, nodes:]), split(ghosts))
    out_out[...] = rows[:halo]
    near_out[...] = rows[halo:]


def second_base(part, ghosts, ham_top, ham_low, first, start, known, shuffle, hits, result_out):
    nodes = first.shape[0]
    duo = known.shape[0]
    ham = (ham_top[:nodes, nodes:], ham_low[:nodes, nodes:])
    second = part[:nodes, :] + mul(ham, split(ghosts[...])) - CENTRE * first[...]
    second = SCALE_TWO * second - SIGMA_ONE * SIGMA_TWO * start[...]
    top, low = split(second.T)
    result = dot(top, shuffle[...]) + dot(low, shuffle[...])
    top, low = split(SCALE_TWO * known[...].T)
    result_out[...] = result + (dot(top, hits[:duo, :]) + dot(low, hits[:duo, :]))


def finish(result, hits, far_in, out_in, near_in, out):
    back = jnp.concatenate([far_in[...], out_in[...], near_in[...]], 0)
    top, low = split(SCALE_TWO * back.T)
    out[...] = result[...] + (dot(top, hits[...]) + dot(low, hits[...]))


def per_device(subspace, ritz, element_ham, connect, send_rows):
    depth, nodes = subspace.shape
    block = ritz.shape[0]
    slots, halo = send_rows.shape[1:]
    partitions = lax.axis_size("mesh")
    groups = lax.axis_size("state")
    across = partitions // 2
    wide = slots * halo
    duo = 2 * halo
    full = nodes + wide

    odd = (lax.axis_index("mesh") % 2).astype(I32).reshape(1)
    group = lax.axis_index("state").astype(I32).reshape(1)
    pairs_far = [(i, (i + across) % partitions) for i in range(partitions)]
    pairs_in = [(i, i ^ 1) for i in range(partitions)]
    pairs_out = [
        (i, (i + 1) % partitions if i % 2 else (i - 1) % partitions) for i in range(partitions)
    ]

    slow = {0, partitions - 1, across, (across + partitions - 1) % partitions}

    def far(rows):
        return lax.ppermute(rows, "mesh", pairs_far)

    def far_apart(rows, lower, upper):
        most = [pair for pair in pairs_far if pair[0] not in slow]
        few = [pair for pair in pairs_far if pair[0] in slow]
        return (
            lax.ppermute(rows, "mesh", most),
            lax.ppermute(lower, "mesh", few),
            lax.ppermute(upper, "mesh", few),
        )

    def out(rows):
        return lax.ppermute(rows, "mesh", pairs_out)

    def near(rows):
        return lax.ppermute(rows, "mesh", pairs_in)

    def gather(rows):
        parts = [
            lax.ppermute(rows, "state", [(i, (i + step) % groups) for i in range(groups)])
            for step in range(1, groups)
        ]
        return parts[0] if len(parts) == 1 else jnp.concatenate(parts, 0)

    def rows_of(count):
        return ((count, block), F32)

    halo_out = [rows_of(duo), rows_of(halo), rows_of(halo)]
    smem = pl.BlockSpec(memory_space=pltpu.SMEM)
    vmem = pl.BlockSpec(memory_space=pltpu.VMEM)
    hbm = pl.BlockSpec(memory_space=pltpu.HBM)

    far_cols, ring_cols, low_cols, high_cols, shuffle = call(
        renumber,
        [
            ((depth // 2, 2 * duo), F32),
            ((depth // 2, 2 * duo), F32),
            ((depth // 2, nodes - wide), F32),
            ((depth // 2, nodes - wide), F32),
            ((nodes, nodes), BF16),
        ],
        in_hbm(send_rows), in_hbm(subspace),
        kept=True,
        in_specs=[hbm, hbm],
        scratch_shapes=[
            pltpu.VMEM(send_rows.shape, I32),
            pltpu.VMEM(subspace.shape, F32),
            pltpu.SemaphoreType.DMA((2,)),
        ],
    )
    far_cols_in = gather(far_cols)
    ring_cols_in = gather(ring_cols)
    low_cols_in = gather(low_cols)
    high_cols_in = gather(high_cols)
    elems, size = connect.shape
    pitch = -(-size // 128) * 128
    blocks = jnp.transpose(element_ham, (1, 0, 2)).reshape(size * elems, size)
    ham_top, ham_low, pick, both, hits, pair = call(
        assemble,
        [
            ((full, full), BF16),
            ((full, full), BF16),
            ((wide, wide), BF16),
            ((wide, wide), BF16),
            ((wide, nodes), BF16),
            ((duo, 2 * duo), F32),
        ],
        odd, send_rows, connect, in_hbm(blocks), shuffle,
        limit=12,
        in_specs=[smem, vmem, vmem, hbm, vmem],
        scratch_shapes=[
            pltpu.VMEM(blocks.shape, F32),
            pltpu.SemaphoreType.DMA,
            pltpu.VMEM((full, elems * pitch), BF16),
            pltpu.VMEM((elems * pitch, 2 * full), BF16),
        ],
    )
    others = groups - 1
    start_own, ritz_top, ritz_low = call(
        rotate_own,
        [
            ((block, nodes), F32),
            ((block, others * depth), BF16),
            ((block, others * depth), BF16),
        ],
        group, far_cols, ring_cols, low_cols, high_cols, in_hbm(ritz),
        limit=12,
        in_specs=[smem, vmem, vmem, vmem, vmem, hbm],
        scratch_shapes=[
            pltpu.VMEM((groups, block, depth), F32),
            pltpu.SemaphoreType.DMA((groups, 2)),
        ],
    )

    start_far, far_rows = call(
        functools.partial(rotate_far, groups),
        [rows_of(duo), ((duo, block + 2 * duo), F32)],
        in_vmem(far_cols_in), start_own, ritz_top, ritz_low, pick, pair,
    )
    far_in = far(far_rows)
    start_edge, out_rows, near_rows = call(
        functools.partial(rotate_ring, groups),
        [rows_of(wide), rows_of(halo), rows_of(halo)],
        in_vmem(ring_cols_in), start_own, start_far, ritz_top, ritz_low, pick,
    )
    out_in, near_in = out(out_rows), near(near_rows)
    part, overlap, couple = call(
        first_part,
        [rows_of(full), ((duo, duo), F32), ((duo, duo), F32)],
        start_edge, far_in, out_in, near_in, ham_top, ham_low,
    )
    (rest_low,) = call(
        functools.partial(rotate_low, groups),
        [((block, nodes - wide), F32)],
        in_vmem(low_cols_in), start_own, ritz_top, ritz_low,
    )

    start_rest, back_far, lower, upper, back_out, back_near = call(
        functools.partial(rotate_rest, groups),
        [rows_of(nodes - wide), rows_of(duo)] + [rows_of(halo)] * 4,
        in_vmem(high_cols_in), rest_low, ritz_top, ritz_low, part, ham_top, ham_low,
    )
    out_in, near_in = out(back_out), near(back_near)
    back_in = far_apart(back_far, lower, upper)
    start, base, packed, adjust = call(
        first_base,
        [rows_of(nodes), rows_of(nodes), rows_of(wide), rows_of(duo)],
        start_edge, start_rest, part, ham_top, ham_low, pick, overlap, back_far,
    )
    (far_rows,) = call(fetch_far, [rows_of(duo)], packed, both, out_in, near_in)
    fetched_far = far(far_rows)
    out_rows, near_rows = call(
        fetch_ring, halo_out[1:], packed, both, *back_in, out_in, near_in
    )
    fetched_out, fetched_near = out(out_rows), near(near_rows)
    first, part, known = call(
        first_own,
        [rows_of(nodes), rows_of(full), rows_of(duo)],
        base, pick, *back_in, out_in, near_in, ham_top, ham_low, couple,
    )

    (far_rows,) = call(
        return_far, [rows_of(duo)], part, ham_top, ham_low, fetched_out, fetched_near
    )
    returned_far = far(far_rows)
    ghosts, out_rows, near_rows = call(
        return_ring,
        [rows_of(wide)] + halo_out[1:],
        part, ham_top, ham_low, fetched_far, adjust, fetched_out, fetched_near,
    )
    returned_out, returned_near = out(out_rows), near(near_rows)
    (result,) = call(
        second_base,
        [((block, nodes), F32)],
        part, ghosts, ham_top, ham_low, first, start, known, shuffle, hits,
    )
    (result,) = call(
        finish, [((block, nodes), F32)], result, hits, returned_far, returned_out, returned_near
    )
    return result


def solution(mesh):
    in_specs = (
        P("state", "mesh"),
        P("state", None),
        P("mesh", None, None),
        P("mesh", None),
        P("mesh", None, None),
    )
    out_specs = P("state", "mesh")
    return jax.shard_map(
        per_device, mesh=mesh, in_specs=in_specs, out_specs=out_specs, check_vma=False
    )
```

```python
import functools

import jax
import jax.numpy as jnp
from jax import lax
from jax.experimental import pallas as pl
from jax.experimental.pallas import tpu as pltpu
from jax.sharding import PartitionSpec as P

F32 = jnp.float32
BF16 = jnp.bfloat16
I32 = jnp.int32
NN = ((1,), (0,))
NT = ((1,), (1,))

HALF = 1.5
CENTRE = 2.5
SIGMA_ONE = HALF / (-1.0 - CENTRE)
SIGMA_TWO = 1.0 / (2.0 / SIGMA_ONE - SIGMA_ONE)
SCALE_ONE = SIGMA_ONE / HALF
SCALE_TWO = 2.0 * SIGMA_TWO / HALF


def dot(a, b, dims=NN):
    return lax.dot_general(a, b, (dims, ((), ())), preferred_element_type=F32)


def split(x):
    top = x.astype(BF16)
    return top, (x - top.astype(F32)).astype(BF16)


def mul(a, b, dims=NN):
    return dot(a[0], b[0], dims) + (dot(a[0], b[1], dims) + dot(a[1], b[0], dims))


def sift(a, x):
    top, low = split(x)
    return dot(a, top) + dot(a, low)


def call(body, outs, *args, limit=8, **rest):
    return pl.pallas_call(
        body,
        out_shape=[jax.ShapeDtypeStruct(*out) for out in outs],
        compiler_params=pltpu.CompilerParams(vmem_limit_bytes=limit << 20),
        cost_estimate=pl.CostEstimate(flops=1000, bytes_accessed=1000, transcendentals=0),
        **rest,
    )(*args)


def in_hbm(x):
    return pltpu.with_memory_space_constraint(x, pltpu.HBM)


def column(row, width):
    down = lax.broadcasted_iota(I32, (width, width), 0)
    along = lax.broadcasted_iota(I32, (width, width), 1)
    return jnp.sum(jnp.where(down == along, row, 0), axis=1, keepdims=True)


def renumber(
    lists_in, subspace_in, far_out, ring_out, low_out, high_out, shuffle_out, lists, subspace, sems
):
    slots, halo = lists.shape[1:]
    depth, nodes = subspace.shape
    duo = 2 * halo
    span = depth // 2
    index_copy = pltpu.make_async_copy(lists_in, lists, sems.at[0])
    index_copy.start()
    copy = pltpu.make_async_copy(subspace_in, subspace, sems.at[1])
    copy.start()
    index_copy.wait()
    ids = lax.broadcasted_iota(I32, (halo, nodes), 1)
    seen = []
    for slot in range(slots):
        sent = column(lists[0, slot : slot + 1, :], halo)
        seen.append(jnp.where(sent == ids, 1.0, 0.0))
    far = jnp.max(jnp.maximum(seen[2], seen[3]), axis=0, keepdims=True)
    ring = jnp.max(jnp.maximum(seen[0], seen[1]), axis=0, keepdims=True) * (1.0 - far)
    down = lax.broadcasted_iota(I32, (nodes, nodes), 0)
    along = lax.broadcasted_iota(I32, (nodes, nodes), 1)
    upto = jnp.where(down <= along, 1.0, 0.0).astype(BF16)
    flags = jnp.concatenate([far, ring, jnp.zeros((6, nodes), F32)], 0)
    counts = dot(flags.astype(BF16), upto).astype(I32)
    far_count, ring_count = counts[0:1], counts[1:2]
    totals = jnp.sum(flags, axis=1, keepdims=True).astype(I32)
    far_total, ring_total = totals[0:1], totals[1:2]
    place = jnp.where(
        far > 0.5,
        far_count - 1,
        jnp.where(
            ring > 0.5,
            far_total + ring_count - 1,
            far_total + ring_total + along[:1] - far_count - ring_count,
        ),
    )
    match = place == down
    shuffle = jnp.where(match, 1.0, 0.0).astype(BF16)
    shuffle_out[...] = shuffle
    copy.wait()
    halves = []
    for part, rest_out in enumerate((low_out, high_out)):
        top, low = split(subspace[part * span : (part + 1) * span, :])
        turned = dot(top, shuffle, NT) + dot(low, shuffle, NT)
        rest_out[...] = turned[:, 2 * duo :]
        halves.append(turned)
    far_out[...] = jnp.concatenate([half[:, :duo] for half in halves], 1)
    ring_out[...] = jnp.concatenate([half[:, duo : 2 * duo] for half in halves], 1)


def assemble(
    odd, lists, connect, blocks_in, shuffle, top_out, low_out, pick_out, both_out, hits_out, pair_out,
    blocks, sem, spread, rows_both,
):
    copy = pltpu.make_async_copy(blocks_in, blocks, sem)
    copy.start()
    elems, size = connect.shape
    slots, halo = lists.shape[1:]
    nodes = shuffle.shape[0]
    wide = slots * halo
    duo = 2 * halo
    swap = odd[0] == 1
    columns = [column(lists[0, slot : slot + 1, :], halo) for slot in range(slots)]
    outer = jnp.where(swap, columns[0], columns[1])
    inner = jnp.where(swap, columns[1], columns[0])
    sent = jnp.concatenate([columns[2], columns[3], outer, inner], 0)
    hits = jnp.where(sent == lax.broadcasted_iota(I32, (wide, nodes), 1), 1.0, 0.0).astype(BF16)
    hits_out[...] = hits
    pick = dot(hits, shuffle[:wide, :], NT).astype(BF16)
    pick_out[...] = pick
    both = dot(pick, pick, NT)
    both_out[...] = both.astype(BF16)

    lane = lax.broadcasted_iota(I32, (halo, 1), 0)
    flag = odd[0]
    ghost = jnp.concatenate(
        [3 * halo + lane, 2 * halo + lane, (1 - flag) * halo + lane, flag * halo + lane], 0
    )
    along = lax.broadcasted_iota(I32, (nodes, nodes), 1).astype(F32)
    origin = jnp.sum(along * shuffle[...].astype(F32), axis=1, keepdims=True).astype(I32)
    pitch = spread.shape[1] // elems
    full = nodes + wide
    numbers = jnp.broadcast_to(jnp.concatenate([origin, nodes + ghost], 0), (full, pitch))
    copy.wait()
    for elem in range(elems):
        cols = slice(elem * pitch, (elem + 1) * pitch)
        wanted = jnp.pad(connect[elem : elem + 1, :], ((0, 0), (0, pitch - size)), constant_values=-1)
        chosen = jnp.where(numbers == wanted, 1.0, 0.0).astype(BF16)
        spread[:, cols] = chosen
        block = blocks[pl.ds(elem, size, stride=elems), :]
        top, low = split(jnp.pad(block, ((0, pitch - size), (0, pitch - size))))
        rows = dot(jnp.concatenate([top, low], 0), chosen, NT)
        top, low = split(rows[:pitch] + rows[pitch:])
        rows_both[cols, :full] = top
        rows_both[cols, full:] = low
    ham = dot(spread[...], rows_both[...])
    ham = ham[:, :full] + ham[:, full:]
    top, low = split(ham)
    top_out[...] = top
    low_out[...] = low
    far = slice(nodes, nodes + duo)
    pair_out[...] = jnp.concatenate([both[:duo, :duo], ham[far, far]], 1)


def rotate_own(
    group, shuffle, subspace_in, ritz_in, start_out, top_out, low_out, subspace, ritz, sem, sems
):
    block, depth = ritz.shape[1:]
    groups = ritz.shape[0]
    parts = sems.shape[1]
    span = block // parts
    own_copy = pltpu.make_async_copy(subspace_in, subspace, sem)
    own_copy.start()
    copies = []
    for step in range(groups):
        first = lax.rem(group[0] + groups - step, groups) * depth
        cols = pl.ds(pl.multiple_of(first, depth), depth)
        for part in range(parts):
            rows = pl.ds(part * span, span)
            copies.append(
                pltpu.make_async_copy(
                    ritz_in.at[rows, cols], ritz.at[step, rows], sems.at[step, part]
                )
            )
            copies[-1].start()
    own_copy.wait()
    own = split(subspace[...])
    for step in range(groups):
        for part in range(parts):
            rows = slice(part * span, (part + 1) * span)
            copies[step * parts + part].wait()
            top, low = split(ritz[step, rows, :])
            if step == 0:
                high, rest = split(mul((top, low), own))
                start_out[rows, :] = dot(high, shuffle[...], NT) + dot(rest, shuffle[...], NT)
            else:
                cols = slice((step - 1) * depth, step * depth)
                top_out[rows, cols] = top
                low_out[rows, cols] = low


def rotate(top, low, columns):
    width = columns.shape[1]
    high, rest = split(columns)
    wide = dot(top, jnp.concatenate([high, rest], 1))
    return wide[:, :width] + (wide[:, width:] + dot(low, high))


def pieces(x, groups, part, axis):
    span = x.shape[axis] // (2 * (groups - 1))
    starts = [(2 * step + part) * span for step in range(groups - 1)]
    if axis == 0:
        return [x[start : start + span, :] for start in starts]
    return [x[:, start : start + span] for start in starts]


def rotate_sides(columns, top, low, groups):
    width = columns.shape[1] // 2
    span = columns.shape[0] // (groups - 1)
    whole = jnp.concatenate(
        [
            columns[step * span : (step + 1) * span, part * width : (part + 1) * width]
            for step in range(groups - 1)
            for part in range(2)
        ],
        0,
    )
    return rotate(top[...], low[...], whole)


def rotate_half(columns, top, low, groups, part):
    return rotate(
        jnp.concatenate(pieces(top, groups, part, 1), 1),
        jnp.concatenate(pieces(low, groups, part, 1), 1),
        columns[...],
    )


def rotate_far(groups, columns, start_own, top, low, pick, pair, start_out, far_out):
    duo, block = start_out.shape
    start = (start_own[:, :duo] + rotate_sides(columns, top, low, groups)).T
    start_out[...] = start
    far_out[:, :block] = sift(pick[:duo, :duo], start)
    far_out[:, block:] = pair[...]


def rotate_ring(groups, columns, start_own, start_far, top, low, pick, start_out, out_out, near_out):
    halo = out_out.shape[0]
    duo = 2 * halo
    start = (start_own[:, duo : 2 * duo] + rotate_sides(columns, top, low, groups)).T
    start = jnp.concatenate([start_far[...], start], 0)
    start_out[...] = start
    packed = sift(pick[duo:, :], start)
    out_out[...] = packed[:halo]
    near_out[...] = packed[halo:]


def rotate_low(groups, columns, start_own, top, low, rest_out):
    edge_nodes = start_own.shape[1] - columns.shape[1]
    rest_out[...] = start_own[:, edge_nodes:] + rotate_half(columns, top, low, groups, 0)


def first_part(start_edge, far_in, out_in, near_in, ham_top, ham_low, part_out, overlap_out, couple_out):
    edge_nodes = start_edge.shape[0]
    nodes = ham_top.shape[0] - 4 * out_in.shape[0]
    duo = far_in.shape[0]
    block = start_edge.shape[1]
    ghosts = jnp.concatenate([far_in[:, :block], out_in[...], near_in[...]], 0)
    part_out[...] = mul(
        (ham_top[:, :edge_nodes], ham_low[:, :edge_nodes]), split(start_edge[...])
    ) + mul((ham_top[:, nodes:], ham_low[:, nodes:]), split(ghosts))
    overlap_out[...] = SCALE_ONE * far_in[:, block : block + duo]
    couple_out[...] = far_in[:, block + duo :]


def rotate_rest(
    groups, columns, rest_low, top, low, part, ham_top, ham_low, rest_out, far_out, out_out, near_out
):
    rest = (rest_low[...] + rotate_half(columns, top, low, groups, 1)).T
    rest_out[...] = rest
    halo = out_out.shape[0]
    edge_nodes, width = part.shape[0] - 4 * halo - rest.shape[0], rest.shape[0]
    nodes = edge_nodes + width
    cols = slice(edge_nodes, nodes)
    back = part[nodes:, :] + mul((ham_top[nodes:, cols], ham_low[nodes:, cols]), split(rest))
    far_out[...] = back[: 2 * halo]
    out_out[...] = back[2 * halo : 3 * halo]
    near_out[...] = back[3 * halo :]


def first_base(
    start_edge, start_rest, part, ham_top, ham_low, pick, overlap, back_far,
    start_out, base_out, packed_out, adjust_out,
):
    nodes = ham_top.shape[0] - pick.shape[0]
    edge_nodes = start_edge.shape[0]
    cols = slice(edge_nodes, nodes)
    start = jnp.concatenate([start_edge[...], start_rest[...]], 0)
    start_out[...] = start
    own = part[:nodes, :] + mul(
        (ham_top[:nodes, cols], ham_low[:nodes, cols]), split(start_rest[...])
    )
    base = SCALE_ONE * (own - CENTRE * start)
    base_out[...] = base
    packed_out[...] = sift(pick[...], base[:edge_nodes])
    adjust_out[...] = mul(split(overlap[...]), split(back_far[...]))


def fetch_far(packed, both, out_in, near_in, far_out):
    duo = 2 * out_in.shape[0]
    back = jnp.concatenate([out_in[...], near_in[...]], 0)
    far_out[...] = packed[:duo, :] + SCALE_ONE * sift(both[:duo, duo:], back)


def fetch_ring(packed, both, far_in, out_in, near_in, out_out, near_out):
    halo = out_in.shape[0]
    back = jnp.concatenate([far_in[...], out_in[...], near_in[...]], 0)
    rows = packed[2 * halo :, :] + SCALE_ONE * sift(both[2 * halo :, :], back)
    out_out[...] = rows[:halo]
    near_out[...] = rows[halo:]


def first_own(
    base, pick, far_in, out_in, near_in, ham_top, ham_low, couple, first_out, part_out, known_out
):
    edge_nodes = pick.shape[1]
    nodes = base.shape[0]
    duo = far_in.shape[0]
    back = jnp.concatenate([far_in[...], out_in[...], near_in[...]], 0)
    edge = base[:edge_nodes, :] + SCALE_ONE * sift(pick[...].T, back)
    first = jnp.concatenate([edge, base[edge_nodes:, :]], 0)
    first_out[...] = first
    part_out[...] = mul((ham_top[:, :nodes], ham_low[:, :nodes]), split(first))
    known_out[...] = mul(split(couple[...]), split(sift(pick[:duo, :], edge)))


def return_far(part, ham_top, ham_low, out_in, near_in, far_out):
    halo = out_in.shape[0]
    nodes = part.shape[0] - 4 * halo
    far = slice(nodes, nodes + 2 * halo)
    ring = slice(nodes + 2 * halo, nodes + 4 * halo)
    ghosts = split(jnp.concatenate([out_in[...], near_in[...]], 0))
    far_out[...] = part[far, :] + mul((ham_top[far, ring], ham_low[far, ring]), ghosts)


def return_ring(
    part, ham_top, ham_low, far_in, adjust, out_in, near_in, ghosts_out, out_out, near_out
):
    halo = out_in.shape[0]
    nodes = part.shape[0] - 4 * halo
    ring = slice(nodes + 2 * halo, nodes + 4 * halo)
    ghosts = jnp.concatenate([far_in[...] + adjust[...], out_in[...], near_in[...]], 0)
    ghosts_out[...] = ghosts
    rows = part[ring, :] + mul((ham_top[ring, nodes:], ham_low[ring, nodes:]), split(ghosts))
    out_out[...] = rows[:halo]
    near_out[...] = rows[halo:]


def second_base(part, ghosts, ham_top, ham_low, first, start, known, shuffle, hits, result_out):
    nodes = first.shape[0]
    duo = known.shape[0]
    ham = (ham_top[:nodes, nodes:], ham_low[:nodes, nodes:])
    second = part[:nodes, :] + mul(ham, split(ghosts[...])) - CENTRE * first[...]
    second = SCALE_TWO * second - SIGMA_ONE * SIGMA_TWO * start[...]
    top, low = split(second.T)
    result = dot(top, shuffle[...]) + dot(low, shuffle[...])
    top, low = split(SCALE_TWO * known[...].T)
    result_out[...] = result + (dot(top, hits[:duo, :]) + dot(low, hits[:duo, :]))


def finish(result, hits, far_in, out_in, near_in, out):
    back = jnp.concatenate([far_in[...], out_in[...], near_in[...]], 0)
    top, low = split(SCALE_TWO * back.T)
    out[...] = result[...] + (dot(top, hits[...]) + dot(low, hits[...]))


def per_device(subspace, ritz, element_ham, connect, send_rows):
    depth, nodes = subspace.shape
    block = ritz.shape[0]
    slots, halo = send_rows.shape[1:]
    partitions = lax.axis_size("mesh")
    groups = lax.axis_size("state")
    across = partitions // 2
    wide = slots * halo
    duo = 2 * halo
    full = nodes + wide

    odd = (lax.axis_index("mesh") % 2).astype(I32).reshape(1)
    group = lax.axis_index("state").astype(I32).reshape(1)
    pairs_far = [(i, (i + across) % partitions) for i in range(partitions)]
    pairs_in = [(i, i ^ 1) for i in range(partitions)]
    pairs_out = [
        (i, (i + 1) % partitions if i % 2 else (i - 1) % partitions) for i in range(partitions)
    ]

    def far(rows):
        return lax.ppermute(rows, "mesh", pairs_far)

    def out(rows):
        return lax.ppermute(rows, "mesh", pairs_out)

    def near(rows):
        return lax.ppermute(rows, "mesh", pairs_in)

    def gather(rows):
        parts = [
            lax.ppermute(rows, "state", [(i, (i + step) % groups) for i in range(groups)])
            for step in range(1, groups)
        ]
        return parts[0] if len(parts) == 1 else jnp.concatenate(parts, 0)

    def rows_of(count):
        return ((count, block), F32)

    halo_out = [rows_of(duo), rows_of(halo), rows_of(halo)]
    smem = pl.BlockSpec(memory_space=pltpu.SMEM)
    vmem = pl.BlockSpec(memory_space=pltpu.VMEM)
    hbm = pl.BlockSpec(memory_space=pltpu.HBM)

    far_cols, ring_cols, low_cols, high_cols, shuffle = call(
        renumber,
        [
            ((depth // 2, 2 * duo), F32),
            ((depth // 2, 2 * duo), F32),
            ((depth // 2, nodes - wide), F32),
            ((depth // 2, nodes - wide), F32),
            ((nodes, nodes), BF16),
        ],
        in_hbm(send_rows), in_hbm(subspace),
        in_specs=[hbm, hbm],
        scratch_shapes=[
            pltpu.VMEM(send_rows.shape, I32),
            pltpu.VMEM(subspace.shape, F32),
            pltpu.SemaphoreType.DMA((2,)),
        ],
    )
    far_cols_in = gather(far_cols)
    ring_cols_in = gather(ring_cols)
    low_cols_in = gather(low_cols)
    high_cols_in = gather(high_cols)
    elems, size = connect.shape
    pitch = -(-size // 128) * 128
    blocks = jnp.transpose(element_ham, (1, 0, 2)).reshape(size * elems, size)
    ham_top, ham_low, pick, both, hits, pair = call(
        assemble,
        [
            ((full, full), BF16),
            ((full, full), BF16),
            ((wide, wide), BF16),
            ((wide, wide), BF16),
            ((wide, nodes), BF16),
            ((duo, 2 * duo), F32),
        ],
        odd, send_rows, connect, in_hbm(blocks), shuffle,
        limit=12,
        in_specs=[smem, vmem, vmem, hbm, vmem],
        scratch_shapes=[
            pltpu.VMEM(blocks.shape, F32),
            pltpu.SemaphoreType.DMA,
            pltpu.VMEM((full, elems * pitch), BF16),
            pltpu.VMEM((elems * pitch, 2 * full), BF16),
        ],
    )
    others = groups - 1
    start_own, ritz_top, ritz_low = call(
        rotate_own,
        [
            ((block, nodes), F32),
            ((block, others * depth), BF16),
            ((block, others * depth), BF16),
        ],
        group, shuffle, in_hbm(subspace), in_hbm(ritz),
        limit=12,
        in_specs=[smem, vmem, hbm, hbm],
        scratch_shapes=[
            pltpu.VMEM(subspace.shape, F32),
            pltpu.VMEM((groups, block, depth), F32),
            pltpu.SemaphoreType.DMA,
            pltpu.SemaphoreType.DMA((groups, 2)),
        ],
    )

    start_far, far_rows = call(
        functools.partial(rotate_far, groups),
        [rows_of(duo), ((duo, block + 2 * duo), F32)],
        far_cols_in, start_own, ritz_top, ritz_low, pick, pair,
    )
    far_in = far(far_rows)
    start_edge, out_rows, near_rows = call(
        functools.partial(rotate_ring, groups),
        [rows_of(wide), rows_of(halo), rows_of(halo)],
        ring_cols_in, start_own, start_far, ritz_top, ritz_low, pick,
    )
    out_in, near_in = out(out_rows), near(near_rows)
    part, overlap, couple = call(
        first_part,
        [rows_of(full), ((duo, duo), F32), ((duo, duo), F32)],
        start_edge, far_in, out_in, near_in, ham_top, ham_low,
    )
    (rest_low,) = call(
        functools.partial(rotate_low, groups),
        [((block, nodes - wide), F32)],
        low_cols_in, start_own, ritz_top, ritz_low,
    )

    start_rest, back_far, back_out, back_near = call(
        functools.partial(rotate_rest, groups),
        [rows_of(nodes - wide)] + halo_out,
        high_cols_in, rest_low, ritz_top, ritz_low, part, ham_top, ham_low,
    )
    far_in, out_in, near_in = far(back_far), out(back_out), near(back_near)
    start, base, packed, adjust = call(
        first_base,
        [rows_of(nodes), rows_of(nodes), rows_of(wide), rows_of(duo)],
        start_edge, start_rest, part, ham_top, ham_low, pick, overlap, back_far,
    )
    (far_rows,) = call(fetch_far, [rows_of(duo)], packed, both, out_in, near_in)
    fetched_far = far(far_rows)
    out_rows, near_rows = call(
        fetch_ring, halo_out[1:], packed, both, far_in, out_in, near_in
    )
    fetched_out, fetched_near = out(out_rows), near(near_rows)
    first, part, known = call(
        first_own,
        [rows_of(nodes), rows_of(full), rows_of(duo)],
        base, pick, far_in, out_in, near_in, ham_top, ham_low, couple,
    )

    (far_rows,) = call(
        return_far, [rows_of(duo)], part, ham_top, ham_low, fetched_out, fetched_near
    )
    returned_far = far(far_rows)
    ghosts, out_rows, near_rows = call(
        return_ring,
        [rows_of(wide)] + halo_out[1:],
        part, ham_top, ham_low, fetched_far, adjust, fetched_out, fetched_near,
    )
    returned_out, returned_near = out(out_rows), near(near_rows)
    (result,) = call(
        second_base,
        [((block, nodes), F32)],
        part, ghosts, ham_top, ham_low, first, start, known, shuffle, hits,
    )
    (result,) = call(
        finish, [((block, nodes), F32)], result, hits, returned_far, returned_out, returned_near
    )
    return result


def solution(mesh):
    in_specs = (
        P("state", "mesh"),
        P("state", None),
        P("mesh", None, None),
        P("mesh", None),
        P("mesh", None, None),
    )
    out_specs = P("state", "mesh")
    return jax.shard_map(
        per_device, mesh=mesh, in_specs=in_specs, out_specs=out_specs, check_vma=False
    )
```

```python
import functools

import jax
import jax.numpy as jnp
from jax import lax
from jax.experimental import pallas as pl
from jax.experimental.pallas import tpu as pltpu
from jax.sharding import PartitionSpec as P

F32 = jnp.float32
BF16 = jnp.bfloat16
I32 = jnp.int32
NN = ((1,), (0,))
NT = ((1,), (1,))

HALF = 1.5
CENTRE = 2.5
SIGMA_ONE = HALF / (-1.0 - CENTRE)
SIGMA_TWO = 1.0 / (2.0 / SIGMA_ONE - SIGMA_ONE)
SCALE_ONE = SIGMA_ONE / HALF
SCALE_TWO = 2.0 * SIGMA_TWO / HALF


def dot(a, b, dims=NN):
    return lax.dot_general(a, b, (dims, ((), ())), preferred_element_type=F32)


def split(x):
    top = x.astype(BF16)
    return top, (x - top.astype(F32)).astype(BF16)


def mul(a, b, dims=NN):
    return dot(a[0], b[0], dims) + (dot(a[0], b[1], dims) + dot(a[1], b[0], dims))


def sift(a, x):
    top, low = split(x)
    return dot(a, top) + dot(a, low)


def call(body, outs, *args, limit=8, **rest):
    return pl.pallas_call(
        body,
        out_shape=[jax.ShapeDtypeStruct(*out) for out in outs],
        compiler_params=pltpu.CompilerParams(vmem_limit_bytes=limit << 20),
        **rest,
    )(*args)


def in_hbm(x):
    return pltpu.with_memory_space_constraint(x, pltpu.HBM)


def column(row, width):
    down = lax.broadcasted_iota(I32, (width, width), 0)
    along = lax.broadcasted_iota(I32, (width, width), 1)
    return jnp.sum(jnp.where(down == along, row, 0), axis=1, keepdims=True)


def renumber(
    lists_in, subspace_in, far_out, ring_out, low_out, high_out, shuffle_out, lists, subspace, sems
):
    slots, halo = lists.shape[1:]
    depth, nodes = subspace.shape
    duo = 2 * halo
    span = depth // 2
    index_copy = pltpu.make_async_copy(lists_in, lists, sems.at[0])
    index_copy.start()
    copy = pltpu.make_async_copy(subspace_in, subspace, sems.at[1])
    copy.start()
    index_copy.wait()
    ids = lax.broadcasted_iota(I32, (halo, nodes), 1)
    seen = []
    for slot in range(slots):
        sent = column(lists[0, slot : slot + 1, :], halo)
        seen.append(jnp.where(sent == ids, 1.0, 0.0))
    far = jnp.max(jnp.maximum(seen[2], seen[3]), axis=0, keepdims=True)
    ring = jnp.max(jnp.maximum(seen[0], seen[1]), axis=0, keepdims=True) * (1.0 - far)
    down = lax.broadcasted_iota(I32, (nodes, nodes), 0)
    along = lax.broadcasted_iota(I32, (nodes, nodes), 1)
    upto = jnp.where(down <= along, 1.0, 0.0).astype(BF16)
    flags = jnp.concatenate([far, ring, jnp.zeros((6, nodes), F32)], 0)
    counts = dot(flags.astype(BF16), upto).astype(I32)
    far_count, ring_count = counts[0:1], counts[1:2]
    totals = jnp.sum(flags, axis=1, keepdims=True).astype(I32)
    far_total, ring_total = totals[0:1], totals[1:2]
    place = jnp.where(
        far > 0.5,
        far_count - 1,
        jnp.where(
            ring > 0.5,
            far_total + ring_count - 1,
            far_total + ring_total + along[:1] - far_count - ring_count,
        ),
    )
    match = place == down
    shuffle = jnp.where(match, 1.0, 0.0).astype(BF16)
    shuffle_out[...] = shuffle
    copy.wait()
    halves = []
    for part, rest_out in enumerate((low_out, high_out)):
        top, low = split(subspace[part * span : (part + 1) * span, :])
        turned = dot(top, shuffle, NT) + dot(low, shuffle, NT)
        rest_out[...] = turned[:, 2 * duo :]
        halves.append(turned)
    far_out[...] = jnp.concatenate([half[:, :duo] for half in halves], 1)
    ring_out[...] = jnp.concatenate([half[:, duo : 2 * duo] for half in halves], 1)


def assemble(
    odd, lists, connect, blocks_in, shuffle, top_out, low_out, pick_out, both_out, hits_out, pair_out,
    blocks, sem, spread, rows_both,
):
    copy = pltpu.make_async_copy(blocks_in, blocks, sem)
    copy.start()
    elems, size = connect.shape
    slots, halo = lists.shape[1:]
    nodes = shuffle.shape[0]
    wide = slots * halo
    duo = 2 * halo
    swap = odd[0] == 1
    columns = [column(lists[0, slot : slot + 1, :], halo) for slot in range(slots)]
    outer = jnp.where(swap, columns[0], columns[1])
    inner = jnp.where(swap, columns[1], columns[0])
    sent = jnp.concatenate([columns[2], columns[3], outer, inner], 0)
    hits = jnp.where(sent == lax.broadcasted_iota(I32, (wide, nodes), 1), 1.0, 0.0).astype(BF16)
    hits_out[...] = hits
    pick = dot(hits, shuffle[:wide, :], NT).astype(BF16)
    pick_out[...] = pick
    both = dot(pick, pick, NT)
    both_out[...] = both.astype(BF16)

    lane = lax.broadcasted_iota(I32, (halo, 1), 0)
    flag = odd[0]
    ghost = jnp.concatenate(
        [3 * halo + lane, 2 * halo + lane, (1 - flag) * halo + lane, flag * halo + lane], 0
    )
    along = lax.broadcasted_iota(I32, (nodes, nodes), 1).astype(F32)
    origin = jnp.sum(along * shuffle[...].astype(F32), axis=1, keepdims=True).astype(I32)
    pitch = spread.shape[1] // elems
    full = nodes + wide
    numbers = jnp.broadcast_to(jnp.concatenate([origin, nodes + ghost], 0), (full, pitch))
    copy.wait()
    for elem in range(elems):
        cols = slice(elem * pitch, (elem + 1) * pitch)
        wanted = jnp.pad(connect[elem : elem + 1, :], ((0, 0), (0, pitch - size)), constant_values=-1)
        chosen = jnp.where(numbers == wanted, 1.0, 0.0).astype(BF16)
        spread[:, cols] = chosen
        block = blocks[pl.ds(elem, size, stride=elems), :]
        top, low = split(jnp.pad(block, ((0, pitch - size), (0, pitch - size))))
        rows = dot(jnp.concatenate([top, low], 0), chosen, NT)
        top, low = split(rows[:pitch] + rows[pitch:])
        rows_both[cols, :full] = top
        rows_both[cols, full:] = low
    ham = dot(spread[...], rows_both[...])
    ham = ham[:, :full] + ham[:, full:]
    top, low = split(ham)
    top_out[...] = top
    low_out[...] = low
    far = slice(nodes, nodes + duo)
    pair_out[...] = jnp.concatenate([both[:duo, :duo], ham[far, far]], 1)


def rotate_own(
    group, shuffle, subspace_in, ritz_in, start_out, top_out, low_out, subspace, ritz, sem, sems
):
    block, depth = ritz.shape[1:]
    groups = ritz.shape[0]
    parts = sems.shape[1]
    span = block // parts
    own_copy = pltpu.make_async_copy(subspace_in, subspace, sem)
    own_copy.start()
    copies = []
    for step in range(groups):
        first = lax.rem(group[0] + groups - step, groups) * depth
        cols = pl.ds(pl.multiple_of(first, depth), depth)
        for part in range(parts):
            rows = pl.ds(part * span, span)
            copies.append(
                pltpu.make_async_copy(
                    ritz_in.at[rows, cols], ritz.at[step, rows], sems.at[step, part]
                )
            )
            copies[-1].start()
    own_copy.wait()
    own = split(subspace[...])
    for step in range(groups):
        for part in range(parts):
            rows = slice(part * span, (part + 1) * span)
            copies[step * parts + part].wait()
            top, low = split(ritz[step, rows, :])
            if step == 0:
                high, rest = split(mul((top, low), own))
                start_out[rows, :] = dot(high, shuffle[...], NT) + dot(rest, shuffle[...], NT)
            else:
                cols = slice((step - 1) * depth, step * depth)
                top_out[rows, cols] = top
                low_out[rows, cols] = low


def rotate(top, low, columns):
    width = columns.shape[1]
    high, rest = split(columns)
    wide = dot(top, jnp.concatenate([high, rest], 1))
    return wide[:, :width] + (wide[:, width:] + dot(low, high))


def pieces(x, groups, part, axis):
    span = x.shape[axis] // (2 * (groups - 1))
    starts = [(2 * step + part) * span for step in range(groups - 1)]
    if axis == 0:
        return [x[start : start + span, :] for start in starts]
    return [x[:, start : start + span] for start in starts]


def rotate_sides(columns, top, low, groups):
    width = columns.shape[1] // 2
    span = columns.shape[0] // (groups - 1)
    whole = jnp.concatenate(
        [
            columns[step * span : (step + 1) * span, part * width : (part + 1) * width]
            for step in range(groups - 1)
            for part in range(2)
        ],
        0,
    )
    return rotate(top[...], low[...], whole)


def rotate_half(columns, top, low, groups, part):
    return rotate(
        jnp.concatenate(pieces(top, groups, part, 1), 1),
        jnp.concatenate(pieces(low, groups, part, 1), 1),
        columns[...],
    )


def rotate_far(groups, columns, start_own, top, low, pick, pair, start_out, far_out):
    duo, block = start_out.shape
    start = (start_own[:, :duo] + rotate_sides(columns, top, low, groups)).T
    start_out[...] = start
    far_out[:, :block] = sift(pick[:duo, :duo], start)
    far_out[:, block:] = pair[...]


def rotate_ring(groups, columns, start_own, start_far, top, low, pick, start_out, out_out, near_out):
    halo = out_out.shape[0]
    duo = 2 * halo
    start = (start_own[:, duo : 2 * duo] + rotate_sides(columns, top, low, groups)).T
    start = jnp.concatenate([start_far[...], start], 0)
    start_out[...] = start
    packed = sift(pick[duo:, :], start)
    out_out[...] = packed[:halo]
    near_out[...] = packed[halo:]


def rotate_low(groups, columns, start_own, top, low, rest_out):
    edge_nodes = start_own.shape[1] - columns.shape[1]
    rest_out[...] = start_own[:, edge_nodes:] + rotate_half(columns, top, low, groups, 0)


def first_part(start_edge, far_in, out_in, near_in, ham_top, ham_low, part_out, overlap_out, couple_out):
    edge_nodes = start_edge.shape[0]
    nodes = ham_top.shape[0] - 4 * out_in.shape[0]
    duo = far_in.shape[0]
    block = start_edge.shape[1]
    ghosts = jnp.concatenate([far_in[:, :block], out_in[...], near_in[...]], 0)
    part_out[...] = mul(
        (ham_top[:, :edge_nodes], ham_low[:, :edge_nodes]), split(start_edge[...])
    ) + mul((ham_top[:, nodes:], ham_low[:, nodes:]), split(ghosts))
    overlap_out[...] = SCALE_ONE * far_in[:, block : block + duo]
    couple_out[...] = far_in[:, block + duo :]


def rotate_rest(
    groups, columns, rest_low, top, low, part, ham_top, ham_low, rest_out, far_out, out_out, near_out
):
    rest = (rest_low[...] + rotate_half(columns, top, low, groups, 1)).T
    rest_out[...] = rest
    halo = out_out.shape[0]
    edge_nodes, width = part.shape[0] - 4 * halo - rest.shape[0], rest.shape[0]
    nodes = edge_nodes + width
    cols = slice(edge_nodes, nodes)
    back = part[nodes:, :] + mul((ham_top[nodes:, cols], ham_low[nodes:, cols]), split(rest))
    far_out[...] = back[: 2 * halo]
    out_out[...] = back[2 * halo : 3 * halo]
    near_out[...] = back[3 * halo :]


def first_base(
    start_edge, start_rest, part, ham_top, ham_low, pick, overlap, back_far,
    start_out, base_out, packed_out, adjust_out,
):
    nodes = ham_top.shape[0] - pick.shape[0]
    edge_nodes = start_edge.shape[0]
    cols = slice(edge_nodes, nodes)
    start = jnp.concatenate([start_edge[...], start_rest[...]], 0)
    start_out[...] = start
    own = part[:nodes, :] + mul(
        (ham_top[:nodes, cols], ham_low[:nodes, cols]), split(start_rest[...])
    )
    base = SCALE_ONE * (own - CENTRE * start)
    base_out[...] = base
    packed_out[...] = sift(pick[...], base[:edge_nodes])
    adjust_out[...] = mul(split(overlap[...]), split(back_far[...]))


def fetch_far(packed, both, out_in, near_in, far_out):
    duo = 2 * out_in.shape[0]
    back = jnp.concatenate([out_in[...], near_in[...]], 0)
    far_out[...] = packed[:duo, :] + SCALE_ONE * sift(both[:duo, duo:], back)


def fetch_ring(packed, both, far_in, out_in, near_in, out_out, near_out):
    halo = out_in.shape[0]
    back = jnp.concatenate([far_in[...], out_in[...], near_in[...]], 0)
    rows = packed[2 * halo :, :] + SCALE_ONE * sift(both[2 * halo :, :], back)
    out_out[...] = rows[:halo]
    near_out[...] = rows[halo:]


def first_own(
    base, pick, far_in, out_in, near_in, ham_top, ham_low, couple, first_out, part_out, known_out
):
    edge_nodes = pick.shape[1]
    nodes = base.shape[0]
    duo = far_in.shape[0]
    back = jnp.concatenate([far_in[...], out_in[...], near_in[...]], 0)
    edge = base[:edge_nodes, :] + SCALE_ONE * sift(pick[...].T, back)
    first = jnp.concatenate([edge, base[edge_nodes:, :]], 0)
    first_out[...] = first
    part_out[...] = mul((ham_top[:, :nodes], ham_low[:, :nodes]), split(first))
    known_out[...] = mul(split(couple[...]), split(sift(pick[:duo, :], edge)))


def return_far(part, ham_top, ham_low, out_in, near_in, far_out):
    halo = out_in.shape[0]
    nodes = part.shape[0] - 4 * halo
    far = slice(nodes, nodes + 2 * halo)
    ring = slice(nodes + 2 * halo, nodes + 4 * halo)
    ghosts = split(jnp.concatenate([out_in[...], near_in[...]], 0))
    far_out[...] = part[far, :] + mul((ham_top[far, ring], ham_low[far, ring]), ghosts)


def return_ring(
    part, ham_top, ham_low, far_in, adjust, out_in, near_in, ghosts_out, out_out, near_out
):
    halo = out_in.shape[0]
    nodes = part.shape[0] - 4 * halo
    ring = slice(nodes + 2 * halo, nodes + 4 * halo)
    ghosts = jnp.concatenate([far_in[...] + adjust[...], out_in[...], near_in[...]], 0)
    ghosts_out[...] = ghosts
    rows = part[ring, :] + mul((ham_top[ring, nodes:], ham_low[ring, nodes:]), split(ghosts))
    out_out[...] = rows[:halo]
    near_out[...] = rows[halo:]


def second_base(part, ghosts, ham_top, ham_low, first, start, known, shuffle, hits, result_out):
    nodes = first.shape[0]
    duo = known.shape[0]
    ham = (ham_top[:nodes, nodes:], ham_low[:nodes, nodes:])
    second = part[:nodes, :] + mul(ham, split(ghosts[...])) - CENTRE * first[...]
    second = SCALE_TWO * second - SIGMA_ONE * SIGMA_TWO * start[...]
    top, low = split(second.T)
    result = dot(top, shuffle[...]) + dot(low, shuffle[...])
    top, low = split(SCALE_TWO * known[...].T)
    result_out[...] = result + (dot(top, hits[:duo, :]) + dot(low, hits[:duo, :]))


def finish(result, hits, far_in, out_in, near_in, out):
    back = jnp.concatenate([far_in[...], out_in[...], near_in[...]], 0)
    top, low = split(SCALE_TWO * back.T)
    out[...] = result[...] + (dot(top, hits[...]) + dot(low, hits[...]))


def per_device(subspace, ritz, element_ham, connect, send_rows):
    depth, nodes = subspace.shape
    block = ritz.shape[0]
    slots, halo = send_rows.shape[1:]
    partitions = lax.axis_size("mesh")
    groups = lax.axis_size("state")
    across = partitions // 2
    wide = slots * halo
    duo = 2 * halo
    full = nodes + wide

    odd = (lax.axis_index("mesh") % 2).astype(I32).reshape(1)
    group = lax.axis_index("state").astype(I32).reshape(1)
    pairs_far = [(i, (i + across) % partitions) for i in range(partitions)]
    pairs_in = [(i, i ^ 1) for i in range(partitions)]
    pairs_out = [
        (i, (i + 1) % partitions if i % 2 else (i - 1) % partitions) for i in range(partitions)
    ]

    def far(rows):
        return lax.ppermute(rows, "mesh", pairs_far)

    def out(rows):
        return lax.ppermute(rows, "mesh", pairs_out)

    def near(rows):
        return lax.ppermute(rows, "mesh", pairs_in)

    def gather(rows):
        parts = [
            lax.ppermute(rows, "state", [(i, (i + step) % groups) for i in range(groups)])
            for step in range(1, groups)
        ]
        return parts[0] if len(parts) == 1 else jnp.concatenate(parts, 0)

    def rows_of(count):
        return ((count, block), F32)

    halo_out = [rows_of(duo), rows_of(halo), rows_of(halo)]
    smem = pl.BlockSpec(memory_space=pltpu.SMEM)
    vmem = pl.BlockSpec(memory_space=pltpu.VMEM)
    hbm = pl.BlockSpec(memory_space=pltpu.HBM)

    far_cols, ring_cols, low_cols, high_cols, shuffle = call(
        renumber,
        [
            ((depth // 2, 2 * duo), F32),
            ((depth // 2, 2 * duo), F32),
            ((depth // 2, nodes - wide), F32),
            ((depth // 2, nodes - wide), F32),
            ((nodes, nodes), BF16),
        ],
        in_hbm(send_rows), in_hbm(subspace),
        in_specs=[hbm, hbm],
        scratch_shapes=[
            pltpu.VMEM(send_rows.shape, I32),
            pltpu.VMEM(subspace.shape, F32),
            pltpu.SemaphoreType.DMA((2,)),
        ],
    )
    far_cols_in = gather(far_cols)
    ring_cols_in = gather(ring_cols)
    low_cols_in = gather(low_cols)
    high_cols_in = gather(high_cols)
    elems, size = connect.shape
    pitch = -(-size // 128) * 128
    blocks = jnp.transpose(element_ham, (1, 0, 2)).reshape(size * elems, size)
    ham_top, ham_low, pick, both, hits, pair = call(
        assemble,
        [
            ((full, full), BF16),
            ((full, full), BF16),
            ((wide, wide), BF16),
            ((wide, wide), BF16),
            ((wide, nodes), BF16),
            ((duo, 2 * duo), F32),
        ],
        odd, send_rows, connect, in_hbm(blocks), shuffle,
        limit=12,
        in_specs=[smem, vmem, vmem, hbm, vmem],
        scratch_shapes=[
            pltpu.VMEM(blocks.shape, F32),
            pltpu.SemaphoreType.DMA,
            pltpu.VMEM((full, elems * pitch), BF16),
            pltpu.VMEM((elems * pitch, 2 * full), BF16),
        ],
    )
    others = groups - 1
    start_own, ritz_top, ritz_low = call(
        rotate_own,
        [
            ((block, nodes), F32),
            ((block, others * depth), BF16),
            ((block, others * depth), BF16),
        ],
        group, shuffle, in_hbm(subspace), in_hbm(ritz),
        limit=12,
        in_specs=[smem, vmem, hbm, hbm],
        scratch_shapes=[
            pltpu.VMEM(subspace.shape, F32),
            pltpu.VMEM((groups, block, depth), F32),
            pltpu.SemaphoreType.DMA,
            pltpu.SemaphoreType.DMA((groups, 2)),
        ],
    )

    start_far, far_rows = call(
        functools.partial(rotate_far, groups),
        [rows_of(duo), ((duo, block + 2 * duo), F32)],
        far_cols_in, start_own, ritz_top, ritz_low, pick, pair,
    )
    far_in = far(far_rows)
    start_edge, out_rows, near_rows = call(
        functools.partial(rotate_ring, groups),
        [rows_of(wide), rows_of(halo), rows_of(halo)],
        ring_cols_in, start_own, start_far, ritz_top, ritz_low, pick,
    )
    out_in, near_in = out(out_rows), near(near_rows)
    part, overlap, couple = call(
        first_part,
        [rows_of(full), ((duo, duo), F32), ((duo, duo), F32)],
        start_edge, far_in, out_in, near_in, ham_top, ham_low,
    )
    (rest_low,) = call(
        functools.partial(rotate_low, groups),
        [((block, nodes - wide), F32)],
        low_cols_in, start_own, ritz_top, ritz_low,
    )

    start_rest, back_far, back_out, back_near = call(
        functools.partial(rotate_rest, groups),
        [rows_of(nodes - wide)] + halo_out,
        high_cols_in, rest_low, ritz_top, ritz_low, part, ham_top, ham_low,
    )
    far_in, out_in, near_in = far(back_far), out(back_out), near(back_near)
    start, base, packed, adjust = call(
        first_base,
        [rows_of(nodes), rows_of(nodes), rows_of(wide), rows_of(duo)],
        start_edge, start_rest, part, ham_top, ham_low, pick, overlap, back_far,
    )
    (far_rows,) = call(fetch_far, [rows_of(duo)], packed, both, out_in, near_in)
    fetched_far = far(far_rows)
    out_rows, near_rows = call(
        fetch_ring, halo_out[1:], packed, both, far_in, out_in, near_in
    )
    fetched_out, fetched_near = out(out_rows), near(near_rows)
    first, part, known = call(
        first_own,
        [rows_of(nodes), rows_of(full), rows_of(duo)],
        base, pick, far_in, out_in, near_in, ham_top, ham_low, couple,
    )

    (far_rows,) = call(
        return_far, [rows_of(duo)], part, ham_top, ham_low, fetched_out, fetched_near
    )
    returned_far = far(far_rows)
    ghosts, out_rows, near_rows = call(
        return_ring,
        [rows_of(wide)] + halo_out[1:],
        part, ham_top, ham_low, fetched_far, adjust, fetched_out, fetched_near,
    )
    returned_out, returned_near = out(out_rows), near(near_rows)
    (result,) = call(
        second_base,
        [((block, nodes), F32)],
        part, ghosts, ham_top, ham_low, first, start, known, shuffle, hits,
    )
    (result,) = call(
        finish, [((block, nodes), F32)], result, hits, returned_far, returned_out, returned_near
    )
    return result


def solution(mesh):
    in_specs = (
        P("state", "mesh"),
        P("state", None),
        P("mesh", None, None),
        P("mesh", None),
        P("mesh", None, None),
    )
    out_specs = P("state", "mesh")
    return jax.shard_map(
        per_device, mesh=mesh, in_specs=in_specs, out_specs=out_specs, check_vma=False
    )
```

```python
import functools

import jax
import jax.numpy as jnp
from jax import lax
from jax.experimental import pallas as pl
from jax.experimental.pallas import tpu as pltpu
from jax.sharding import PartitionSpec as P

F32 = jnp.float32
BF16 = jnp.bfloat16
I32 = jnp.int32
NN = ((1,), (0,))
NT = ((1,), (1,))

HALF = 1.5
CENTRE = 2.5
SIGMA_ONE = HALF / (-1.0 - CENTRE)
SIGMA_TWO = 1.0 / (2.0 / SIGMA_ONE - SIGMA_ONE)
SCALE_ONE = SIGMA_ONE / HALF
SCALE_TWO = 2.0 * SIGMA_TWO / HALF


def dot(a, b, dims=NN):
    return lax.dot_general(a, b, (dims, ((), ())), preferred_element_type=F32)


def split(x):
    top = x.astype(BF16)
    return top, (x - top.astype(F32)).astype(BF16)


def mul(a, b, dims=NN):
    return dot(a[0], b[0], dims) + (dot(a[0], b[1], dims) + dot(a[1], b[0], dims))


def sift(a, x):
    top, low = split(x)
    return dot(a, top) + dot(a, low)


def call(body, outs, *args, limit=8, **rest):
    return pl.pallas_call(
        body,
        out_shape=[jax.ShapeDtypeStruct(*out) for out in outs],
        compiler_params=pltpu.CompilerParams(vmem_limit_bytes=limit << 20),
        **rest,
    )(*args)


def in_hbm(x):
    return pltpu.with_memory_space_constraint(x, pltpu.HBM)


def column(row, width):
    down = lax.broadcasted_iota(I32, (width, width), 0)
    along = lax.broadcasted_iota(I32, (width, width), 1)
    return jnp.sum(jnp.where(down == along, row, 0), axis=1, keepdims=True)


def renumber(
    lists_in, subspace_in, far_out, ring_out, low_out, high_out, shuffle_out, lists, subspace, sems
):
    slots, halo = lists.shape[1:]
    depth, nodes = subspace.shape
    duo = 2 * halo
    span = depth // 2
    index_copy = pltpu.make_async_copy(lists_in, lists, sems.at[0])
    index_copy.start()
    copy = pltpu.make_async_copy(subspace_in, subspace, sems.at[1])
    copy.start()
    index_copy.wait()
    ids = lax.broadcasted_iota(I32, (halo, nodes), 1)
    seen = []
    for slot in range(slots):
        sent = column(lists[0, slot : slot + 1, :], halo)
        seen.append(jnp.where(sent == ids, 1.0, 0.0))
    far = jnp.max(jnp.maximum(seen[2], seen[3]), axis=0, keepdims=True)
    ring = jnp.max(jnp.maximum(seen[0], seen[1]), axis=0, keepdims=True) * (1.0 - far)
    down = lax.broadcasted_iota(I32, (nodes, nodes), 0)
    along = lax.broadcasted_iota(I32, (nodes, nodes), 1)
    upto = jnp.where(down <= along, 1.0, 0.0).astype(BF16)
    flags = jnp.concatenate([far, ring, jnp.zeros((6, nodes), F32)], 0)
    counts = dot(flags.astype(BF16), upto).astype(I32)
    far_count, ring_count = counts[0:1], counts[1:2]
    totals = jnp.sum(flags, axis=1, keepdims=True).astype(I32)
    far_total, ring_total = totals[0:1], totals[1:2]
    place = jnp.where(
        far > 0.5,
        far_count - 1,
        jnp.where(
            ring > 0.5,
            far_total + ring_count - 1,
            far_total + ring_total + along[:1] - far_count - ring_count,
        ),
    )
    match = place == down
    shuffle = jnp.where(match, 1.0, 0.0).astype(BF16)
    shuffle_out[...] = shuffle
    copy.wait()
    halves = []
    for part, rest_out in enumerate((low_out, high_out)):
        top, low = split(subspace[part * span : (part + 1) * span, :])
        turned = dot(top, shuffle, NT) + dot(low, shuffle, NT)
        rest_out[...] = turned[:, 2 * duo :]
        halves.append(turned)
    far_out[...] = jnp.concatenate([half[:, :duo] for half in halves], 1)
    ring_out[...] = jnp.concatenate([half[:, duo : 2 * duo] for half in halves], 1)


def assemble(
    odd, lists, connect, blocks_in, shuffle, top_out, low_out, pick_out, both_out, hits_out, pair_out,
    blocks, sem, spread, rows_both,
):
    copy = pltpu.make_async_copy(blocks_in, blocks, sem)
    copy.start()
    elems, size = connect.shape
    slots, halo = lists.shape[1:]
    nodes = shuffle.shape[0]
    wide = slots * halo
    duo = 2 * halo
    swap = odd[0] == 1
    columns = [column(lists[0, slot : slot + 1, :], halo) for slot in range(slots)]
    outer = jnp.where(swap, columns[0], columns[1])
    inner = jnp.where(swap, columns[1], columns[0])
    sent = jnp.concatenate([columns[2], columns[3], outer, inner], 0)
    hits = jnp.where(sent == lax.broadcasted_iota(I32, (wide, nodes), 1), 1.0, 0.0).astype(BF16)
    hits_out[...] = hits
    pick = dot(hits, shuffle[:wide, :], NT).astype(BF16)
    pick_out[...] = pick
    both = dot(pick, pick, NT)
    both_out[...] = both.astype(BF16)

    lane = lax.broadcasted_iota(I32, (halo, 1), 0)
    flag = odd[0]
    ghost = jnp.concatenate(
        [3 * halo + lane, 2 * halo + lane, (1 - flag) * halo + lane, flag * halo + lane], 0
    )
    along = lax.broadcasted_iota(I32, (nodes, nodes), 1).astype(F32)
    origin = jnp.sum(along * shuffle[...].astype(F32), axis=1, keepdims=True).astype(I32)
    pitch = spread.shape[1] // elems
    full = nodes + wide
    numbers = jnp.broadcast_to(jnp.concatenate([origin, nodes + ghost], 0), (full, pitch))
    copy.wait()
    for elem in range(elems):
        cols = slice(elem * pitch, (elem + 1) * pitch)
        wanted = jnp.pad(connect[elem : elem + 1, :], ((0, 0), (0, pitch - size)), constant_values=-1)
        chosen = jnp.where(numbers == wanted, 1.0, 0.0).astype(BF16)
        spread[:, cols] = chosen
        block = blocks[pl.ds(elem, size, stride=elems), :]
        top, low = split(jnp.pad(block, ((0, pitch - size), (0, pitch - size))))
        rows = dot(jnp.concatenate([top, low], 0), chosen, NT)
        top, low = split(rows[:pitch] + rows[pitch:])
        rows_both[cols, :full] = top
        rows_both[cols, full:] = low
    ham = dot(spread[...], rows_both[...])
    ham = ham[:, :full] + ham[:, full:]
    top, low = split(ham)
    top_out[...] = top
    low_out[...] = low
    far = slice(nodes, nodes + duo)
    pair_out[...] = jnp.concatenate([both[:duo, :duo], ham[far, far]], 1)


def rotate_own(
    group, shuffle, subspace_in, ritz_in, start_out, top_out, low_out, subspace, ritz, sems
):
    block, depth = ritz.shape[1:]
    groups = ritz.shape[0]
    parts = sems.shape[1]
    span = depth // parts
    copies = []
    for step in range(groups):
        first = lax.rem(group[0] + groups - step, groups) * depth
        for part in range(parts):
            if step == 0:
                rows = pl.ds(part * span, span)
                copies.append(
                    pltpu.make_async_copy(
                        subspace_in.at[rows], subspace.at[rows], sems.at[groups, part]
                    )
                )
                copies[-1].start()
            cols = pl.ds(pl.multiple_of(first + part * span, span), span)
            copies.append(
                pltpu.make_async_copy(
                    ritz_in.at[:, cols],
                    ritz.at[step, :, pl.ds(part * span, span)],
                    sems.at[step, part],
                )
            )
            copies[-1].start()
    total = None
    for part in range(parts):
        here = slice(part * span, (part + 1) * span)
        copies[2 * part].wait()
        copies[2 * part + 1].wait()
        term = mul(split(ritz[0, :, here]), split(subspace[here, :]))
        total = term if total is None else total + term
    top, low = split(total)
    start_out[...] = dot(top, shuffle[...], NT) + dot(low, shuffle[...], NT)
    for step in range(1, groups):
        for part in range(parts):
            copies[parts + step * parts + part].wait()
            top, low = split(ritz[step, :, part * span : (part + 1) * span])
            cols = slice((step - 1) * depth + part * span, (step - 1) * depth + (part + 1) * span)
            top_out[:, cols] = top
            low_out[:, cols] = low


def rotate(top, low, columns):
    width = columns.shape[1]
    high, rest = split(columns)
    wide = dot(top, jnp.concatenate([high, rest], 1))
    return wide[:, :width] + (wide[:, width:] + dot(low, high))


def pieces(x, groups, part, axis):
    span = x.shape[axis] // (2 * (groups - 1))
    starts = [(2 * step + part) * span for step in range(groups - 1)]
    if axis == 0:
        return [x[start : start + span, :] for start in starts]
    return [x[:, start : start + span] for start in starts]


def rotate_sides(columns, top, low, groups):
    width = columns.shape[1] // 2
    span = columns.shape[0] // (groups - 1)
    whole = jnp.concatenate(
        [
            columns[step * span : (step + 1) * span, part * width : (part + 1) * width]
            for step in range(groups - 1)
            for part in range(2)
        ],
        0,
    )
    return rotate(top[...], low[...], whole)


def rotate_half(columns, top, low, groups, part):
    return rotate(
        jnp.concatenate(pieces(top, groups, part, 1), 1),
        jnp.concatenate(pieces(low, groups, part, 1), 1),
        columns[...],
    )


def rotate_far(groups, columns, start_own, top, low, pick, pair, start_out, far_out):
    duo, block = start_out.shape
    start = (start_own[:, :duo] + rotate_sides(columns, top, low, groups)).T
    start_out[...] = start
    far_out[:, :block] = sift(pick[:duo, :duo], start)
    far_out[:, block:] = pair[...]


def rotate_ring(groups, columns, start_own, start_far, top, low, pick, start_out, out_out, near_out):
    halo = out_out.shape[0]
    duo = 2 * halo
    start = (start_own[:, duo : 2 * duo] + rotate_sides(columns, top, low, groups)).T
    start = jnp.concatenate([start_far[...], start], 0)
    start_out[...] = start
    packed = sift(pick[duo:, :], start)
    out_out[...] = packed[:halo]
    near_out[...] = packed[halo:]


def rotate_low(groups, columns, start_own, top, low, rest_out):
    edge_nodes = start_own.shape[1] - columns.shape[1]
    rest_out[...] = start_own[:, edge_nodes:] + rotate_half(columns, top, low, groups, 0)


def first_part(start_edge, far_in, out_in, near_in, ham_top, ham_low, part_out, overlap_out, couple_out):
    edge_nodes = start_edge.shape[0]
    nodes = ham_top.shape[0] - 4 * out_in.shape[0]
    duo = far_in.shape[0]
    block = start_edge.shape[1]
    ghosts = jnp.concatenate([far_in[:, :block], out_in[...], near_in[...]], 0)
    part_out[...] = mul(
        (ham_top[:, :edge_nodes], ham_low[:, :edge_nodes]), split(start_edge[...])
    ) + mul((ham_top[:, nodes:], ham_low[:, nodes:]), split(ghosts))
    overlap_out[...] = SCALE_ONE * far_in[:, block : block + duo]
    couple_out[...] = far_in[:, block + duo :]


def rotate_rest(
    groups, columns, rest_low, top, low, part, ham_top, ham_low, rest_out, far_out, out_out, near_out
):
    rest = (rest_low[...] + rotate_half(columns, top, low, groups, 1)).T
    rest_out[...] = rest
    halo = out_out.shape[0]
    edge_nodes, width = part.shape[0] - 4 * halo - rest.shape[0], rest.shape[0]
    nodes = edge_nodes + width
    cols = slice(edge_nodes, nodes)
    back = part[nodes:, :] + mul((ham_top[nodes:, cols], ham_low[nodes:, cols]), split(rest))
    far_out[...] = back[: 2 * halo]
    out_out[...] = back[2 * halo : 3 * halo]
    near_out[...] = back[3 * halo :]


def first_base(
    start_edge, start_rest, part, ham_top, ham_low, pick, overlap, back_far,
    start_out, base_out, packed_out, adjust_out,
):
    nodes = ham_top.shape[0] - pick.shape[0]
    edge_nodes = start_edge.shape[0]
    cols = slice(edge_nodes, nodes)
    start = jnp.concatenate([start_edge[...], start_rest[...]], 0)
    start_out[...] = start
    own = part[:nodes, :] + mul(
        (ham_top[:nodes, cols], ham_low[:nodes, cols]), split(start_rest[...])
    )
    base = SCALE_ONE * (own - CENTRE * start)
    base_out[...] = base
    packed_out[...] = sift(pick[...], base[:edge_nodes])
    adjust_out[...] = mul(split(overlap[...]), split(back_far[...]))


def fetch_far(packed, both, out_in, near_in, far_out):
    duo = 2 * out_in.shape[0]
    back = jnp.concatenate([out_in[...], near_in[...]], 0)
    far_out[...] = packed[:duo, :] + SCALE_ONE * sift(both[:duo, duo:], back)


def fetch_ring(packed, both, far_in, out_in, near_in, out_out, near_out):
    halo = out_in.shape[0]
    back = jnp.concatenate([far_in[...], out_in[...], near_in[...]], 0)
    rows = packed[2 * halo :, :] + SCALE_ONE * sift(both[2 * halo :, :], back)
    out_out[...] = rows[:halo]
    near_out[...] = rows[halo:]


def first_own(
    base, pick, far_in, out_in, near_in, ham_top, ham_low, couple, first_out, part_out, known_out
):
    edge_nodes = pick.shape[1]
    nodes = base.shape[0]
    duo = far_in.shape[0]
    back = jnp.concatenate([far_in[...], out_in[...], near_in[...]], 0)
    edge = base[:edge_nodes, :] + SCALE_ONE * sift(pick[...].T, back)
    first = jnp.concatenate([edge, base[edge_nodes:, :]], 0)
    first_out[...] = first
    part_out[...] = mul((ham_top[:, :nodes], ham_low[:, :nodes]), split(first))
    known_out[...] = mul(split(couple[...]), split(sift(pick[:duo, :], edge)))


def return_far(part, ham_top, ham_low, out_in, near_in, far_out):
    halo = out_in.shape[0]
    nodes = part.shape[0] - 4 * halo
    far = slice(nodes, nodes + 2 * halo)
    ring = slice(nodes + 2 * halo, nodes + 4 * halo)
    ghosts = split(jnp.concatenate([out_in[...], near_in[...]], 0))
    far_out[...] = part[far, :] + mul((ham_top[far, ring], ham_low[far, ring]), ghosts)


def return_ring(
    part, ham_top, ham_low, far_in, adjust, out_in, near_in, ghosts_out, out_out, near_out
):
    halo = out_in.shape[0]
    nodes = part.shape[0] - 4 * halo
    ring = slice(nodes + 2 * halo, nodes + 4 * halo)
    ghosts = jnp.concatenate([far_in[...] + adjust[...], out_in[...], near_in[...]], 0)
    ghosts_out[...] = ghosts
    rows = part[ring, :] + mul((ham_top[ring, nodes:], ham_low[ring, nodes:]), split(ghosts))
    out_out[...] = rows[:halo]
    near_out[...] = rows[halo:]


def second_base(part, ghosts, ham_top, ham_low, first, start, known, shuffle, hits, result_out):
    nodes = first.shape[0]
    duo = known.shape[0]
    ham = (ham_top[:nodes, nodes:], ham_low[:nodes, nodes:])
    second = part[:nodes, :] + mul(ham, split(ghosts[...])) - CENTRE * first[...]
    second = SCALE_TWO * second - SIGMA_ONE * SIGMA_TWO * start[...]
    top, low = split(second.T)
    result = dot(top, shuffle[...]) + dot(low, shuffle[...])
    top, low = split(SCALE_TWO * known[...].T)
    result_out[...] = result + (dot(top, hits[:duo, :]) + dot(low, hits[:duo, :]))


def finish(result, hits, far_in, out_in, near_in, out):
    back = jnp.concatenate([far_in[...], out_in[...], near_in[...]], 0)
    top, low = split(SCALE_TWO * back.T)
    out[...] = result[...] + (dot(top, hits[...]) + dot(low, hits[...]))


def per_device(subspace, ritz, element_ham, connect, send_rows):
    depth, nodes = subspace.shape
    block = ritz.shape[0]
    slots, halo = send_rows.shape[1:]
    partitions = lax.axis_size("mesh")
    groups = lax.axis_size("state")
    across = partitions // 2
    wide = slots * halo
    duo = 2 * halo
    full = nodes + wide

    odd = (lax.axis_index("mesh") % 2).astype(I32).reshape(1)
    group = lax.axis_index("state").astype(I32).reshape(1)
    pairs_far = [(i, (i + across) % partitions) for i in range(partitions)]
    pairs_in = [(i, i ^ 1) for i in range(partitions)]
    pairs_out = [
        (i, (i + 1) % partitions if i % 2 else (i - 1) % partitions) for i in range(partitions)
    ]

    def far(rows):
        return lax.ppermute(rows, "mesh", pairs_far)

    def out(rows):
        return lax.ppermute(rows, "mesh", pairs_out)

    def near(rows):
        return lax.ppermute(rows, "mesh", pairs_in)

    def gather(rows):
        parts = [
            lax.ppermute(rows, "state", [(i, (i + step) % groups) for i in range(groups)])
            for step in range(1, groups)
        ]
        return parts[0] if len(parts) == 1 else jnp.concatenate(parts, 0)

    def rows_of(count):
        return ((count, block), F32)

    halo_out = [rows_of(duo), rows_of(halo), rows_of(halo)]
    smem = pl.BlockSpec(memory_space=pltpu.SMEM)
    vmem = pl.BlockSpec(memory_space=pltpu.VMEM)
    hbm = pl.BlockSpec(memory_space=pltpu.HBM)

    far_cols, ring_cols, low_cols, high_cols, shuffle = call(
        renumber,
        [
            ((depth // 2, 2 * duo), F32),
            ((depth // 2, 2 * duo), F32),
            ((depth // 2, nodes - wide), F32),
            ((depth // 2, nodes - wide), F32),
            ((nodes, nodes), BF16),
        ],
        in_hbm(send_rows), in_hbm(subspace),
        in_specs=[hbm, hbm],
        scratch_shapes=[
            pltpu.VMEM(send_rows.shape, I32),
            pltpu.VMEM(subspace.shape, F32),
            pltpu.SemaphoreType.DMA((2,)),
        ],
    )
    far_cols_in = gather(far_cols)
    ring_cols_in = gather(ring_cols)
    low_cols_in = gather(low_cols)
    high_cols_in = gather(high_cols)
    elems, size = connect.shape
    pitch = -(-size // 128) * 128
    blocks = jnp.transpose(element_ham, (1, 0, 2)).reshape(size * elems, size)
    ham_top, ham_low, pick, both, hits, pair = call(
        assemble,
        [
            ((full, full), BF16),
            ((full, full), BF16),
            ((wide, wide), BF16),
            ((wide, wide), BF16),
            ((wide, nodes), BF16),
            ((duo, 2 * duo), F32),
        ],
        odd, send_rows, connect, in_hbm(blocks), shuffle,
        limit=12,
        in_specs=[smem, vmem, vmem, hbm, vmem],
        scratch_shapes=[
            pltpu.VMEM(blocks.shape, F32),
            pltpu.SemaphoreType.DMA,
            pltpu.VMEM((full, elems * pitch), BF16),
            pltpu.VMEM((elems * pitch, 2 * full), BF16),
        ],
    )
    others = groups - 1
    start_own, ritz_top, ritz_low = call(
        rotate_own,
        [
            ((block, nodes), F32),
            ((block, others * depth), BF16),
            ((block, others * depth), BF16),
        ],
        group, shuffle, in_hbm(subspace), in_hbm(ritz),
        limit=12,
        in_specs=[smem, vmem, hbm, hbm],
        scratch_shapes=[
            pltpu.VMEM(subspace.shape, F32),
            pltpu.VMEM((groups, block, depth), F32),
            pltpu.SemaphoreType.DMA((groups + 1, 1)),
        ],
    )

    start_far, far_rows = call(
        functools.partial(rotate_far, groups),
        [rows_of(duo), ((duo, block + 2 * duo), F32)],
        far_cols_in, start_own, ritz_top, ritz_low, pick, pair,
    )
    far_in = far(far_rows)
    start_edge, out_rows, near_rows = call(
        functools.partial(rotate_ring, groups),
        [rows_of(wide), rows_of(halo), rows_of(halo)],
        ring_cols_in, start_own, start_far, ritz_top, ritz_low, pick,
    )
    out_in, near_in = out(out_rows), near(near_rows)
    part, overlap, couple = call(
        first_part,
        [rows_of(full), ((duo, duo), F32), ((duo, duo), F32)],
        start_edge, far_in, out_in, near_in, ham_top, ham_low,
    )
    (rest_low,) = call(
        functools.partial(rotate_low, groups),
        [((block, nodes - wide), F32)],
        low_cols_in, start_own, ritz_top, ritz_low,
    )

    start_rest, back_far, back_out, back_near = call(
        functools.partial(rotate_rest, groups),
        [rows_of(nodes - wide)] + halo_out,
        high_cols_in, rest_low, ritz_top, ritz_low, part, ham_top, ham_low,
    )
    far_in, out_in, near_in = far(back_far), out(back_out), near(back_near)
    start, base, packed, adjust = call(
        first_base,
        [rows_of(nodes), rows_of(nodes), rows_of(wide), rows_of(duo)],
        start_edge, start_rest, part, ham_top, ham_low, pick, overlap, back_far,
    )
    (far_rows,) = call(fetch_far, [rows_of(duo)], packed, both, out_in, near_in)
    fetched_far = far(far_rows)
    out_rows, near_rows = call(
        fetch_ring, halo_out[1:], packed, both, far_in, out_in, near_in
    )
    fetched_out, fetched_near = out(out_rows), near(near_rows)
    first, part, known = call(
        first_own,
        [rows_of(nodes), rows_of(full), rows_of(duo)],
        base, pick, far_in, out_in, near_in, ham_top, ham_low, couple,
    )

    (far_rows,) = call(
        return_far, [rows_of(duo)], part, ham_top, ham_low, fetched_out, fetched_near
    )
    returned_far = far(far_rows)
    ghosts, out_rows, near_rows = call(
        return_ring,
        [rows_of(wide)] + halo_out[1:],
        part, ham_top, ham_low, fetched_far, adjust, fetched_out, fetched_near,
    )
    returned_out, returned_near = out(out_rows), near(near_rows)
    (result,) = call(
        second_base,
        [((block, nodes), F32)],
        part, ghosts, ham_top, ham_low, first, start, known, shuffle, hits,
    )
    (result,) = call(
        finish, [((block, nodes), F32)], result, hits, returned_far, returned_out, returned_near
    )
    return result


def solution(mesh):
    in_specs = (
        P("state", "mesh"),
        P("state", None),
        P("mesh", None, None),
        P("mesh", None),
        P("mesh", None, None),
    )
    out_specs = P("state", "mesh")
    return jax.shard_map(
        per_device, mesh=mesh, in_specs=in_specs, out_specs=out_specs, check_vma=False
    )
```

```python
import functools

import jax
import jax.numpy as jnp
from jax import lax
from jax.experimental import pallas as pl
from jax.experimental.pallas import tpu as pltpu
from jax.sharding import PartitionSpec as P

F32 = jnp.float32
BF16 = jnp.bfloat16
I32 = jnp.int32
NN = ((1,), (0,))
NT = ((1,), (1,))

HALF = 1.5
CENTRE = 2.5
SIGMA_ONE = HALF / (-1.0 - CENTRE)
SIGMA_TWO = 1.0 / (2.0 / SIGMA_ONE - SIGMA_ONE)
SCALE_ONE = SIGMA_ONE / HALF
SCALE_TWO = 2.0 * SIGMA_TWO / HALF


def dot(a, b, dims=NN):
    return lax.dot_general(a, b, (dims, ((), ())), preferred_element_type=F32)


def split(x):
    top = x.astype(BF16)
    return top, (x - top.astype(F32)).astype(BF16)


def mul(a, b, dims=NN):
    return dot(a[0], b[0], dims) + (dot(a[0], b[1], dims) + dot(a[1], b[0], dims))


def sift(a, x):
    top, low = split(x)
    return dot(a, top) + dot(a, low)


def call(body, outs, *args, limit=8, **rest):
    return pl.pallas_call(
        body,
        out_shape=[jax.ShapeDtypeStruct(*out) for out in outs],
        compiler_params=pltpu.CompilerParams(vmem_limit_bytes=limit << 20),
        **rest,
    )(*args)


def in_hbm(x):
    return pltpu.with_memory_space_constraint(x, pltpu.HBM)


def column(row, width):
    down = lax.broadcasted_iota(I32, (width, width), 0)
    along = lax.broadcasted_iota(I32, (width, width), 1)
    return jnp.sum(jnp.where(down == along, row, 0), axis=1, keepdims=True)


def renumber(
    lists_in, subspace_in, far_out, ring_out, low_out, high_out, shuffle_out, lists, subspace, sems
):
    slots, halo = lists.shape[1:]
    depth, nodes = subspace.shape
    duo = 2 * halo
    span = depth // 2
    index_copy = pltpu.make_async_copy(lists_in, lists, sems.at[0])
    index_copy.start()
    copy = pltpu.make_async_copy(subspace_in, subspace, sems.at[1])
    copy.start()
    index_copy.wait()
    ids = lax.broadcasted_iota(I32, (halo, nodes), 1)
    seen = []
    for slot in range(slots):
        sent = column(lists[0, slot : slot + 1, :], halo)
        seen.append(jnp.where(sent == ids, 1.0, 0.0))
    far = jnp.max(jnp.maximum(seen[2], seen[3]), axis=0, keepdims=True)
    ring = jnp.max(jnp.maximum(seen[0], seen[1]), axis=0, keepdims=True) * (1.0 - far)
    down = lax.broadcasted_iota(I32, (nodes, nodes), 0)
    along = lax.broadcasted_iota(I32, (nodes, nodes), 1)
    upto = jnp.where(down <= along, 1.0, 0.0).astype(BF16)
    flags = jnp.concatenate([far, ring, jnp.zeros((6, nodes), F32)], 0)
    counts = dot(flags.astype(BF16), upto).astype(I32)
    far_count, ring_count = counts[0:1], counts[1:2]
    totals = jnp.sum(flags, axis=1, keepdims=True).astype(I32)
    far_total, ring_total = totals[0:1], totals[1:2]
    place = jnp.where(
        far > 0.5,
        far_count - 1,
        jnp.where(
            ring > 0.5,
            far_total + ring_count - 1,
            far_total + ring_total + along[:1] - far_count - ring_count,
        ),
    )
    match = place == down
    shuffle = jnp.where(match, 1.0, 0.0).astype(BF16)
    shuffle_out[...] = shuffle
    copy.wait()
    halves = []
    for part, rest_out in enumerate((low_out, high_out)):
        top, low = split(subspace[part * span : (part + 1) * span, :])
        turned = dot(top, shuffle, NT) + dot(low, shuffle, NT)
        rest_out[...] = turned[:, 2 * duo :]
        halves.append(turned)
    far_out[...] = jnp.concatenate([half[:, :duo] for half in halves], 1)
    ring_out[...] = jnp.concatenate([half[:, duo : 2 * duo] for half in halves], 1)


def assemble(
    odd, lists, connect, blocks_in, shuffle, top_out, low_out, pick_out, both_out, hits_out, pair_out,
    blocks, sem, spread, rows_both,
):
    copy = pltpu.make_async_copy(blocks_in, blocks.at[pl.ds(0, blocks_in.shape[0])], sem)
    copy.start()
    elems, size = connect.shape
    slots, halo = lists.shape[1:]
    nodes = shuffle.shape[0]
    wide = slots * halo
    duo = 2 * halo
    swap = odd[0] == 1
    columns = [column(lists[0, slot : slot + 1, :], halo) for slot in range(slots)]
    outer = jnp.where(swap, columns[0], columns[1])
    inner = jnp.where(swap, columns[1], columns[0])
    sent = jnp.concatenate([columns[2], columns[3], outer, inner], 0)
    hits = jnp.where(sent == lax.broadcasted_iota(I32, (wide, nodes), 1), 1.0, 0.0).astype(BF16)
    hits_out[...] = hits
    pick = dot(hits, shuffle[:wide, :], NT).astype(BF16)
    pick_out[...] = pick
    both = dot(pick, pick, NT)
    both_out[...] = both.astype(BF16)

    lane = lax.broadcasted_iota(I32, (halo, 1), 0)
    flag = odd[0]
    ghost = jnp.concatenate(
        [3 * halo + lane, 2 * halo + lane, (1 - flag) * halo + lane, flag * halo + lane], 0
    )
    along = lax.broadcasted_iota(I32, (nodes, nodes), 1).astype(F32)
    origin = jnp.sum(along * shuffle[...].astype(F32), axis=1, keepdims=True).astype(I32)
    pitch = spread.shape[1] // elems
    full = nodes + wide
    numbers = jnp.broadcast_to(jnp.concatenate([origin, nodes + ghost], 0), (full, pitch))
    copy.wait()
    for elem in range(elems):
        cols = slice(elem * pitch, (elem + 1) * pitch)
        wanted = jnp.pad(connect[elem : elem + 1, :], ((0, 0), (0, pitch - size)), constant_values=-1)
        chosen = jnp.where(numbers == wanted, 1.0, 0.0).astype(BF16)
        spread[:, cols] = chosen
        block = blocks[pl.ds(elem, size, stride=elems), :]
        top, low = split(jnp.pad(block, ((0, pitch - size), (0, pitch - size))))
        rows = dot(jnp.concatenate([top, low], 0), chosen, NT)
        top, low = split(rows[:pitch] + rows[pitch:])
        rows_both[cols, :full] = top
        rows_both[cols, full:] = low
    ham = dot(spread[...], rows_both[...])
    ham = ham[:, :full] + ham[:, full:]
    top, low = split(ham)
    top_out[...] = top
    low_out[...] = low
    far = slice(nodes, nodes + duo)
    pair_out[...] = jnp.concatenate([both[:duo, :duo], ham[far, far]], 1)


def rotate_own(
    group, shuffle, subspace_in, ritz_in, start_out, top_out, low_out, subspace, ritz, sems
):
    block, depth = ritz.shape[1:]
    groups = ritz.shape[0]
    parts = sems.shape[1]
    span = depth // parts
    copies = []
    for step in range(groups):
        first = lax.rem(group[0] + groups - step, groups) * depth
        for part in range(parts):
            if step == 0:
                rows = pl.ds(part * span, span)
                copies.append(
                    pltpu.make_async_copy(
                        subspace_in.at[rows], subspace.at[rows], sems.at[groups, part]
                    )
                )
                copies[-1].start()
            cols = pl.ds(pl.multiple_of(first + part * span, span), span)
            copies.append(
                pltpu.make_async_copy(
                    ritz_in.at[:, cols],
                    ritz.at[step, :, pl.ds(part * span, span)],
                    sems.at[step, part],
                )
            )
            copies[-1].start()
    total = None
    for part in range(parts):
        here = slice(part * span, (part + 1) * span)
        copies[2 * part].wait()
        copies[2 * part + 1].wait()
        term = mul(split(ritz[0, :, here]), split(subspace[here, :]))
        total = term if total is None else total + term
    top, low = split(total)
    start_out[...] = dot(top, shuffle[...], NT) + dot(low, shuffle[...], NT)
    for step in range(1, groups):
        for part in range(parts):
            copies[parts + step * parts + part].wait()
            top, low = split(ritz[step, :, part * span : (part + 1) * span])
            cols = slice((step - 1) * depth + part * span, (step - 1) * depth + (part + 1) * span)
            top_out[:, cols] = top
            low_out[:, cols] = low


def rotate(top, low, columns):
    width = columns.shape[1]
    high, rest = split(columns)
    wide = dot(top, jnp.concatenate([high, rest], 1))
    return wide[:, :width] + (wide[:, width:] + dot(low, high))


def pieces(x, groups, part, axis):
    span = x.shape[axis] // (2 * (groups - 1))
    starts = [(2 * step + part) * span for step in range(groups - 1)]
    if axis == 0:
        return [x[start : start + span, :] for start in starts]
    return [x[:, start : start + span] for start in starts]


def rotate_sides(columns, top, low, groups):
    width = columns.shape[1] // 2
    span = columns.shape[0] // (groups - 1)
    whole = jnp.concatenate(
        [
            columns[step * span : (step + 1) * span, part * width : (part + 1) * width]
            for step in range(groups - 1)
            for part in range(2)
        ],
        0,
    )
    return rotate(top[...], low[...], whole)


def rotate_half(columns, top, low, groups, part):
    return rotate(
        jnp.concatenate(pieces(top, groups, part, 1), 1),
        jnp.concatenate(pieces(low, groups, part, 1), 1),
        columns[...],
    )


def rotate_far(groups, columns, start_own, top, low, pick, pair, start_out, far_out):
    duo, block = start_out.shape
    start = (start_own[:, :duo] + rotate_sides(columns, top, low, groups)).T
    start_out[...] = start
    far_out[:, :block] = sift(pick[:duo, :duo], start)
    far_out[:, block:] = pair[...]


def rotate_ring(groups, columns, start_own, start_far, top, low, pick, start_out, out_out, near_out):
    halo = out_out.shape[0]
    duo = 2 * halo
    start = (start_own[:, duo : 2 * duo] + rotate_sides(columns, top, low, groups)).T
    start = jnp.concatenate([start_far[...], start], 0)
    start_out[...] = start
    packed = sift(pick[duo:, :], start)
    out_out[...] = packed[:halo]
    near_out[...] = packed[halo:]


def rotate_low(groups, columns, start_own, top, low, rest_out):
    edge_nodes = start_own.shape[1] - columns.shape[1]
    rest_out[...] = start_own[:, edge_nodes:] + rotate_half(columns, top, low, groups, 0)


def first_part(start_edge, far_in, out_in, near_in, ham_top, ham_low, part_out, overlap_out, couple_out):
    edge_nodes = start_edge.shape[0]
    nodes = ham_top.shape[0] - 4 * out_in.shape[0]
    duo = far_in.shape[0]
    block = start_edge.shape[1]
    ghosts = jnp.concatenate([far_in[:, :block], out_in[...], near_in[...]], 0)
    part_out[...] = mul(
        (ham_top[:, :edge_nodes], ham_low[:, :edge_nodes]), split(start_edge[...])
    ) + mul((ham_top[:, nodes:], ham_low[:, nodes:]), split(ghosts))
    overlap_out[...] = SCALE_ONE * far_in[:, block : block + duo]
    couple_out[...] = far_in[:, block + duo :]


def rotate_rest(
    groups, columns, rest_low, top, low, part, ham_top, ham_low, rest_out, far_out, out_out, near_out
):
    rest = (rest_low[...] + rotate_half(columns, top, low, groups, 1)).T
    rest_out[...] = rest
    halo = out_out.shape[0]
    edge_nodes, width = part.shape[0] - 4 * halo - rest.shape[0], rest.shape[0]
    nodes = edge_nodes + width
    cols = slice(edge_nodes, nodes)
    back = part[nodes:, :] + mul((ham_top[nodes:, cols], ham_low[nodes:, cols]), split(rest))
    far_out[...] = back[: 2 * halo]
    out_out[...] = back[2 * halo : 3 * halo]
    near_out[...] = back[3 * halo :]


def first_base(
    start_edge, start_rest, part, ham_top, ham_low, pick, overlap, back_far,
    start_out, base_out, packed_out, adjust_out,
):
    nodes = ham_top.shape[0] - pick.shape[0]
    edge_nodes = start_edge.shape[0]
    cols = slice(edge_nodes, nodes)
    start = jnp.concatenate([start_edge[...], start_rest[...]], 0)
    start_out[...] = start
    own = part[:nodes, :] + mul(
        (ham_top[:nodes, cols], ham_low[:nodes, cols]), split(start_rest[...])
    )
    base = SCALE_ONE * (own - CENTRE * start)
    base_out[...] = base
    packed_out[...] = sift(pick[...], base[:edge_nodes])
    adjust_out[...] = mul(split(overlap[...]), split(back_far[...]))


def fetch_far(packed, both, out_in, near_in, far_out):
    duo = 2 * out_in.shape[0]
    back = jnp.concatenate([out_in[...], near_in[...]], 0)
    far_out[...] = packed[:duo, :] + SCALE_ONE * sift(both[:duo, duo:], back)


def fetch_ring(packed, both, far_in, out_in, near_in, out_out, near_out):
    halo = out_in.shape[0]
    back = jnp.concatenate([far_in[...], out_in[...], near_in[...]], 0)
    rows = packed[2 * halo :, :] + SCALE_ONE * sift(both[2 * halo :, :], back)
    out_out[...] = rows[:halo]
    near_out[...] = rows[halo:]


def first_own(
    base, pick, far_in, out_in, near_in, ham_top, ham_low, couple, first_out, part_out, known_out
):
    edge_nodes = pick.shape[1]
    nodes = base.shape[0]
    duo = far_in.shape[0]
    back = jnp.concatenate([far_in[...], out_in[...], near_in[...]], 0)
    edge = base[:edge_nodes, :] + SCALE_ONE * sift(pick[...].T, back)
    first = jnp.concatenate([edge, base[edge_nodes:, :]], 0)
    first_out[...] = first
    part_out[...] = mul((ham_top[:, :nodes], ham_low[:, :nodes]), split(first))
    known_out[...] = mul(split(couple[...]), split(sift(pick[:duo, :], edge)))


def return_far(part, ham_top, ham_low, out_in, near_in, far_out):
    halo = out_in.shape[0]
    nodes = part.shape[0] - 4 * halo
    far = slice(nodes, nodes + 2 * halo)
    ring = slice(nodes + 2 * halo, nodes + 4 * halo)
    ghosts = split(jnp.concatenate([out_in[...], near_in[...]], 0))
    far_out[...] = part[far, :] + mul((ham_top[far, ring], ham_low[far, ring]), ghosts)


def return_ring(
    part, ham_top, ham_low, far_in, adjust, out_in, near_in, ghosts_out, out_out, near_out
):
    halo = out_in.shape[0]
    nodes = part.shape[0] - 4 * halo
    ring = slice(nodes + 2 * halo, nodes + 4 * halo)
    ghosts = jnp.concatenate([far_in[...] + adjust[...], out_in[...], near_in[...]], 0)
    ghosts_out[...] = ghosts
    rows = part[ring, :] + mul((ham_top[ring, nodes:], ham_low[ring, nodes:]), split(ghosts))
    out_out[...] = rows[:halo]
    near_out[...] = rows[halo:]


def second_base(part, ghosts, ham_top, ham_low, first, start, known, shuffle, hits, result_out):
    nodes = first.shape[0]
    duo = known.shape[0]
    ham = (ham_top[:nodes, nodes:], ham_low[:nodes, nodes:])
    second = part[:nodes, :] + mul(ham, split(ghosts[...])) - CENTRE * first[...]
    second = SCALE_TWO * second - SIGMA_ONE * SIGMA_TWO * start[...]
    top, low = split(second.T)
    result = dot(top, shuffle[...]) + dot(low, shuffle[...])
    top, low = split(SCALE_TWO * known[...].T)
    result_out[...] = result + (dot(top, hits[:duo, :]) + dot(low, hits[:duo, :]))


def finish(result, hits, far_in, out_in, near_in, out):
    back = jnp.concatenate([far_in[...], out_in[...], near_in[...]], 0)
    top, low = split(SCALE_TWO * back.T)
    out[...] = result[...] + (dot(top, hits[...]) + dot(low, hits[...]))


def per_device(subspace, ritz, element_ham, connect, send_rows):
    depth, nodes = subspace.shape
    block = ritz.shape[0]
    slots, halo = send_rows.shape[1:]
    partitions = lax.axis_size("mesh")
    groups = lax.axis_size("state")
    across = partitions // 2
    wide = slots * halo
    duo = 2 * halo
    full = nodes + wide

    odd = (lax.axis_index("mesh") % 2).astype(I32).reshape(1)
    group = lax.axis_index("state").astype(I32).reshape(1)
    pairs_far = [(i, (i + across) % partitions) for i in range(partitions)]
    pairs_in = [(i, i ^ 1) for i in range(partitions)]
    pairs_out = [
        (i, (i + 1) % partitions if i % 2 else (i - 1) % partitions) for i in range(partitions)
    ]

    def far(rows):
        return lax.ppermute(rows, "mesh", pairs_far)

    def out(rows):
        return lax.ppermute(rows, "mesh", pairs_out)

    def near(rows):
        return lax.ppermute(rows, "mesh", pairs_in)

    def gather(rows):
        parts = [
            lax.ppermute(rows, "state", [(i, (i + step) % groups) for i in range(groups)])
            for step in range(1, groups)
        ]
        return parts[0] if len(parts) == 1 else jnp.concatenate(parts, 0)

    def rows_of(count):
        return ((count, block), F32)

    halo_out = [rows_of(duo), rows_of(halo), rows_of(halo)]
    smem = pl.BlockSpec(memory_space=pltpu.SMEM)
    vmem = pl.BlockSpec(memory_space=pltpu.VMEM)
    hbm = pl.BlockSpec(memory_space=pltpu.HBM)

    far_cols, ring_cols, low_cols, high_cols, shuffle = call(
        renumber,
        [
            ((depth // 2, 2 * duo), F32),
            ((depth // 2, 2 * duo), F32),
            ((depth // 2, nodes - wide), F32),
            ((depth // 2, nodes - wide), F32),
            ((nodes, nodes), BF16),
        ],
        in_hbm(send_rows), in_hbm(subspace),
        in_specs=[hbm, hbm],
        scratch_shapes=[
            pltpu.VMEM(send_rows.shape, I32),
            pltpu.VMEM(subspace.shape, F32),
            pltpu.SemaphoreType.DMA((2,)),
        ],
    )
    far_cols_in = gather(far_cols)
    ring_cols_in = gather(ring_cols)
    low_cols_in = gather(low_cols)
    high_cols_in = gather(high_cols)
    elems, size = connect.shape
    pitch = -(-size // 128) * 128
    blocks = jnp.transpose(element_ham, (1, 0, 2)).reshape(size * elems, size)
    ham_top, ham_low, pick, both, hits, pair = call(
        assemble,
        [
            ((full, full), BF16),
            ((full, full), BF16),
            ((wide, wide), BF16),
            ((wide, wide), BF16),
            ((wide, nodes), BF16),
            ((duo, 2 * duo), F32),
        ],
        odd, send_rows, connect, in_hbm(blocks), shuffle,
        limit=12,
        in_specs=[smem, vmem, vmem, hbm, vmem],
        scratch_shapes=[
            pltpu.VMEM((pitch * elems, size), F32),
            pltpu.SemaphoreType.DMA,
            pltpu.VMEM((full, elems * pitch), BF16),
            pltpu.VMEM((elems * pitch, 2 * full), BF16),
        ],
    )
    others = groups - 1
    start_own, ritz_top, ritz_low = call(
        rotate_own,
        [
            ((block, nodes), F32),
            ((block, others * depth), BF16),
            ((block, others * depth), BF16),
        ],
        group, shuffle, in_hbm(subspace), in_hbm(ritz),
        limit=12,
        in_specs=[smem, vmem, hbm, hbm],
        scratch_shapes=[
            pltpu.VMEM(subspace.shape, F32),
            pltpu.VMEM((groups, block, depth), F32),
            pltpu.SemaphoreType.DMA((groups + 1, 1)),
        ],
    )

    start_far, far_rows = call(
        functools.partial(rotate_far, groups),
        [rows_of(duo), ((duo, block + 2 * duo), F32)],
        far_cols_in, start_own, ritz_top, ritz_low, pick, pair,
    )
    far_in = far(far_rows)
    start_edge, out_rows, near_rows = call(
        functools.partial(rotate_ring, groups),
        [rows_of(wide), rows_of(halo), rows_of(halo)],
        ring_cols_in, start_own, start_far, ritz_top, ritz_low, pick,
    )
    out_in, near_in = out(out_rows), near(near_rows)
    part, overlap, couple = call(
        first_part,
        [rows_of(full), ((duo, duo), F32), ((duo, duo), F32)],
        start_edge, far_in, out_in, near_in, ham_top, ham_low,
    )
    (rest_low,) = call(
        functools.partial(rotate_low, groups),
        [((block, nodes - wide), F32)],
        low_cols_in, start_own, ritz_top, ritz_low,
    )

    start_rest, back_far, back_out, back_near = call(
        functools.partial(rotate_rest, groups),
        [rows_of(nodes - wide)] + halo_out,
        high_cols_in, rest_low, ritz_top, ritz_low, part, ham_top, ham_low,
    )
    far_in, out_in, near_in = far(back_far), out(back_out), near(back_near)
    start, base, packed, adjust = call(
        first_base,
        [rows_of(nodes), rows_of(nodes), rows_of(wide), rows_of(duo)],
        start_edge, start_rest, part, ham_top, ham_low, pick, overlap, back_far,
    )
    (far_rows,) = call(fetch_far, [rows_of(duo)], packed, both, out_in, near_in)
    fetched_far = far(far_rows)
    out_rows, near_rows = call(
        fetch_ring, halo_out[1:], packed, both, far_in, out_in, near_in
    )
    fetched_out, fetched_near = out(out_rows), near(near_rows)
    first, part, known = call(
        first_own,
        [rows_of(nodes), rows_of(full), rows_of(duo)],
        base, pick, far_in, out_in, near_in, ham_top, ham_low, couple,
    )

    (far_rows,) = call(
        return_far, [rows_of(duo)], part, ham_top, ham_low, fetched_out, fetched_near
    )
    returned_far = far(far_rows)
    ghosts, out_rows, near_rows = call(
        return_ring,
        [rows_of(wide)] + halo_out[1:],
        part, ham_top, ham_low, fetched_far, adjust, fetched_out, fetched_near,
    )
    returned_out, returned_near = out(out_rows), near(near_rows)
    (result,) = call(
        second_base,
        [((block, nodes), F32)],
        part, ghosts, ham_top, ham_low, first, start, known, shuffle, hits,
    )
    (result,) = call(
        finish, [((block, nodes), F32)], result, hits, returned_far, returned_out, returned_near
    )
    return result


def solution(mesh):
    in_specs = (
        P("state", "mesh"),
        P("state", None),
        P("mesh", None, None),
        P("mesh", None),
        P("mesh", None, None),
    )
    out_specs = P("state", "mesh")
    return jax.shard_map(
        per_device, mesh=mesh, in_specs=in_specs, out_specs=out_specs, check_vma=False
    )
```

```python
import functools

import jax
import jax.numpy as jnp
from jax import lax
from jax.experimental import pallas as pl
from jax.experimental.pallas import tpu as pltpu
from jax.sharding import PartitionSpec as P

F32 = jnp.float32
BF16 = jnp.bfloat16
I32 = jnp.int32
NN = ((1,), (0,))
NT = ((1,), (1,))

HALF = 1.5
CENTRE = 2.5
SIGMA_ONE = HALF / (-1.0 - CENTRE)
SIGMA_TWO = 1.0 / (2.0 / SIGMA_ONE - SIGMA_ONE)
SCALE_ONE = SIGMA_ONE / HALF
SCALE_TWO = 2.0 * SIGMA_TWO / HALF


def dot(a, b, dims=NN):
    return lax.dot_general(a, b, (dims, ((), ())), preferred_element_type=F32)


def split(x):
    top = x.astype(BF16)
    return top, (x - top.astype(F32)).astype(BF16)


def mul(a, b, dims=NN):
    return dot(a[0], b[0], dims) + (dot(a[0], b[1], dims) + dot(a[1], b[0], dims))


def sift(a, x):
    return dot(jnp.concatenate([a, a], 1), jnp.concatenate(split(x), 0))


def call(body, outs, *args, limit=8, **rest):
    return pl.pallas_call(
        body,
        out_shape=[jax.ShapeDtypeStruct(*out) for out in outs],
        compiler_params=pltpu.CompilerParams(vmem_limit_bytes=limit << 20),
        **rest,
    )(*args)


def in_hbm(x):
    return pltpu.with_memory_space_constraint(x, pltpu.HBM)


def column(row, width):
    down = lax.broadcasted_iota(I32, (width, width), 0)
    along = lax.broadcasted_iota(I32, (width, width), 1)
    return jnp.sum(jnp.where(down == along, row, 0), axis=1, keepdims=True)


def renumber(
    lists_in, subspace_in, far_out, ring_out, low_out, high_out, shuffle_out, lists, subspace, sems
):
    slots, halo = lists.shape[1:]
    depth, nodes = subspace.shape
    duo = 2 * halo
    span = depth // 2
    index_copy = pltpu.make_async_copy(lists_in, lists, sems.at[0])
    index_copy.start()
    copy = pltpu.make_async_copy(subspace_in, subspace, sems.at[1])
    copy.start()
    index_copy.wait()
    ids = lax.broadcasted_iota(I32, (halo, nodes), 1)
    seen = []
    for slot in range(slots):
        sent = column(lists[0, slot : slot + 1, :], halo)
        seen.append(jnp.where(sent == ids, 1.0, 0.0))
    far = jnp.max(jnp.maximum(seen[2], seen[3]), axis=0, keepdims=True)
    ring = jnp.max(jnp.maximum(seen[0], seen[1]), axis=0, keepdims=True) * (1.0 - far)
    down = lax.broadcasted_iota(I32, (nodes, nodes), 0)
    along = lax.broadcasted_iota(I32, (nodes, nodes), 1)
    upto = jnp.where(down <= along, 1.0, 0.0).astype(BF16)
    flags = jnp.concatenate([far, ring, jnp.zeros((6, nodes), F32)], 0)
    counts = dot(flags.astype(BF16), upto).astype(I32)
    far_count, ring_count = counts[0:1], counts[1:2]
    totals = jnp.sum(flags, axis=1, keepdims=True).astype(I32)
    far_total, ring_total = totals[0:1], totals[1:2]
    place = jnp.where(
        far > 0.5,
        far_count - 1,
        jnp.where(
            ring > 0.5,
            far_total + ring_count - 1,
            far_total + ring_total + along[:1] - far_count - ring_count,
        ),
    )
    match = place == down
    shuffle = jnp.where(match, 1.0, 0.0).astype(BF16)
    shuffle_out[...] = shuffle
    twice = jnp.concatenate([shuffle, shuffle], 1)
    copy.wait()
    halves = []
    for part, rest_out in enumerate((low_out, high_out)):
        both_parts = jnp.concatenate(split(subspace[part * span : (part + 1) * span, :]), 1)
        turned = dot(both_parts, twice, NT)
        rest_out[...] = turned[:, 2 * duo :]
        halves.append(turned)
    far_out[...] = jnp.concatenate([half[:, :duo] for half in halves], 1)
    ring_out[...] = jnp.concatenate([half[:, duo : 2 * duo] for half in halves], 1)


def assemble(
    odd, lists, connect, blocks_in, shuffle, top_out, low_out, pick_out, both_out, hits_out, pair_out,
    blocks, sem, spread, rows_both,
):
    copy = pltpu.make_async_copy(blocks_in, blocks.at[pl.ds(0, blocks_in.shape[0])], sem)
    copy.start()
    elems, size = connect.shape
    slots, halo = lists.shape[1:]
    nodes = shuffle.shape[0]
    wide = slots * halo
    duo = 2 * halo
    swap = odd[0] == 1
    columns = [column(lists[0, slot : slot + 1, :], halo) for slot in range(slots)]
    outer = jnp.where(swap, columns[0], columns[1])
    inner = jnp.where(swap, columns[1], columns[0])
    sent = jnp.concatenate([columns[2], columns[3], outer, inner], 0)
    hits = jnp.where(sent == lax.broadcasted_iota(I32, (wide, nodes), 1), 1.0, 0.0).astype(BF16)
    hits_out[...] = hits
    pick = dot(hits, shuffle[:wide, :], NT).astype(BF16)
    pick_out[...] = pick
    both = dot(pick, pick, NT)
    both_out[...] = both.astype(BF16)

    lane = lax.broadcasted_iota(I32, (halo, 1), 0)
    flag = odd[0]
    ghost = jnp.concatenate(
        [3 * halo + lane, 2 * halo + lane, (1 - flag) * halo + lane, flag * halo + lane], 0
    )
    along = lax.broadcasted_iota(I32, (nodes, nodes), 1).astype(F32)
    origin = jnp.sum(along * shuffle[...].astype(F32), axis=1, keepdims=True).astype(I32)
    pitch = spread.shape[1] // elems
    full = nodes + wide
    numbers = jnp.broadcast_to(jnp.concatenate([origin, nodes + ghost], 0), (full, pitch))
    copy.wait()
    for elem in range(elems):
        cols = slice(elem * pitch, (elem + 1) * pitch)
        wanted = jnp.pad(connect[elem : elem + 1, :], ((0, 0), (0, pitch - size)), constant_values=-1)
        chosen = jnp.where(numbers == wanted, 1.0, 0.0).astype(BF16)
        spread[:, cols] = chosen
        block = blocks[pl.ds(elem, size, stride=elems), :]
        top, low = split(jnp.pad(block, ((0, pitch - size), (0, pitch - size))))
        rows = dot(jnp.concatenate([top, low], 0), chosen, NT)
        top, low = split(rows[:pitch] + rows[pitch:])
        rows_both[cols, :full] = top
        rows_both[cols, full:] = low
    ham = dot(spread[...], rows_both[...])
    ham = ham[:, :full] + ham[:, full:]
    top, low = split(ham)
    top_out[...] = top
    low_out[...] = low
    far = slice(nodes, nodes + duo)
    pair_out[...] = jnp.concatenate([both[:duo, :duo], ham[far, far]], 1)


def rotate_own(
    group, shuffle, subspace_in, ritz_in, start_out, top_out, low_out, subspace, ritz, sems
):
    block, depth = ritz.shape[1:]
    groups = ritz.shape[0]
    parts = sems.shape[1]
    span = depth // parts
    copies = []
    for step in range(groups):
        first = lax.rem(group[0] + groups - step, groups) * depth
        for part in range(parts):
            if step == 0:
                rows = pl.ds(part * span, span)
                copies.append(
                    pltpu.make_async_copy(
                        subspace_in.at[rows], subspace.at[rows], sems.at[groups, part]
                    )
                )
                copies[-1].start()
            cols = pl.ds(pl.multiple_of(first + part * span, span), span)
            copies.append(
                pltpu.make_async_copy(
                    ritz_in.at[:, cols],
                    ritz.at[step, :, pl.ds(part * span, span)],
                    sems.at[step, part],
                )
            )
            copies[-1].start()
    total = None
    for part in range(parts):
        here = slice(part * span, (part + 1) * span)
        copies[2 * part].wait()
        copies[2 * part + 1].wait()
        term = mul(split(ritz[0, :, here]), split(subspace[here, :]))
        total = term if total is None else total + term
    top, low = split(total)
    start_out[...] = dot(top, shuffle[...], NT) + dot(low, shuffle[...], NT)
    for step in range(1, groups):
        for part in range(parts):
            copies[parts + step * parts + part].wait()
            top, low = split(ritz[step, :, part * span : (part + 1) * span])
            cols = slice((step - 1) * depth + part * span, (step - 1) * depth + (part + 1) * span)
            top_out[:, cols] = top
            low_out[:, cols] = low


def rotate(top, low, columns):
    width = columns.shape[1]
    high, rest = split(columns)
    wide = dot(top, jnp.concatenate([high, rest], 1))
    return wide[:, :width] + (wide[:, width:] + dot(low, high))


def pieces(x, groups, part, axis):
    span = x.shape[axis] // (2 * (groups - 1))
    starts = [(2 * step + part) * span for step in range(groups - 1)]
    if axis == 0:
        return [x[start : start + span, :] for start in starts]
    return [x[:, start : start + span] for start in starts]


def rotate_sides(columns, top, low, groups):
    width = columns.shape[1] // 2
    span = columns.shape[0] // (groups - 1)
    whole = jnp.concatenate(
        [
            columns[step * span : (step + 1) * span, part * width : (part + 1) * width]
            for step in range(groups - 1)
            for part in range(2)
        ],
        0,
    )
    return rotate(top[...], low[...], whole)


def rotate_half(columns, top, low, groups, part):
    return rotate(
        jnp.concatenate(pieces(top, groups, part, 1), 1),
        jnp.concatenate(pieces(low, groups, part, 1), 1),
        columns[...],
    )


def rotate_far(groups, columns, start_own, top, low, pick, pair, start_out, far_out):
    duo, block = start_out.shape
    start = (start_own[:, :duo] + rotate_sides(columns, top, low, groups)).T
    start_out[...] = start
    far_out[:, :block] = sift(pick[:duo, :duo], start)
    far_out[:, block:] = pair[...]


def rotate_ring(groups, columns, start_own, start_far, top, low, pick, start_out, out_out, near_out):
    halo = out_out.shape[0]
    duo = 2 * halo
    start = (start_own[:, duo : 2 * duo] + rotate_sides(columns, top, low, groups)).T
    start = jnp.concatenate([start_far[...], start], 0)
    start_out[...] = start
    packed = sift(pick[duo:, :], start)
    out_out[...] = packed[:halo]
    near_out[...] = packed[halo:]


def rotate_low(groups, columns, start_own, top, low, rest_out):
    edge_nodes = start_own.shape[1] - columns.shape[1]
    rest_out[...] = start_own[:, edge_nodes:] + rotate_half(columns, top, low, groups, 0)


def first_part(start_edge, far_in, out_in, near_in, ham_top, ham_low, part_out, overlap_out, couple_out):
    edge_nodes = start_edge.shape[0]
    nodes = ham_top.shape[0] - 4 * out_in.shape[0]
    duo = far_in.shape[0]
    block = start_edge.shape[1]
    ghosts = jnp.concatenate([far_in[:, :block], out_in[...], near_in[...]], 0)
    part_out[...] = mul(
        (ham_top[:, :edge_nodes], ham_low[:, :edge_nodes]), split(start_edge[...])
    ) + mul((ham_top[:, nodes:], ham_low[:, nodes:]), split(ghosts))
    overlap_out[...] = SCALE_ONE * far_in[:, block : block + duo]
    couple_out[...] = far_in[:, block + duo :]


def rotate_rest(
    groups, columns, rest_low, top, low, part, ham_top, ham_low, rest_out, far_out, out_out, near_out
):
    rest = (rest_low[...] + rotate_half(columns, top, low, groups, 1)).T
    rest_out[...] = rest
    halo = out_out.shape[0]
    edge_nodes, width = part.shape[0] - 4 * halo - rest.shape[0], rest.shape[0]
    nodes = edge_nodes + width
    cols = slice(edge_nodes, nodes)
    back = part[nodes:, :] + mul((ham_top[nodes:, cols], ham_low[nodes:, cols]), split(rest))
    far_out[...] = back[: 2 * halo]
    out_out[...] = back[2 * halo : 3 * halo]
    near_out[...] = back[3 * halo :]


def first_base(
    start_edge, start_rest, part, ham_top, ham_low, pick, overlap, back_far,
    start_out, base_out, packed_out, adjust_out,
):
    nodes = ham_top.shape[0] - pick.shape[0]
    edge_nodes = start_edge.shape[0]
    cols = slice(edge_nodes, nodes)
    start = jnp.concatenate([start_edge[...], start_rest[...]], 0)
    start_out[...] = start
    own = part[:nodes, :] + mul(
        (ham_top[:nodes, cols], ham_low[:nodes, cols]), split(start_rest[...])
    )
    base = SCALE_ONE * (own - CENTRE * start)
    base_out[...] = base
    packed_out[...] = sift(pick[...], base[:edge_nodes])
    adjust_out[...] = mul(split(overlap[...]), split(back_far[...]))


def fetch_far(packed, both, out_in, near_in, far_out):
    duo = 2 * out_in.shape[0]
    back = jnp.concatenate([out_in[...], near_in[...]], 0)
    far_out[...] = packed[:duo, :] + SCALE_ONE * sift(both[:duo, duo:], back)


def fetch_ring(packed, both, far_in, out_in, near_in, out_out, near_out):
    halo = out_in.shape[0]
    back = jnp.concatenate([far_in[...], out_in[...], near_in[...]], 0)
    rows = packed[2 * halo :, :] + SCALE_ONE * sift(both[2 * halo :, :], back)
    out_out[...] = rows[:halo]
    near_out[...] = rows[halo:]


def first_own(
    base, pick, far_in, out_in, near_in, ham_top, ham_low, couple, first_out, part_out, known_out
):
    edge_nodes = pick.shape[1]
    nodes = base.shape[0]
    duo = far_in.shape[0]
    back = jnp.concatenate([far_in[...], out_in[...], near_in[...]], 0)
    edge = base[:edge_nodes, :] + SCALE_ONE * sift(pick[...].T, back)
    first = jnp.concatenate([edge, base[edge_nodes:, :]], 0)
    first_out[...] = first
    part_out[...] = mul((ham_top[:, :nodes], ham_low[:, :nodes]), split(first))
    known_out[...] = mul(split(couple[...]), split(sift(pick[:duo, :], edge)))


def return_far(part, ham_top, ham_low, out_in, near_in, far_out):
    halo = out_in.shape[0]
    nodes = part.shape[0] - 4 * halo
    far = slice(nodes, nodes + 2 * halo)
    ring = slice(nodes + 2 * halo, nodes + 4 * halo)
    ghosts = split(jnp.concatenate([out_in[...], near_in[...]], 0))
    far_out[...] = part[far, :] + mul((ham_top[far, ring], ham_low[far, ring]), ghosts)


def return_ring(
    part, ham_top, ham_low, far_in, adjust, out_in, near_in, ghosts_out, out_out, near_out
):
    halo = out_in.shape[0]
    nodes = part.shape[0] - 4 * halo
    ring = slice(nodes + 2 * halo, nodes + 4 * halo)
    ghosts = jnp.concatenate([far_in[...] + adjust[...], out_in[...], near_in[...]], 0)
    ghosts_out[...] = ghosts
    rows = part[ring, :] + mul((ham_top[ring, nodes:], ham_low[ring, nodes:]), split(ghosts))
    out_out[...] = rows[:halo]
    near_out[...] = rows[halo:]


def second_base(part, ghosts, ham_top, ham_low, first, start, known, shuffle, hits, result_out):
    nodes = first.shape[0]
    duo = known.shape[0]
    ham = (ham_top[:nodes, nodes:], ham_low[:nodes, nodes:])
    second = part[:nodes, :] + mul(ham, split(ghosts[...])) - CENTRE * first[...]
    second = SCALE_TWO * second - SIGMA_ONE * SIGMA_TWO * start[...]
    top, low = split(second.T)
    result = dot(top, shuffle[...]) + dot(low, shuffle[...])
    top, low = split(SCALE_TWO * known[...].T)
    result_out[...] = result + (dot(top, hits[:duo, :]) + dot(low, hits[:duo, :]))


def finish(result, hits, far_in, out_in, near_in, out):
    back = jnp.concatenate([far_in[...], out_in[...], near_in[...]], 0)
    columns = jnp.concatenate(split(SCALE_TWO * back.T), 1)
    out[...] = result[...] + dot(columns, jnp.concatenate([hits[...], hits[...]], 0))


def per_device(subspace, ritz, element_ham, connect, send_rows):
    depth, nodes = subspace.shape
    block = ritz.shape[0]
    slots, halo = send_rows.shape[1:]
    partitions = lax.axis_size("mesh")
    groups = lax.axis_size("state")
    across = partitions // 2
    wide = slots * halo
    duo = 2 * halo
    full = nodes + wide

    odd = (lax.axis_index("mesh") % 2).astype(I32).reshape(1)
    group = lax.axis_index("state").astype(I32).reshape(1)
    pairs_far = [(i, (i + across) % partitions) for i in range(partitions)]
    pairs_in = [(i, i ^ 1) for i in range(partitions)]
    pairs_out = [
        (i, (i + 1) % partitions if i % 2 else (i - 1) % partitions) for i in range(partitions)
    ]

    def far(rows):
        return lax.ppermute(rows, "mesh", pairs_far)

    def out(rows):
        return lax.ppermute(rows, "mesh", pairs_out)

    def near(rows):
        return lax.ppermute(rows, "mesh", pairs_in)

    def gather(rows):
        parts = [
            lax.ppermute(rows, "state", [(i, (i + step) % groups) for i in range(groups)])
            for step in range(1, groups)
        ]
        return parts[0] if len(parts) == 1 else jnp.concatenate(parts, 0)

    def rows_of(count):
        return ((count, block), F32)

    halo_out = [rows_of(duo), rows_of(halo), rows_of(halo)]
    smem = pl.BlockSpec(memory_space=pltpu.SMEM)
    vmem = pl.BlockSpec(memory_space=pltpu.VMEM)
    hbm = pl.BlockSpec(memory_space=pltpu.HBM)

    far_cols, ring_cols, low_cols, high_cols, shuffle = call(
        renumber,
        [
            ((depth // 2, 2 * duo), F32),
            ((depth // 2, 2 * duo), F32),
            ((depth // 2, nodes - wide), F32),
            ((depth // 2, nodes - wide), F32),
            ((nodes, nodes), BF16),
        ],
        in_hbm(send_rows), in_hbm(subspace),
        in_specs=[hbm, hbm],
        scratch_shapes=[
            pltpu.VMEM(send_rows.shape, I32),
            pltpu.VMEM(subspace.shape, F32),
            pltpu.SemaphoreType.DMA((2,)),
        ],
    )
    far_cols_in = gather(far_cols)
    ring_cols_in = gather(ring_cols)
    low_cols_in = gather(low_cols)
    high_cols_in = gather(high_cols)
    elems, size = connect.shape
    pitch = -(-size // 128) * 128
    blocks = jnp.transpose(element_ham, (1, 0, 2)).reshape(size * elems, size)
    ham_top, ham_low, pick, both, hits, pair = call(
        assemble,
        [
            ((full, full), BF16),
            ((full, full), BF16),
            ((wide, wide), BF16),
            ((wide, wide), BF16),
            ((wide, nodes), BF16),
            ((duo, 2 * duo), F32),
        ],
        odd, send_rows, connect, in_hbm(blocks), shuffle,
        limit=12,
        in_specs=[smem, vmem, vmem, hbm, vmem],
        scratch_shapes=[
            pltpu.VMEM((pitch * elems, size), F32),
            pltpu.SemaphoreType.DMA,
            pltpu.VMEM((full, elems * pitch), BF16),
            pltpu.VMEM((elems * pitch, 2 * full), BF16),
        ],
    )
    others = groups - 1
    start_own, ritz_top, ritz_low = call(
        rotate_own,
        [
            ((block, nodes), F32),
            ((block, others * depth), BF16),
            ((block, others * depth), BF16),
        ],
        group, shuffle, in_hbm(subspace), in_hbm(ritz),
        limit=12,
        in_specs=[smem, vmem, hbm, hbm],
        scratch_shapes=[
            pltpu.VMEM(subspace.shape, F32),
            pltpu.VMEM((groups, block, depth), F32),
            pltpu.SemaphoreType.DMA((groups + 1, 1)),
        ],
    )

    start_far, far_rows = call(
        functools.partial(rotate_far, groups),
        [rows_of(duo), ((duo, block + 2 * duo), F32)],
        far_cols_in, start_own, ritz_top, ritz_low, pick, pair,
    )
    far_in = far(far_rows)
    start_edge, out_rows, near_rows = call(
        functools.partial(rotate_ring, groups),
        [rows_of(wide), rows_of(halo), rows_of(halo)],
        ring_cols_in, start_own, start_far, ritz_top, ritz_low, pick,
    )
    out_in, near_in = out(out_rows), near(near_rows)
    part, overlap, couple = call(
        first_part,
        [rows_of(full), ((duo, duo), F32), ((duo, duo), F32)],
        start_edge, far_in, out_in, near_in, ham_top, ham_low,
    )
    (rest_low,) = call(
        functools.partial(rotate_low, groups),
        [((block, nodes - wide), F32)],
        low_cols_in, start_own, ritz_top, ritz_low,
    )

    start_rest, back_far, back_out, back_near = call(
        functools.partial(rotate_rest, groups),
        [rows_of(nodes - wide)] + halo_out,
        high_cols_in, rest_low, ritz_top, ritz_low, part, ham_top, ham_low,
    )
    far_in, out_in, near_in = far(back_far), out(back_out), near(back_near)
    start, base, packed, adjust = call(
        first_base,
        [rows_of(nodes), rows_of(nodes), rows_of(wide), rows_of(duo)],
        start_edge, start_rest, part, ham_top, ham_low, pick, overlap, back_far,
    )
    (far_rows,) = call(fetch_far, [rows_of(duo)], packed, both, out_in, near_in)
    fetched_far = far(far_rows)
    out_rows, near_rows = call(
        fetch_ring, halo_out[1:], packed, both, far_in, out_in, near_in
    )
    fetched_out, fetched_near = out(out_rows), near(near_rows)
    first, part, known = call(
        first_own,
        [rows_of(nodes), rows_of(full), rows_of(duo)],
        base, pick, far_in, out_in, near_in, ham_top, ham_low, couple,
    )

    (far_rows,) = call(
        return_far, [rows_of(duo)], part, ham_top, ham_low, fetched_out, fetched_near
    )
    returned_far = far(far_rows)
    ghosts, out_rows, near_rows = call(
        return_ring,
        [rows_of(wide)] + halo_out[1:],
        part, ham_top, ham_low, fetched_far, adjust, fetched_out, fetched_near,
    )
    returned_out, returned_near = out(out_rows), near(near_rows)
    (result,) = call(
        second_base,
        [((block, nodes), F32)],
        part, ghosts, ham_top, ham_low, first, start, known, shuffle, hits,
    )
    (result,) = call(
        finish, [((block, nodes), F32)], result, hits, returned_far, returned_out, returned_near
    )
    return result


def solution(mesh):
    in_specs = (
        P("state", "mesh"),
        P("state", None),
        P("mesh", None, None),
        P("mesh", None),
        P("mesh", None, None),
    )
    out_specs = P("state", "mesh")
    return jax.shard_map(
        per_device, mesh=mesh, in_specs=in_specs, out_specs=out_specs, check_vma=False
    )
```

```python
import functools

import jax
import jax.numpy as jnp
from jax import lax
from jax.experimental import pallas as pl
from jax.experimental.pallas import tpu as pltpu
from jax.sharding import PartitionSpec as P

F32 = jnp.float32
BF16 = jnp.bfloat16
I32 = jnp.int32
NN = ((1,), (0,))
NT = ((1,), (1,))

HALF = 1.5
CENTRE = 2.5
SIGMA_ONE = HALF / (-1.0 - CENTRE)
SIGMA_TWO = 1.0 / (2.0 / SIGMA_ONE - SIGMA_ONE)
SCALE_ONE = SIGMA_ONE / HALF
SCALE_TWO = 2.0 * SIGMA_TWO / HALF


def dot(a, b, dims=NN):
    return lax.dot_general(a, b, (dims, ((), ())), preferred_element_type=F32)


def split(x):
    top = x.astype(BF16)
    return top, (x - top.astype(F32)).astype(BF16)


def mul(a, b, dims=NN):
    return dot(a[0], b[0], dims) + (dot(a[0], b[1], dims) + dot(a[1], b[0], dims))


def sift(a, x):
    return dot(jnp.concatenate([a, a], 1), jnp.concatenate(split(x), 0))


def call(body, outs, *args, limit=8, **rest):
    return pl.pallas_call(
        body,
        out_shape=[jax.ShapeDtypeStruct(*out) for out in outs],
        compiler_params=pltpu.CompilerParams(vmem_limit_bytes=limit << 20),
        **rest,
    )(*args)


def in_hbm(x):
    return pltpu.with_memory_space_constraint(x, pltpu.HBM)


def column(row, width):
    down = lax.broadcasted_iota(I32, (width, width), 0)
    along = lax.broadcasted_iota(I32, (width, width), 1)
    return jnp.sum(jnp.where(down == along, row, 0), axis=1, keepdims=True)


def renumber(
    lists_in, subspace_in, far_out, ring_out, low_out, high_out, shuffle_out, lists, subspace, sems
):
    slots, halo = lists.shape[1:]
    depth, nodes = subspace.shape
    duo = 2 * halo
    span = depth // 2
    index_copy = pltpu.make_async_copy(lists_in, lists, sems.at[0])
    index_copy.start()
    copy = pltpu.make_async_copy(subspace_in, subspace, sems.at[1])
    copy.start()
    index_copy.wait()
    ids = lax.broadcasted_iota(I32, (halo, nodes), 1)
    seen = []
    for slot in range(slots):
        sent = column(lists[0, slot : slot + 1, :], halo)
        seen.append(jnp.where(sent == ids, 1.0, 0.0))
    far = jnp.max(jnp.maximum(seen[2], seen[3]), axis=0, keepdims=True)
    ring = jnp.max(jnp.maximum(seen[0], seen[1]), axis=0, keepdims=True) * (1.0 - far)
    down = lax.broadcasted_iota(I32, (nodes, nodes), 0)
    along = lax.broadcasted_iota(I32, (nodes, nodes), 1)
    upto = jnp.where(down <= along, 1.0, 0.0).astype(BF16)
    flags = jnp.concatenate([far, ring, jnp.zeros((6, nodes), F32)], 0)
    counts = dot(flags.astype(BF16), upto).astype(I32)
    far_count, ring_count = counts[0:1], counts[1:2]
    totals = jnp.sum(flags, axis=1, keepdims=True).astype(I32)
    far_total, ring_total = totals[0:1], totals[1:2]
    place = jnp.where(
        far > 0.5,
        far_count - 1,
        jnp.where(
            ring > 0.5,
            far_total + ring_count - 1,
            far_total + ring_total + along[:1] - far_count - ring_count,
        ),
    )
    match = place == down
    shuffle = jnp.where(match, 1.0, 0.0).astype(BF16)
    shuffle_out[...] = shuffle
    twice = jnp.concatenate([shuffle, shuffle], 1)
    copy.wait()
    halves = []
    for part, rest_out in enumerate((low_out, high_out)):
        both_parts = jnp.concatenate(split(subspace[part * span : (part + 1) * span, :]), 1)
        turned = dot(both_parts, twice, NT)
        rest_out[...] = turned[:, 2 * duo :]
        halves.append(turned)
    far_out[...] = jnp.concatenate([half[:, :duo] for half in halves], 1)
    ring_out[...] = jnp.concatenate([half[:, duo : 2 * duo] for half in halves], 1)


def assemble(
    odd, lists, connect, blocks_in, shuffle, top_out, low_out, pick_out, both_out, hits_out, pair_out,
    blocks, sem, spread, rows_both,
):
    copy = pltpu.make_async_copy(blocks_in, blocks.at[pl.ds(0, blocks_in.shape[0])], sem)
    copy.start()
    elems, size = connect.shape
    slots, halo = lists.shape[1:]
    nodes = shuffle.shape[0]
    wide = slots * halo
    duo = 2 * halo
    swap = odd[0] == 1
    columns = [column(lists[0, slot : slot + 1, :], halo) for slot in range(slots)]
    outer = jnp.where(swap, columns[0], columns[1])
    inner = jnp.where(swap, columns[1], columns[0])
    sent = jnp.concatenate([columns[2], columns[3], outer, inner], 0)
    hits = jnp.where(sent == lax.broadcasted_iota(I32, (wide, nodes), 1), 1.0, 0.0).astype(BF16)
    hits_out[...] = hits
    pick = dot(hits, shuffle[:wide, :], NT).astype(BF16)
    pick_out[...] = pick
    both = dot(pick, pick, NT)
    both_out[...] = both.astype(BF16)

    lane = lax.broadcasted_iota(I32, (halo, 1), 0)
    flag = odd[0]
    ghost = jnp.concatenate(
        [3 * halo + lane, 2 * halo + lane, (1 - flag) * halo + lane, flag * halo + lane], 0
    )
    along = lax.broadcasted_iota(I32, (nodes, nodes), 1).astype(F32)
    origin = jnp.sum(along * shuffle[...].astype(F32), axis=1, keepdims=True).astype(I32)
    pitch = spread.shape[1] // elems
    full = nodes + wide
    numbers = jnp.broadcast_to(jnp.concatenate([origin, nodes + ghost], 0), (full, pitch))
    copy.wait()
    for elem in range(elems):
        cols = slice(elem * pitch, (elem + 1) * pitch)
        wanted = jnp.pad(connect[elem : elem + 1, :], ((0, 0), (0, pitch - size)), constant_values=-1)
        chosen = jnp.where(numbers == wanted, 1.0, 0.0).astype(BF16)
        spread[:, cols] = chosen
        block = blocks[pl.ds(elem, size, stride=elems), :]
        top, low = split(jnp.pad(block, ((0, pitch - size), (0, pitch - size))))
        rows = dot(jnp.concatenate([top, low], 0), chosen, NT)
        top, low = split(rows[:pitch] + rows[pitch:])
        rows_both[cols, :full] = top
        rows_both[cols, full:] = low
    ham = dot(spread[...], rows_both[...])
    ham = ham[:, :full] + ham[:, full:]
    top, low = split(ham)
    top_out[...] = top
    low_out[...] = low
    far = slice(nodes, nodes + duo)
    pair_out[...] = jnp.concatenate([both[:duo, :duo], ham[far, far]], 1)


def rotate_own(
    group, shuffle, subspace_in, ritz_in, start_out, top_out, low_out, subspace, ritz, sems
):
    block, depth = ritz.shape[1:]
    groups = ritz.shape[0]
    parts = sems.shape[1]
    span = depth // parts
    copies = []
    for step in range(groups):
        first = lax.rem(group[0] + groups - step, groups) * depth
        for part in range(parts):
            if step == 0:
                rows = pl.ds(part * span, span)
                copies.append(
                    pltpu.make_async_copy(
                        subspace_in.at[rows], subspace.at[rows], sems.at[groups, part]
                    )
                )
                copies[-1].start()
            cols = pl.ds(pl.multiple_of(first + part * span, span), span)
            copies.append(
                pltpu.make_async_copy(
                    ritz_in.at[:, cols],
                    ritz.at[step, :, pl.ds(part * span, span)],
                    sems.at[step, part],
                )
            )
            copies[-1].start()
    total = None
    for part in range(parts):
        here = slice(part * span, (part + 1) * span)
        copies[2 * part].wait()
        copies[2 * part + 1].wait()
        term = mul(split(ritz[0, :, here]), split(subspace[here, :]))
        total = term if total is None else total + term
    top, low = split(total)
    start_out[...] = dot(top, shuffle[...], NT) + dot(low, shuffle[...], NT)
    for step in range(1, groups):
        for part in range(parts):
            copies[parts + step * parts + part].wait()
            top, low = split(ritz[step, :, part * span : (part + 1) * span])
            cols = slice((step - 1) * depth + part * span, (step - 1) * depth + (part + 1) * span)
            top_out[:, cols] = top
            low_out[:, cols] = low


def rotate(top, low, columns):
    width = columns.shape[1]
    high, rest = split(columns)
    wide = dot(top, jnp.concatenate([high, rest], 1))
    return wide[:, :width] + (wide[:, width:] + dot(low, high))


def pieces(x, groups, part, axis):
    span = x.shape[axis] // (2 * (groups - 1))
    starts = [(2 * step + part) * span for step in range(groups - 1)]
    if axis == 0:
        return [x[start : start + span, :] for start in starts]
    return [x[:, start : start + span] for start in starts]


def rotate_sides(columns, top, low, groups):
    width = columns.shape[1] // 2
    span = columns.shape[0] // (groups - 1)
    whole = jnp.concatenate(
        [
            columns[step * span : (step + 1) * span, part * width : (part + 1) * width]
            for step in range(groups - 1)
            for part in range(2)
        ],
        0,
    )
    return rotate(top[...], low[...], whole)


def rotate_half(columns, top, low, groups, part):
    return rotate(
        jnp.concatenate(pieces(top, groups, part, 1), 1),
        jnp.concatenate(pieces(low, groups, part, 1), 1),
        columns[...],
    )


def rotate_far(groups, columns, start_own, top, low, pick, pair, start_out, far_out):
    duo, block = start_out.shape
    start = (start_own[:, :duo] + rotate_sides(columns, top, low, groups)).T
    start_out[...] = start
    far_out[:, :block] = sift(pick[:duo, :duo], start)
    far_out[:, block:] = pair[...]


def rotate_ring(groups, columns, start_own, start_far, top, low, pick, start_out, out_out, near_out):
    halo = out_out.shape[0]
    duo = 2 * halo
    start = (start_own[:, duo : 2 * duo] + rotate_sides(columns, top, low, groups)).T
    start = jnp.concatenate([start_far[...], start], 0)
    start_out[...] = start
    packed = sift(pick[duo:, :], start)
    out_out[...] = packed[:halo]
    near_out[...] = packed[halo:]


def rotate_low(groups, columns, start_own, top, low, rest_out):
    edge_nodes = start_own.shape[1] - columns.shape[1]
    rest_out[...] = start_own[:, edge_nodes:] + rotate_half(columns, top, low, groups, 0)


def first_part(start_edge, far_in, near_in, out_in, ham_top, ham_low, part_out, overlap_out, couple_out):
    edge_nodes = start_edge.shape[0]
    nodes = ham_top.shape[0] - 4 * out_in.shape[0]
    duo = far_in.shape[0]
    block = start_edge.shape[1]
    ghosts = jnp.concatenate([far_in[:, :block], out_in[...], near_in[...]], 0)
    part_out[...] = mul(
        (ham_top[:, :edge_nodes], ham_low[:, :edge_nodes]), split(start_edge[...])
    ) + mul((ham_top[:, nodes:], ham_low[:, nodes:]), split(ghosts))
    overlap_out[...] = SCALE_ONE * far_in[:, block : block + duo]
    couple_out[...] = far_in[:, block + duo :]


def rotate_rest(
    groups, columns, rest_low, top, low, part, ham_top, ham_low, rest_out, far_out, out_out, near_out
):
    rest = (rest_low[...] + rotate_half(columns, top, low, groups, 1)).T
    rest_out[...] = rest
    halo = out_out.shape[0]
    edge_nodes, width = part.shape[0] - 4 * halo - rest.shape[0], rest.shape[0]
    nodes = edge_nodes + width
    cols = slice(edge_nodes, nodes)
    back = part[nodes:, :] + mul((ham_top[nodes:, cols], ham_low[nodes:, cols]), split(rest))
    far_out[...] = back[: 2 * halo]
    out_out[...] = back[2 * halo : 3 * halo]
    near_out[...] = back[3 * halo :]


def first_base(
    start_edge, start_rest, part, ham_top, ham_low, pick, overlap, back_far,
    start_out, base_out, packed_out, adjust_out,
):
    nodes = ham_top.shape[0] - pick.shape[0]
    edge_nodes = start_edge.shape[0]
    cols = slice(edge_nodes, nodes)
    start = jnp.concatenate([start_edge[...], start_rest[...]], 0)
    start_out[...] = start
    own = part[:nodes, :] + mul(
        (ham_top[:nodes, cols], ham_low[:nodes, cols]), split(start_rest[...])
    )
    base = SCALE_ONE * (own - CENTRE * start)
    base_out[...] = base
    packed_out[...] = sift(pick[...], base[:edge_nodes])
    adjust_out[...] = mul(split(overlap[...]), split(back_far[...]))


def fetch_far(packed, both, near_in, out_in, far_out):
    duo = 2 * out_in.shape[0]
    back = jnp.concatenate([out_in[...], near_in[...]], 0)
    far_out[...] = packed[:duo, :] + SCALE_ONE * sift(both[:duo, duo:], back)


def fetch_ring(packed, both, far_in, near_in, out_in, out_out, near_out):
    halo = out_in.shape[0]
    back = jnp.concatenate([far_in[...], out_in[...], near_in[...]], 0)
    rows = packed[2 * halo :, :] + SCALE_ONE * sift(both[2 * halo :, :], back)
    out_out[...] = rows[:halo]
    near_out[...] = rows[halo:]


def first_own(
    base, pick, far_in, near_in, out_in, ham_top, ham_low, couple, first_out, part_out, known_out
):
    edge_nodes = pick.shape[1]
    nodes = base.shape[0]
    duo = far_in.shape[0]
    back = jnp.concatenate([far_in[...], out_in[...], near_in[...]], 0)
    edge = base[:edge_nodes, :] + SCALE_ONE * sift(pick[...].T, back)
    first = jnp.concatenate([edge, base[edge_nodes:, :]], 0)
    first_out[...] = first
    part_out[...] = mul((ham_top[:, :nodes], ham_low[:, :nodes]), split(first))
    known_out[...] = mul(split(couple[...]), split(sift(pick[:duo, :], edge)))


def return_far(part, ham_top, ham_low, near_in, out_in, far_out):
    halo = out_in.shape[0]
    nodes = part.shape[0] - 4 * halo
    far = slice(nodes, nodes + 2 * halo)
    ring = slice(nodes + 2 * halo, nodes + 4 * halo)
    ghosts = split(jnp.concatenate([out_in[...], near_in[...]], 0))
    far_out[...] = part[far, :] + mul((ham_top[far, ring], ham_low[far, ring]), ghosts)


def return_ring(
    part, ham_top, ham_low, far_in, adjust, near_in, out_in, ghosts_out, out_out, near_out
):
    halo = out_in.shape[0]
    nodes = part.shape[0] - 4 * halo
    ring = slice(nodes + 2 * halo, nodes + 4 * halo)
    ghosts = jnp.concatenate([far_in[...] + adjust[...], out_in[...], near_in[...]], 0)
    ghosts_out[...] = ghosts
    rows = part[ring, :] + mul((ham_top[ring, nodes:], ham_low[ring, nodes:]), split(ghosts))
    out_out[...] = rows[:halo]
    near_out[...] = rows[halo:]


def second_base(part, ghosts, ham_top, ham_low, first, start, known, shuffle, hits, result_out):
    nodes = first.shape[0]
    duo = known.shape[0]
    ham = (ham_top[:nodes, nodes:], ham_low[:nodes, nodes:])
    second = part[:nodes, :] + mul(ham, split(ghosts[...])) - CENTRE * first[...]
    second = SCALE_TWO * second - SIGMA_ONE * SIGMA_TWO * start[...]
    top, low = split(second.T)
    result = dot(top, shuffle[...]) + dot(low, shuffle[...])
    top, low = split(SCALE_TWO * known[...].T)
    result_out[...] = result + (dot(top, hits[:duo, :]) + dot(low, hits[:duo, :]))


def finish(result, hits, far_in, near_in, out_in, out):
    back = jnp.concatenate([far_in[...], out_in[...], near_in[...]], 0)
    columns = jnp.concatenate(split(SCALE_TWO * back.T), 1)
    out[...] = result[...] + dot(columns, jnp.concatenate([hits[...], hits[...]], 0))


def per_device(subspace, ritz, element_ham, connect, send_rows):
    depth, nodes = subspace.shape
    block = ritz.shape[0]
    slots, halo = send_rows.shape[1:]
    partitions = lax.axis_size("mesh")
    groups = lax.axis_size("state")
    across = partitions // 2
    wide = slots * halo
    duo = 2 * halo
    full = nodes + wide

    odd = (lax.axis_index("mesh") % 2).astype(I32).reshape(1)
    group = lax.axis_index("state").astype(I32).reshape(1)
    pairs_far = [(i, (i + across) % partitions) for i in range(partitions)]
    pairs_in = [(i, i ^ 1) for i in range(partitions)]
    pairs_out = [
        (i, (i + 1) % partitions if i % 2 else (i - 1) % partitions) for i in range(partitions)
    ]

    def far(rows):
        return lax.ppermute(rows, "mesh", pairs_far)

    def out(rows):
        return lax.ppermute(rows, "mesh", pairs_out)

    def near(rows):
        return lax.ppermute(rows, "mesh", pairs_in)

    def gather(rows):
        parts = [
            lax.ppermute(rows, "state", [(i, (i + step) % groups) for i in range(groups)])
            for step in range(1, groups)
        ]
        return parts[0] if len(parts) == 1 else jnp.concatenate(parts, 0)

    def rows_of(count):
        return ((count, block), F32)

    halo_out = [rows_of(duo), rows_of(halo), rows_of(halo)]
    smem = pl.BlockSpec(memory_space=pltpu.SMEM)
    vmem = pl.BlockSpec(memory_space=pltpu.VMEM)
    hbm = pl.BlockSpec(memory_space=pltpu.HBM)

    far_cols, ring_cols, low_cols, high_cols, shuffle = call(
        renumber,
        [
            ((depth // 2, 2 * duo), F32),
            ((depth // 2, 2 * duo), F32),
            ((depth // 2, nodes - wide), F32),
            ((depth // 2, nodes - wide), F32),
            ((nodes, nodes), BF16),
        ],
        in_hbm(send_rows), in_hbm(subspace),
        in_specs=[hbm, hbm],
        scratch_shapes=[
            pltpu.VMEM(send_rows.shape, I32),
            pltpu.VMEM(subspace.shape, F32),
            pltpu.SemaphoreType.DMA((2,)),
        ],
    )
    far_cols_in = gather(far_cols)
    ring_cols_in = gather(ring_cols)
    low_cols_in = gather(low_cols)
    high_cols_in = gather(high_cols)
    elems, size = connect.shape
    pitch = -(-size // 128) * 128
    blocks = jnp.transpose(element_ham, (1, 0, 2)).reshape(size * elems, size)
    ham_top, ham_low, pick, both, hits, pair = call(
        assemble,
        [
            ((full, full), BF16),
            ((full, full), BF16),
            ((wide, wide), BF16),
            ((wide, wide), BF16),
            ((wide, nodes), BF16),
            ((duo, 2 * duo), F32),
        ],
        odd, send_rows, connect, in_hbm(blocks), shuffle,
        limit=12,
        in_specs=[smem, vmem, vmem, hbm, vmem],
        scratch_shapes=[
            pltpu.VMEM((pitch * elems, size), F32),
            pltpu.SemaphoreType.DMA,
            pltpu.VMEM((full, elems * pitch), BF16),
            pltpu.VMEM((elems * pitch, 2 * full), BF16),
        ],
    )
    others = groups - 1
    start_own, ritz_top, ritz_low = call(
        rotate_own,
        [
            ((block, nodes), F32),
            ((block, others * depth), BF16),
            ((block, others * depth), BF16),
        ],
        group, shuffle, in_hbm(subspace), in_hbm(ritz),
        limit=12,
        in_specs=[smem, vmem, hbm, hbm],
        scratch_shapes=[
            pltpu.VMEM(subspace.shape, F32),
            pltpu.VMEM((groups, block, depth), F32),
            pltpu.SemaphoreType.DMA((groups + 1, 1)),
        ],
    )

    start_far, far_rows = call(
        functools.partial(rotate_far, groups),
        [rows_of(duo), ((duo, block + 2 * duo), F32)],
        far_cols_in, start_own, ritz_top, ritz_low, pick, pair,
    )
    far_in = far(far_rows)
    start_edge, out_rows, near_rows = call(
        functools.partial(rotate_ring, groups),
        [rows_of(wide), rows_of(halo), rows_of(halo)],
        ring_cols_in, start_own, start_far, ritz_top, ritz_low, pick,
    )
    near_in, out_in = near(near_rows), out(out_rows)
    part, overlap, couple = call(
        first_part,
        [rows_of(full), ((duo, duo), F32), ((duo, duo), F32)],
        start_edge, far_in, near_in, out_in, ham_top, ham_low,
    )
    (rest_low,) = call(
        functools.partial(rotate_low, groups),
        [((block, nodes - wide), F32)],
        low_cols_in, start_own, ritz_top, ritz_low,
    )

    start_rest, back_far, back_out, back_near = call(
        functools.partial(rotate_rest, groups),
        [rows_of(nodes - wide)] + halo_out,
        high_cols_in, rest_low, ritz_top, ritz_low, part, ham_top, ham_low,
    )
    far_in, near_in, out_in = far(back_far), near(back_near), out(back_out)
    start, base, packed, adjust = call(
        first_base,
        [rows_of(nodes), rows_of(nodes), rows_of(wide), rows_of(duo)],
        start_edge, start_rest, part, ham_top, ham_low, pick, overlap, back_far,
    )
    (far_rows,) = call(fetch_far, [rows_of(duo)], packed, both, near_in, out_in)
    fetched_far = far(far_rows)
    out_rows, near_rows = call(
        fetch_ring, halo_out[1:], packed, both, far_in, near_in, out_in
    )
    fetched_near, fetched_out = near(near_rows), out(out_rows)
    first, part, known = call(
        first_own,
        [rows_of(nodes), rows_of(full), rows_of(duo)],
        base, pick, far_in, near_in, out_in, ham_top, ham_low, couple,
    )

    (far_rows,) = call(
        return_far, [rows_of(duo)], part, ham_top, ham_low, fetched_near, fetched_out
    )
    returned_far = far(far_rows)
    ghosts, out_rows, near_rows = call(
        return_ring,
        [rows_of(wide)] + halo_out[1:],
        part, ham_top, ham_low, fetched_far, adjust, fetched_near, fetched_out,
    )
    returned_near, returned_out = near(near_rows), out(out_rows)
    (result,) = call(
        second_base,
        [((block, nodes), F32)],
        part, ghosts, ham_top, ham_low, first, start, known, shuffle, hits,
    )
    (result,) = call(
        finish, [((block, nodes), F32)], result, hits, returned_far, returned_near, returned_out
    )
    return result


def solution(mesh):
    in_specs = (
        P("state", "mesh"),
        P("state", None),
        P("mesh", None, None),
        P("mesh", None),
        P("mesh", None, None),
    )
    out_specs = P("state", "mesh")
    return jax.shard_map(
        per_device, mesh=mesh, in_specs=in_specs, out_specs=out_specs, check_vma=False
    )
```

```python
import functools

import jax
import jax.numpy as jnp
from jax import lax
from jax.experimental import pallas as pl
from jax.experimental.pallas import tpu as pltpu
from jax.sharding import PartitionSpec as P

F32 = jnp.float32
BF16 = jnp.bfloat16
I32 = jnp.int32
NN = ((1,), (0,))
NT = ((1,), (1,))

HALF = 1.5
CENTRE = 2.5
SIGMA_ONE = HALF / (-1.0 - CENTRE)
SIGMA_TWO = 1.0 / (2.0 / SIGMA_ONE - SIGMA_ONE)
SCALE_ONE = SIGMA_ONE / HALF
SCALE_TWO = 2.0 * SIGMA_TWO / HALF


def dot(a, b, dims=NN):
    return lax.dot_general(a, b, (dims, ((), ())), preferred_element_type=F32)


def split(x):
    top = x.astype(BF16)
    return top, (x - top.astype(F32)).astype(BF16)


def mul(a, b, dims=NN):
    if dims == NN and a[0].shape[1] == 128:
        left = jnp.concatenate([a[0], a[0], a[1]], 1)
        return dot(left, jnp.concatenate([b[0], b[1], b[0]], 0))
    return dot(a[0], b[0], dims) + (dot(a[0], b[1], dims) + dot(a[1], b[0], dims))


def sift(a, x):
    return dot(jnp.concatenate([a, a], 1), jnp.concatenate(split(x), 0))


def call(body, outs, *args, limit=8, **rest):
    return pl.pallas_call(
        body,
        out_shape=[jax.ShapeDtypeStruct(*out) for out in outs],
        compiler_params=pltpu.CompilerParams(vmem_limit_bytes=limit << 20),
        **rest,
    )(*args)


def in_hbm(x):
    return pltpu.with_memory_space_constraint(x, pltpu.HBM)


def column(row, width):
    down = lax.broadcasted_iota(I32, (width, width), 0)
    along = lax.broadcasted_iota(I32, (width, width), 1)
    return jnp.sum(jnp.where(down == along, row, 0), axis=1, keepdims=True)


def renumber(
    lists_in, subspace_in, far_out, ring_out, low_out, high_out, shuffle_out, lists, subspace, sems
):
    slots, halo = lists.shape[1:]
    depth, nodes = subspace.shape
    duo = 2 * halo
    span = depth // 2
    index_copy = pltpu.make_async_copy(lists_in, lists, sems.at[0])
    index_copy.start()
    copy = pltpu.make_async_copy(subspace_in, subspace, sems.at[1])
    copy.start()
    index_copy.wait()
    ids = lax.broadcasted_iota(I32, (halo, nodes), 1)
    seen = []
    for slot in range(slots):
        sent = column(lists[0, slot : slot + 1, :], halo)
        seen.append(jnp.where(sent == ids, 1.0, 0.0))
    far = jnp.max(jnp.maximum(seen[2], seen[3]), axis=0, keepdims=True)
    ring = jnp.max(jnp.maximum(seen[0], seen[1]), axis=0, keepdims=True) * (1.0 - far)
    down = lax.broadcasted_iota(I32, (nodes, nodes), 0)
    along = lax.broadcasted_iota(I32, (nodes, nodes), 1)
    upto = jnp.where(down <= along, 1.0, 0.0).astype(BF16)
    flags = jnp.concatenate([far, ring, jnp.zeros((6, nodes), F32)], 0)
    counts = dot(flags.astype(BF16), upto).astype(I32)
    far_count, ring_count = counts[0:1], counts[1:2]
    totals = jnp.sum(flags, axis=1, keepdims=True).astype(I32)
    far_total, ring_total = totals[0:1], totals[1:2]
    place = jnp.where(
        far > 0.5,
        far_count - 1,
        jnp.where(
            ring > 0.5,
            far_total + ring_count - 1,
            far_total + ring_total + along[:1] - far_count - ring_count,
        ),
    )
    match = place == down
    shuffle = jnp.where(match, 1.0, 0.0).astype(BF16)
    shuffle_out[...] = shuffle
    twice = jnp.concatenate([shuffle, shuffle], 1)
    copy.wait()
    halves = []
    for part, rest_out in enumerate((low_out, high_out)):
        both_parts = jnp.concatenate(split(subspace[part * span : (part + 1) * span, :]), 1)
        turned = dot(both_parts, twice, NT)
        rest_out[...] = turned[:, 2 * duo :]
        halves.append(turned)
    far_out[...] = jnp.concatenate([half[:, :duo] for half in halves], 1)
    ring_out[...] = jnp.concatenate([half[:, duo : 2 * duo] for half in halves], 1)


def assemble(
    odd, lists, connect, blocks_in, shuffle, top_out, low_out, pick_out, both_out, hits_out, pair_out,
    blocks, sem, spread, rows_both,
):
    copy = pltpu.make_async_copy(blocks_in, blocks.at[pl.ds(0, blocks_in.shape[0])], sem)
    copy.start()
    elems, size = connect.shape
    slots, halo = lists.shape[1:]
    nodes = shuffle.shape[0]
    wide = slots * halo
    duo = 2 * halo
    swap = odd[0] == 1
    columns = [column(lists[0, slot : slot + 1, :], halo) for slot in range(slots)]
    outer = jnp.where(swap, columns[0], columns[1])
    inner = jnp.where(swap, columns[1], columns[0])
    sent = jnp.concatenate([columns[2], columns[3], outer, inner], 0)
    hits = jnp.where(sent == lax.broadcasted_iota(I32, (wide, nodes), 1), 1.0, 0.0).astype(BF16)
    hits_out[...] = hits
    pick = dot(hits, shuffle[:wide, :], NT).astype(BF16)
    pick_out[...] = pick
    both = dot(pick, pick, NT)
    both_out[...] = both.astype(BF16)

    lane = lax.broadcasted_iota(I32, (halo, 1), 0)
    flag = odd[0]
    ghost = jnp.concatenate(
        [3 * halo + lane, 2 * halo + lane, (1 - flag) * halo + lane, flag * halo + lane], 0
    )
    along = lax.broadcasted_iota(I32, (nodes, nodes), 1).astype(F32)
    origin = jnp.sum(along * shuffle[...].astype(F32), axis=1, keepdims=True).astype(I32)
    pitch = spread.shape[1] // elems
    full = nodes + wide
    numbers = jnp.broadcast_to(jnp.concatenate([origin, nodes + ghost], 0), (full, pitch))
    copy.wait()
    for elem in range(elems):
        cols = slice(elem * pitch, (elem + 1) * pitch)
        wanted = jnp.pad(connect[elem : elem + 1, :], ((0, 0), (0, pitch - size)), constant_values=-1)
        chosen = jnp.where(numbers == wanted, 1.0, 0.0).astype(BF16)
        spread[:, cols] = chosen
        block = blocks[pl.ds(elem, size, stride=elems), :]
        top, low = split(jnp.pad(block, ((0, pitch - size), (0, pitch - size))))
        rows = dot(jnp.concatenate([top, low], 0), chosen, NT)
        top, low = split(rows[:pitch] + rows[pitch:])
        rows_both[cols, :full] = top
        rows_both[cols, full:] = low
    ham = dot(spread[...], rows_both[...])
    ham = ham[:, :full] + ham[:, full:]
    top, low = split(ham)
    top_out[...] = top
    low_out[...] = low
    far = slice(nodes, nodes + duo)
    pair_out[...] = jnp.concatenate([both[:duo, :duo], ham[far, far]], 1)


def rotate_own(
    group, shuffle, subspace_in, ritz_in, start_out, top_out, low_out, subspace, ritz, sems
):
    block, depth = ritz.shape[1:]
    groups = ritz.shape[0]
    parts = sems.shape[1]
    span = depth // parts
    copies = []
    for step in range(groups):
        first = lax.rem(group[0] + groups - step, groups) * depth
        for part in range(parts):
            if step == 0:
                rows = pl.ds(part * span, span)
                copies.append(
                    pltpu.make_async_copy(
                        subspace_in.at[rows], subspace.at[rows], sems.at[groups, part]
                    )
                )
                copies[-1].start()
            cols = pl.ds(pl.multiple_of(first + part * span, span), span)
            copies.append(
                pltpu.make_async_copy(
                    ritz_in.at[:, cols],
                    ritz.at[step, :, pl.ds(part * span, span)],
                    sems.at[step, part],
                )
            )
            copies[-1].start()
    total = None
    for part in range(parts):
        here = slice(part * span, (part + 1) * span)
        copies[2 * part].wait()
        copies[2 * part + 1].wait()
        term = mul(split(ritz[0, :, here]), split(subspace[here, :]))
        total = term if total is None else total + term
    top, low = split(total)
    start_out[...] = dot(top, shuffle[...], NT) + dot(low, shuffle[...], NT)
    for step in range(1, groups):
        for part in range(parts):
            copies[parts + step * parts + part].wait()
            top, low = split(ritz[step, :, part * span : (part + 1) * span])
            cols = slice((step - 1) * depth + part * span, (step - 1) * depth + (part + 1) * span)
            top_out[:, cols] = top
            low_out[:, cols] = low


def rotate(top, low, columns):
    width = columns.shape[1]
    high, rest = split(columns)
    wide = dot(top, jnp.concatenate([high, rest], 1))
    return wide[:, :width] + (wide[:, width:] + dot(low, high))


def pieces(x, groups, part, axis):
    span = x.shape[axis] // (2 * (groups - 1))
    starts = [(2 * step + part) * span for step in range(groups - 1)]
    if axis == 0:
        return [x[start : start + span, :] for start in starts]
    return [x[:, start : start + span] for start in starts]


def rotate_sides(columns, top, low, groups):
    width = columns.shape[1] // 2
    span = columns.shape[0] // (groups - 1)
    whole = jnp.concatenate(
        [
            columns[step * span : (step + 1) * span, part * width : (part + 1) * width]
            for step in range(groups - 1)
            for part in range(2)
        ],
        0,
    )
    return rotate(top[...], low[...], whole)


def rotate_half(columns, top, low, groups, part):
    return rotate(
        jnp.concatenate(pieces(top, groups, part, 1), 1),
        jnp.concatenate(pieces(low, groups, part, 1), 1),
        columns[...],
    )


def rotate_far(groups, columns, start_own, top, low, pick, pair, start_out, far_out):
    duo, block = start_out.shape
    start = (start_own[:, :duo] + rotate_sides(columns, top, low, groups)).T
    start_out[...] = start
    far_out[:, :block] = sift(pick[:duo, :duo], start)
    far_out[:, block:] = pair[...]


def rotate_ring(groups, columns, start_own, start_far, top, low, pick, start_out, out_out, near_out):
    halo = out_out.shape[0]
    duo = 2 * halo
    start = (start_own[:, duo : 2 * duo] + rotate_sides(columns, top, low, groups)).T
    start = jnp.concatenate([start_far[...], start], 0)
    start_out[...] = start
    packed = sift(pick[duo:, :], start)
    out_out[...] = packed[:halo]
    near_out[...] = packed[halo:]


def rotate_low(groups, columns, start_own, top, low, rest_out):
    edge_nodes = start_own.shape[1] - columns.shape[1]
    rest_out[...] = start_own[:, edge_nodes:] + rotate_half(columns, top, low, groups, 0)


def first_part(start_edge, far_in, out_in, near_in, ham_top, ham_low, part_out, overlap_out, couple_out):
    edge_nodes = start_edge.shape[0]
    nodes = ham_top.shape[0] - 4 * out_in.shape[0]
    duo = far_in.shape[0]
    block = start_edge.shape[1]
    ghosts = jnp.concatenate([far_in[:, :block], out_in[...], near_in[...]], 0)
    part_out[...] = mul(
        (ham_top[:, :edge_nodes], ham_low[:, :edge_nodes]), split(start_edge[...])
    ) + mul((ham_top[:, nodes:], ham_low[:, nodes:]), split(ghosts))
    overlap_out[...] = SCALE_ONE * far_in[:, block : block + duo]
    couple_out[...] = far_in[:, block + duo :]


def rotate_rest(
    groups, columns, rest_low, top, low, part, ham_top, ham_low, rest_out, far_out, out_out, near_out
):
    rest = (rest_low[...] + rotate_half(columns, top, low, groups, 1)).T
    rest_out[...] = rest
    halo = out_out.shape[0]
    edge_nodes, width = part.shape[0] - 4 * halo - rest.shape[0], rest.shape[0]
    nodes = edge_nodes + width
    cols = slice(edge_nodes, nodes)
    back = part[nodes:, :] + mul((ham_top[nodes:, cols], ham_low[nodes:, cols]), split(rest))
    far_out[...] = back[: 2 * halo]
    out_out[...] = back[2 * halo : 3 * halo]
    near_out[...] = back[3 * halo :]


def first_base(
    start_edge, start_rest, part, ham_top, ham_low, pick, overlap, back_far,
    start_out, base_out, packed_out, adjust_out,
):
    nodes = ham_top.shape[0] - pick.shape[0]
    edge_nodes = start_edge.shape[0]
    cols = slice(edge_nodes, nodes)
    start = jnp.concatenate([start_edge[...], start_rest[...]], 0)
    start_out[...] = start
    own = part[:nodes, :] + mul(
        (ham_top[:nodes, cols], ham_low[:nodes, cols]), split(start_rest[...])
    )
    base = SCALE_ONE * (own - CENTRE * start)
    base_out[...] = base
    packed_out[...] = sift(pick[...], base[:edge_nodes])
    adjust_out[...] = mul(split(overlap[...]), split(back_far[...]))


def fetch_far(packed, both, out_in, near_in, far_out):
    duo = 2 * out_in.shape[0]
    back = jnp.concatenate([out_in[...], near_in[...]], 0)
    far_out[...] = packed[:duo, :] + SCALE_ONE * sift(both[:duo, duo:], back)


def fetch_ring(packed, both, far_in, out_in, near_in, out_out, near_out):
    halo = out_in.shape[0]
    back = jnp.concatenate([far_in[...], out_in[...], near_in[...]], 0)
    rows = packed[2 * halo :, :] + SCALE_ONE * sift(both[2 * halo :, :], back)
    out_out[...] = rows[:halo]
    near_out[...] = rows[halo:]


def first_own(
    base, pick, far_in, out_in, near_in, ham_top, ham_low, couple, first_out, part_out, known_out
):
    edge_nodes = pick.shape[1]
    nodes = base.shape[0]
    duo = far_in.shape[0]
    back = jnp.concatenate([far_in[...], out_in[...], near_in[...]], 0)
    edge = base[:edge_nodes, :] + SCALE_ONE * sift(pick[...].T, back)
    first = jnp.concatenate([edge, base[edge_nodes:, :]], 0)
    first_out[...] = first
    part_out[...] = mul((ham_top[:, :nodes], ham_low[:, :nodes]), split(first))
    known_out[...] = mul(split(couple[...]), split(sift(pick[:duo, :], edge)))


def return_far(part, ham_top, ham_low, out_in, near_in, far_out):
    halo = out_in.shape[0]
    nodes = part.shape[0] - 4 * halo
    far = slice(nodes, nodes + 2 * halo)
    ring = slice(nodes + 2 * halo, nodes + 4 * halo)
    ghosts = split(jnp.concatenate([out_in[...], near_in[...]], 0))
    far_out[...] = part[far, :] + mul((ham_top[far, ring], ham_low[far, ring]), ghosts)


def return_ring(
    part, ham_top, ham_low, far_in, adjust, out_in, near_in, ghosts_out, out_out, near_out
):
    halo = out_in.shape[0]
    nodes = part.shape[0] - 4 * halo
    ring = slice(nodes + 2 * halo, nodes + 4 * halo)
    ghosts = jnp.concatenate([far_in[...] + adjust[...], out_in[...], near_in[...]], 0)
    ghosts_out[...] = ghosts
    rows = part[ring, :] + mul((ham_top[ring, nodes:], ham_low[ring, nodes:]), split(ghosts))
    out_out[...] = rows[:halo]
    near_out[...] = rows[halo:]


def second_base(part, ghosts, ham_top, ham_low, first, start, known, shuffle, hits, result_out):
    nodes = first.shape[0]
    duo = known.shape[0]
    ham = (ham_top[:nodes, nodes:], ham_low[:nodes, nodes:])
    second = part[:nodes, :] + mul(ham, split(ghosts[...])) - CENTRE * first[...]
    second = SCALE_TWO * second - SIGMA_ONE * SIGMA_TWO * start[...]
    top, low = split(second.T)
    result = dot(top, shuffle[...]) + dot(low, shuffle[...])
    top, low = split(SCALE_TWO * known[...].T)
    result_out[...] = result + (dot(top, hits[:duo, :]) + dot(low, hits[:duo, :]))


def finish(result, hits, far_in, out_in, near_in, out):
    back = jnp.concatenate([far_in[...], out_in[...], near_in[...]], 0)
    columns = jnp.concatenate(split(SCALE_TWO * back.T), 1)
    out[...] = result[...] + dot(columns, jnp.concatenate([hits[...], hits[...]], 0))


def per_device(subspace, ritz, element_ham, connect, send_rows):
    depth, nodes = subspace.shape
    block = ritz.shape[0]
    slots, halo = send_rows.shape[1:]
    partitions = lax.axis_size("mesh")
    groups = lax.axis_size("state")
    across = partitions // 2
    wide = slots * halo
    duo = 2 * halo
    full = nodes + wide

    odd = (lax.axis_index("mesh") % 2).astype(I32).reshape(1)
    group = lax.axis_index("state").astype(I32).reshape(1)
    pairs_far = [(i, (i + across) % partitions) for i in range(partitions)]
    pairs_in = [(i, i ^ 1) for i in range(partitions)]
    pairs_out = [
        (i, (i + 1) % partitions if i % 2 else (i - 1) % partitions) for i in range(partitions)
    ]

    def far(rows):
        return lax.ppermute(rows, "mesh", pairs_far)

    def out(rows):
        return lax.ppermute(rows, "mesh", pairs_out)

    def near(rows):
        return lax.ppermute(rows, "mesh", pairs_in)

    def gather(rows):
        parts = [
            lax.ppermute(rows, "state", [(i, (i + step) % groups) for i in range(groups)])
            for step in range(1, groups)
        ]
        return parts[0] if len(parts) == 1 else jnp.concatenate(parts, 0)

    def rows_of(count):
        return ((count, block), F32)

    halo_out = [rows_of(duo), rows_of(halo), rows_of(halo)]
    smem = pl.BlockSpec(memory_space=pltpu.SMEM)
    vmem = pl.BlockSpec(memory_space=pltpu.VMEM)
    hbm = pl.BlockSpec(memory_space=pltpu.HBM)

    far_cols, ring_cols, low_cols, high_cols, shuffle = call(
        renumber,
        [
            ((depth // 2, 2 * duo), F32),
            ((depth // 2, 2 * duo), F32),
            ((depth // 2, nodes - wide), F32),
            ((depth // 2, nodes - wide), F32),
            ((nodes, nodes), BF16),
        ],
        in_hbm(send_rows), in_hbm(subspace),
        in_specs=[hbm, hbm],
        scratch_shapes=[
            pltpu.VMEM(send_rows.shape, I32),
            pltpu.VMEM(subspace.shape, F32),
            pltpu.SemaphoreType.DMA((2,)),
        ],
    )
    far_cols_in = gather(far_cols)
    ring_cols_in = gather(ring_cols)
    low_cols_in = gather(low_cols)
    high_cols_in = gather(high_cols)
    elems, size = connect.shape
    pitch = -(-size // 128) * 128
    blocks = jnp.transpose(element_ham, (1, 0, 2)).reshape(size * elems, size)
    ham_top, ham_low, pick, both, hits, pair = call(
        assemble,
        [
            ((full, full), BF16),
            ((full, full), BF16),
            ((wide, wide), BF16),
            ((wide, wide), BF16),
            ((wide, nodes), BF16),
            ((duo, 2 * duo), F32),
        ],
        odd, send_rows, connect, in_hbm(blocks), shuffle,
        limit=12,
        in_specs=[smem, vmem, vmem, hbm, vmem],
        scratch_shapes=[
            pltpu.VMEM((pitch * elems, size), F32),
            pltpu.SemaphoreType.DMA,
            pltpu.VMEM((full, elems * pitch), BF16),
            pltpu.VMEM((elems * pitch, 2 * full), BF16),
        ],
    )
    others = groups - 1
    start_own, ritz_top, ritz_low = call(
        rotate_own,
        [
            ((block, nodes), F32),
            ((block, others * depth), BF16),
            ((block, others * depth), BF16),
        ],
        group, shuffle, in_hbm(subspace), in_hbm(ritz),
        limit=12,
        in_specs=[smem, vmem, hbm, hbm],
        scratch_shapes=[
            pltpu.VMEM(subspace.shape, F32),
            pltpu.VMEM((groups, block, depth), F32),
            pltpu.SemaphoreType.DMA((groups + 1, 1)),
        ],
    )

    start_far, far_rows = call(
        functools.partial(rotate_far, groups),
        [rows_of(duo), ((duo, block + 2 * duo), F32)],
        far_cols_in, start_own, ritz_top, ritz_low, pick, pair,
    )
    far_in = far(far_rows)
    start_edge, out_rows, near_rows = call(
        functools.partial(rotate_ring, groups),
        [rows_of(wide), rows_of(halo), rows_of(halo)],
        ring_cols_in, start_own, start_far, ritz_top, ritz_low, pick,
    )
    out_in, near_in = out(out_rows), near(near_rows)
    part, overlap, couple = call(
        first_part,
        [rows_of(full), ((duo, duo), F32), ((duo, duo), F32)],
        start_edge, far_in, out_in, near_in, ham_top, ham_low,
    )
    (rest_low,) = call(
        functools.partial(rotate_low, groups),
        [((block, nodes - wide), F32)],
        low_cols_in, start_own, ritz_top, ritz_low,
    )

    start_rest, back_far, back_out, back_near = call(
        functools.partial(rotate_rest, groups),
        [rows_of(nodes - wide)] + halo_out,
        high_cols_in, rest_low, ritz_top, ritz_low, part, ham_top, ham_low,
    )
    far_in, out_in, near_in = far(back_far), out(back_out), near(back_near)
    start, base, packed, adjust = call(
        first_base,
        [rows_of(nodes), rows_of(nodes), rows_of(wide), rows_of(duo)],
        start_edge, start_rest, part, ham_top, ham_low, pick, overlap, back_far,
    )
    (far_rows,) = call(fetch_far, [rows_of(duo)], packed, both, out_in, near_in)
    fetched_far = far(far_rows)
    out_rows, near_rows = call(
        fetch_ring, halo_out[1:], packed, both, far_in, out_in, near_in
    )
    fetched_out, fetched_near = out(out_rows), near(near_rows)
    first, part, known = call(
        first_own,
        [rows_of(nodes), rows_of(full), rows_of(duo)],
        base, pick, far_in, out_in, near_in, ham_top, ham_low, couple,
    )

    (far_rows,) = call(
        return_far, [rows_of(duo)], part, ham_top, ham_low, fetched_out, fetched_near
    )
    returned_far = far(far_rows)
    ghosts, out_rows, near_rows = call(
        return_ring,
        [rows_of(wide)] + halo_out[1:],
        part, ham_top, ham_low, fetched_far, adjust, fetched_out, fetched_near,
    )
    returned_out, returned_near = out(out_rows), near(near_rows)
    (result,) = call(
        second_base,
        [((block, nodes), F32)],
        part, ghosts, ham_top, ham_low, first, start, known, shuffle, hits,
    )
    (result,) = call(
        finish, [((block, nodes), F32)], result, hits, returned_far, returned_out, returned_near
    )
    return result


def solution(mesh):
    in_specs = (
        P("state", "mesh"),
        P("state", None),
        P("mesh", None, None),
        P("mesh", None),
        P("mesh", None, None),
    )
    out_specs = P("state", "mesh")
    return jax.shard_map(
        per_device, mesh=mesh, in_specs=in_specs, out_specs=out_specs, check_vma=False
    )
```

```python
import functools

import jax
import jax.numpy as jnp
from jax import lax
from jax.experimental import pallas as pl
from jax.experimental.pallas import tpu as pltpu
from jax.sharding import PartitionSpec as P

F32 = jnp.float32
BF16 = jnp.bfloat16
I32 = jnp.int32
NN = ((1,), (0,))
NT = ((1,), (1,))

HALF = 1.5
CENTRE = 2.5
SIGMA_ONE = HALF / (-1.0 - CENTRE)
SIGMA_TWO = 1.0 / (2.0 / SIGMA_ONE - SIGMA_ONE)
SCALE_ONE = SIGMA_ONE / HALF
SCALE_TWO = 2.0 * SIGMA_TWO / HALF


def dot(a, b, dims=NN):
    return lax.dot_general(a, b, (dims, ((), ())), preferred_element_type=F32)


def split(x):
    top = x.astype(BF16)
    return top, (x - top.astype(F32)).astype(BF16)


def mul(a, b, dims=NN):
    if dims == NN and a[0].shape[1] == 128:
        left = jnp.concatenate([a[0], a[0], a[1]], 1)
        return dot(left, jnp.concatenate([b[0], b[1], b[0]], 0))
    return dot(a[0], b[0], dims) + (dot(a[0], b[1], dims) + dot(a[1], b[0], dims))


def sift(a, x):
    return dot(jnp.concatenate([a, a], 1), jnp.concatenate(split(x), 0))


def call(body, outs, *args, limit=8, **rest):
    return pl.pallas_call(
        body,
        out_shape=[jax.ShapeDtypeStruct(*out) for out in outs],
        compiler_params=pltpu.CompilerParams(vmem_limit_bytes=limit << 20),
        **rest,
    )(*args)


def in_hbm(x):
    return pltpu.with_memory_space_constraint(x, pltpu.HBM)


def column(row, width):
    down = lax.broadcasted_iota(I32, (width, width), 0)
    along = lax.broadcasted_iota(I32, (width, width), 1)
    return jnp.sum(jnp.where(down == along, row, 0), axis=1, keepdims=True)


def renumber(
    lists_in, subspace_in, far_out, ring_out, low_out, high_out, shuffle_out, lists, subspace, sems
):
    slots, halo = lists.shape[1:]
    depth, nodes = subspace.shape
    duo = 2 * halo
    span = depth // 2
    index_copy = pltpu.make_async_copy(lists_in, lists, sems.at[0])
    index_copy.start()
    copy = pltpu.make_async_copy(subspace_in, subspace, sems.at[1])
    copy.start()
    index_copy.wait()
    ids = lax.broadcasted_iota(I32, (halo, nodes), 1)
    seen = []
    for slot in range(slots):
        sent = column(lists[0, slot : slot + 1, :], halo)
        seen.append(jnp.where(sent == ids, 1.0, 0.0))
    far = jnp.max(jnp.maximum(seen[2], seen[3]), axis=0, keepdims=True)
    ring = jnp.max(jnp.maximum(seen[0], seen[1]), axis=0, keepdims=True) * (1.0 - far)
    down = lax.broadcasted_iota(I32, (nodes, nodes), 0)
    along = lax.broadcasted_iota(I32, (nodes, nodes), 1)
    upto = jnp.where(down <= along, 1.0, 0.0).astype(BF16)
    flags = jnp.concatenate([far, ring, jnp.zeros((6, nodes), F32)], 0)
    counts = dot(flags.astype(BF16), upto).astype(I32)
    far_count, ring_count = counts[0:1], counts[1:2]
    totals = jnp.sum(flags, axis=1, keepdims=True).astype(I32)
    far_total, ring_total = totals[0:1], totals[1:2]
    place = jnp.where(
        far > 0.5,
        far_count - 1,
        jnp.where(
            ring > 0.5,
            far_total + ring_count - 1,
            far_total + ring_total + along[:1] - far_count - ring_count,
        ),
    )
    match = place == down
    shuffle = jnp.where(match, 1.0, 0.0).astype(BF16)
    shuffle_out[...] = shuffle
    twice = jnp.concatenate([shuffle, shuffle], 1)
    copy.wait()
    halves = []
    for part, rest_out in enumerate((low_out, high_out)):
        both_parts = jnp.concatenate(split(subspace[part * span : (part + 1) * span, :]), 1)
        turned = dot(both_parts, twice, NT)
        rest_out[...] = turned[:, 2 * duo :]
        halves.append(turned)
    far_out[...] = jnp.concatenate([half[:, :duo] for half in halves], 1)
    ring_out[...] = jnp.concatenate([half[:, duo : 2 * duo] for half in halves], 1)


def assemble(
    odd, lists, connect, blocks_in, shuffle, top_out, low_out, pick_out, both_out, hits_out, pair_out,
    blocks, sem, spread, rows_both,
):
    copy = pltpu.make_async_copy(blocks_in, blocks.at[pl.ds(0, blocks_in.shape[0])], sem)
    copy.start()
    elems, size = connect.shape
    slots, halo = lists.shape[1:]
    nodes = shuffle.shape[0]
    wide = slots * halo
    duo = 2 * halo
    swap = odd[0] == 1
    columns = [column(lists[0, slot : slot + 1, :], halo) for slot in range(slots)]
    outer = jnp.where(swap, columns[0], columns[1])
    inner = jnp.where(swap, columns[1], columns[0])
    sent = jnp.concatenate([columns[2], columns[3], outer, inner], 0)
    hits = jnp.where(sent == lax.broadcasted_iota(I32, (wide, nodes), 1), 1.0, 0.0).astype(BF16)
    hits_out[...] = hits
    pick = dot(hits, shuffle[:wide, :], NT).astype(BF16)
    pick_out[...] = pick
    both = dot(pick, pick, NT)
    both_out[...] = both.astype(BF16)

    lane = lax.broadcasted_iota(I32, (halo, 1), 0)
    flag = odd[0]
    ghost = jnp.concatenate(
        [3 * halo + lane, 2 * halo + lane, (1 - flag) * halo + lane, flag * halo + lane], 0
    )
    along = lax.broadcasted_iota(I32, (nodes, nodes), 1).astype(F32)
    origin = jnp.sum(along * shuffle[...].astype(F32), axis=1, keepdims=True).astype(I32)
    pitch = spread.shape[1] // elems
    full = nodes + wide
    numbers = jnp.broadcast_to(jnp.concatenate([origin, nodes + ghost], 0), (full, pitch))
    copy.wait()
    for elem in range(elems):
        cols = slice(elem * pitch, (elem + 1) * pitch)
        wanted = jnp.pad(connect[elem : elem + 1, :], ((0, 0), (0, pitch - size)), constant_values=-1)
        chosen = jnp.where(numbers == wanted, 1.0, 0.0).astype(BF16)
        spread[:, cols] = chosen
        block = blocks[pl.ds(elem, size, stride=elems), :]
        top, low = split(jnp.pad(block, ((0, pitch - size), (0, pitch - size))))
        rows = dot(jnp.concatenate([top, low], 0), chosen, NT)
        top, low = split(rows[:pitch] + rows[pitch:])
        rows_both[cols, :full] = top
        rows_both[cols, full:] = low
    ham = dot(spread[...], rows_both[...])
    ham = ham[:, :full] + ham[:, full:]
    top, low = split(ham)
    top_out[...] = top
    low_out[...] = low
    far = slice(nodes, nodes + duo)
    pair_out[...] = jnp.concatenate([both[:duo, :duo], ham[far, far]], 1)


def rotate_own(
    group, shuffle, subspace_in, ritz_in, start_out, top_out, low_out, subspace, ritz, sems
):
    block, depth = ritz.shape[1:]
    groups = ritz.shape[0]
    parts = sems.shape[1]
    span = depth // parts
    copies = []
    for step in range(groups):
        first = lax.rem(group[0] + groups - step, groups) * depth
        for part in range(parts):
            if step == 0:
                rows = pl.ds(part * span, span)
                copies.append(
                    pltpu.make_async_copy(
                        subspace_in.at[rows], subspace.at[rows], sems.at[groups, part]
                    )
                )
                copies[-1].start()
            cols = pl.ds(pl.multiple_of(first + part * span, span), span)
            copies.append(
                pltpu.make_async_copy(
                    ritz_in.at[:, cols],
                    ritz.at[step, :, pl.ds(part * span, span)],
                    sems.at[step, part],
                )
            )
            copies[-1].start()
    total = None
    for part in range(parts):
        here = slice(part * span, (part + 1) * span)
        copies[2 * part].wait()
        copies[2 * part + 1].wait()
        term = mul(split(ritz[0, :, here]), split(subspace[here, :]))
        total = term if total is None else total + term
    top, low = split(total)
    start_out[...] = dot(top, shuffle[...], NT) + dot(low, shuffle[...], NT)
    for step in range(1, groups):
        for part in range(parts):
            copies[parts + step * parts + part].wait()
            top, low = split(ritz[step, :, part * span : (part + 1) * span])
            cols = slice((step - 1) * depth + part * span, (step - 1) * depth + (part + 1) * span)
            top_out[:, cols] = top
            low_out[:, cols] = low


def rotate(top, low, columns):
    width = columns.shape[1]
    high, rest = split(columns)
    wide = dot(top, jnp.concatenate([high, rest], 1))
    return wide[:, :width] + (wide[:, width:] + dot(low, high))


def pieces(x, groups, part, axis):
    span = x.shape[axis] // (2 * (groups - 1))
    starts = [(2 * step + part) * span for step in range(groups - 1)]
    if axis == 0:
        return [x[start : start + span, :] for start in starts]
    return [x[:, start : start + span] for start in starts]


def rotate_sides(columns, top, low, groups):
    width = columns.shape[1] // 2
    span = columns.shape[0] // (groups - 1)
    whole = jnp.concatenate(
        [
            columns[step * span : (step + 1) * span, part * width : (part + 1) * width]
            for step in range(groups - 1)
            for part in range(2)
        ],
        0,
    )
    return rotate(top[...], low[...], whole)


def rotate_half(columns, top, low, groups, part):
    return rotate(
        jnp.concatenate(pieces(top, groups, part, 1), 1),
        jnp.concatenate(pieces(low, groups, part, 1), 1),
        columns[...],
    )


def rotate_far(groups, columns, start_own, top, low, pick, pair, start_out, far_out):
    duo, block = start_out.shape
    start = (start_own[:, :duo] + rotate_sides(columns, top, low, groups)).T
    start_out[...] = start
    far_out[:, :block] = sift(pick[:duo, :duo], start)
    far_out[:, block:] = pair[...]


def rotate_ring(groups, columns, start_own, start_far, top, low, pick, start_out, out_out, near_out):
    halo = out_out.shape[0]
    duo = 2 * halo
    start = (start_own[:, duo : 2 * duo] + rotate_sides(columns, top, low, groups)).T
    start = jnp.concatenate([start_far[...], start], 0)
    start_out[...] = start
    packed = sift(pick[duo:, :], start)
    out_out[...] = packed[:halo]
    near_out[...] = packed[halo:]


def rotate_low(groups, columns, start_own, top, low, rest_out):
    edge_nodes = start_own.shape[1] - columns.shape[1]
    rest_out[...] = start_own[:, edge_nodes:] + rotate_half(columns, top, low, groups, 0)


def first_part(start_edge, far_in, out_in, near_in, ham_top, ham_low, part_out, overlap_out, couple_out):
    edge_nodes = start_edge.shape[0]
    nodes = ham_top.shape[0] - 4 * out_in.shape[0]
    duo = far_in.shape[0]
    block = start_edge.shape[1]
    ghosts = jnp.concatenate([far_in[:, :block], out_in[...], near_in[...]], 0)
    part_out[...] = mul(
        (ham_top[:, :edge_nodes], ham_low[:, :edge_nodes]), split(start_edge[...])
    ) + mul((ham_top[:, nodes:], ham_low[:, nodes:]), split(ghosts))
    overlap_out[...] = SCALE_ONE * far_in[:, block : block + duo]
    couple_out[...] = far_in[:, block + duo :]


def rotate_rest(
    groups, columns, rest_low, top, low, part, ham_top, ham_low, rest_out, far_out, out_out, near_out
):
    rest = (rest_low[...] + rotate_half(columns, top, low, groups, 1)).T
    rest_out[...] = rest
    halo = out_out.shape[0]
    edge_nodes, width = part.shape[0] - 4 * halo - rest.shape[0], rest.shape[0]
    nodes = edge_nodes + width
    cols = slice(edge_nodes, nodes)
    back = part[nodes:, :] + mul((ham_top[nodes:, cols], ham_low[nodes:, cols]), split(rest))
    far_out[...] = back[: 2 * halo]
    out_out[...] = back[2 * halo : 3 * halo]
    near_out[...] = back[3 * halo :]


def first_base(
    start_edge, start_rest, part, ham_top, ham_low, pick, overlap, back_far,
    start_out, base_out, packed_out, adjust_out,
):
    nodes = ham_top.shape[0] - pick.shape[0]
    edge_nodes = start_edge.shape[0]
    cols = slice(edge_nodes, nodes)
    start = jnp.concatenate([start_edge[...], start_rest[...]], 0)
    start_out[...] = start
    own = part[:nodes, :] + mul(
        (ham_top[:nodes, cols], ham_low[:nodes, cols]), split(start_rest[...])
    )
    base = SCALE_ONE * (own - CENTRE * start)
    base_out[...] = base
    packed_out[...] = sift(pick[...], base[:edge_nodes])
    adjust_out[...] = mul(split(overlap[...]), split(back_far[...]))


def fetch_far(packed, both, near_in, out_in, far_out):
    duo = 2 * out_in.shape[0]
    back = jnp.concatenate([out_in[...], near_in[...]], 0)
    far_out[...] = packed[:duo, :] + SCALE_ONE * sift(both[:duo, duo:], back)


def fetch_ring(packed, both, far_in, out_in, near_in, out_out, near_out):
    halo = out_in.shape[0]
    back = jnp.concatenate([far_in[...], out_in[...], near_in[...]], 0)
    rows = packed[2 * halo :, :] + SCALE_ONE * sift(both[2 * halo :, :], back)
    out_out[...] = rows[:halo]
    near_out[...] = rows[halo:]


def first_own(
    base, pick, far_in, out_in, near_in, ham_top, ham_low, couple, first_out, part_out, known_out
):
    edge_nodes = pick.shape[1]
    nodes = base.shape[0]
    duo = far_in.shape[0]
    back = jnp.concatenate([far_in[...], out_in[...], near_in[...]], 0)
    edge = base[:edge_nodes, :] + SCALE_ONE * sift(pick[...].T, back)
    first = jnp.concatenate([edge, base[edge_nodes:, :]], 0)
    first_out[...] = first
    part_out[...] = mul((ham_top[:, :nodes], ham_low[:, :nodes]), split(first))
    known_out[...] = mul(split(couple[...]), split(sift(pick[:duo, :], edge)))


def return_far(part, ham_top, ham_low, out_in, near_in, far_out):
    halo = out_in.shape[0]
    nodes = part.shape[0] - 4 * halo
    far = slice(nodes, nodes + 2 * halo)
    ring = slice(nodes + 2 * halo, nodes + 4 * halo)
    ghosts = split(jnp.concatenate([out_in[...], near_in[...]], 0))
    far_out[...] = part[far, :] + mul((ham_top[far, ring], ham_low[far, ring]), ghosts)


def return_ring(
    part, ham_top, ham_low, far_in, adjust, out_in, near_in, ghosts_out, out_out, near_out
):
    halo = out_in.shape[0]
    nodes = part.shape[0] - 4 * halo
    ring = slice(nodes + 2 * halo, nodes + 4 * halo)
    ghosts = jnp.concatenate([far_in[...] + adjust[...], out_in[...], near_in[...]], 0)
    ghosts_out[...] = ghosts
    rows = part[ring, :] + mul((ham_top[ring, nodes:], ham_low[ring, nodes:]), split(ghosts))
    out_out[...] = rows[:halo]
    near_out[...] = rows[halo:]


def second_base(part, ghosts, ham_top, ham_low, first, start, known, shuffle, hits, result_out):
    nodes = first.shape[0]
    duo = known.shape[0]
    ham = (ham_top[:nodes, nodes:], ham_low[:nodes, nodes:])
    second = part[:nodes, :] + mul(ham, split(ghosts[...])) - CENTRE * first[...]
    second = SCALE_TWO * second - SIGMA_ONE * SIGMA_TWO * start[...]
    top, low = split(second.T)
    result = dot(top, shuffle[...]) + dot(low, shuffle[...])
    top, low = split(SCALE_TWO * known[...].T)
    result_out[...] = result + (dot(top, hits[:duo, :]) + dot(low, hits[:duo, :]))


def finish(result, hits, far_in, out_in, near_in, out):
    back = jnp.concatenate([far_in[...], out_in[...], near_in[...]], 0)
    columns = jnp.concatenate(split(SCALE_TWO * back.T), 1)
    out[...] = result[...] + dot(columns, jnp.concatenate([hits[...], hits[...]], 0))


def per_device(subspace, ritz, element_ham, connect, send_rows):
    depth, nodes = subspace.shape
    block = ritz.shape[0]
    slots, halo = send_rows.shape[1:]
    partitions = lax.axis_size("mesh")
    groups = lax.axis_size("state")
    across = partitions // 2
    wide = slots * halo
    duo = 2 * halo
    full = nodes + wide

    odd = (lax.axis_index("mesh") % 2).astype(I32).reshape(1)
    group = lax.axis_index("state").astype(I32).reshape(1)
    pairs_far = [(i, (i + across) % partitions) for i in range(partitions)]
    pairs_in = [(i, i ^ 1) for i in range(partitions)]
    pairs_out = [
        (i, (i + 1) % partitions if i % 2 else (i - 1) % partitions) for i in range(partitions)
    ]

    def far(rows):
        return lax.ppermute(rows, "mesh", pairs_far)

    def out(rows):
        return lax.ppermute(rows, "mesh", pairs_out)

    def near(rows):
        return lax.ppermute(rows, "mesh", pairs_in)

    def gather(rows):
        parts = [
            lax.ppermute(rows, "state", [(i, (i + step) % groups) for i in range(groups)])
            for step in range(1, groups)
        ]
        return parts[0] if len(parts) == 1 else jnp.concatenate(parts, 0)

    def rows_of(count):
        return ((count, block), F32)

    halo_out = [rows_of(duo), rows_of(halo), rows_of(halo)]
    smem = pl.BlockSpec(memory_space=pltpu.SMEM)
    vmem = pl.BlockSpec(memory_space=pltpu.VMEM)
    hbm = pl.BlockSpec(memory_space=pltpu.HBM)

    far_cols, ring_cols, low_cols, high_cols, shuffle = call(
        renumber,
        [
            ((depth // 2, 2 * duo), F32),
            ((depth // 2, 2 * duo), F32),
            ((depth // 2, nodes - wide), F32),
            ((depth // 2, nodes - wide), F32),
            ((nodes, nodes), BF16),
        ],
        in_hbm(send_rows), in_hbm(subspace),
        in_specs=[hbm, hbm],
        scratch_shapes=[
            pltpu.VMEM(send_rows.shape, I32),
            pltpu.VMEM(subspace.shape, F32),
            pltpu.SemaphoreType.DMA((2,)),
        ],
    )
    far_cols_in = gather(far_cols)
    ring_cols_in = gather(ring_cols)
    low_cols_in = gather(low_cols)
    high_cols_in = gather(high_cols)
    elems, size = connect.shape
    pitch = -(-size // 128) * 128
    blocks = jnp.transpose(element_ham, (1, 0, 2)).reshape(size * elems, size)
    ham_top, ham_low, pick, both, hits, pair = call(
        assemble,
        [
            ((full, full), BF16),
            ((full, full), BF16),
            ((wide, wide), BF16),
            ((wide, wide), BF16),
            ((wide, nodes), BF16),
            ((duo, 2 * duo), F32),
        ],
        odd, send_rows, connect, in_hbm(blocks), shuffle,
        limit=12,
        in_specs=[smem, vmem, vmem, hbm, vmem],
        scratch_shapes=[
            pltpu.VMEM((pitch * elems, size), F32),
            pltpu.SemaphoreType.DMA,
            pltpu.VMEM((full, elems * pitch), BF16),
            pltpu.VMEM((elems * pitch, 2 * full), BF16),
        ],
    )
    others = groups - 1
    start_own, ritz_top, ritz_low = call(
        rotate_own,
        [
            ((block, nodes), F32),
            ((block, others * depth), BF16),
            ((block, others * depth), BF16),
        ],
        group, shuffle, in_hbm(subspace), in_hbm(ritz),
        limit=12,
        in_specs=[smem, vmem, hbm, hbm],
        scratch_shapes=[
            pltpu.VMEM(subspace.shape, F32),
            pltpu.VMEM((groups, block, depth), F32),
            pltpu.SemaphoreType.DMA((groups + 1, 1)),
        ],
    )

    start_far, far_rows = call(
        functools.partial(rotate_far, groups),
        [rows_of(duo), ((duo, block + 2 * duo), F32)],
        far_cols_in, start_own, ritz_top, ritz_low, pick, pair,
    )
    far_in = far(far_rows)
    start_edge, out_rows, near_rows = call(
        functools.partial(rotate_ring, groups),
        [rows_of(wide), rows_of(halo), rows_of(halo)],
        ring_cols_in, start_own, start_far, ritz_top, ritz_low, pick,
    )
    out_in, near_in = out(out_rows), near(near_rows)
    part, overlap, couple = call(
        first_part,
        [rows_of(full), ((duo, duo), F32), ((duo, duo), F32)],
        start_edge, far_in, out_in, near_in, ham_top, ham_low,
    )
    (rest_low,) = call(
        functools.partial(rotate_low, groups),
        [((block, nodes - wide), F32)],
        low_cols_in, start_own, ritz_top, ritz_low,
    )

    start_rest, back_far, back_out, back_near = call(
        functools.partial(rotate_rest, groups),
        [rows_of(nodes - wide)] + halo_out,
        high_cols_in, rest_low, ritz_top, ritz_low, part, ham_top, ham_low,
    )
    far_in, near_in, out_in = far(back_far), near(back_near), out(back_out)
    start, base, packed, adjust = call(
        first_base,
        [rows_of(nodes), rows_of(nodes), rows_of(wide), rows_of(duo)],
        start_edge, start_rest, part, ham_top, ham_low, pick, overlap, back_far,
    )
    (far_rows,) = call(fetch_far, [rows_of(duo)], packed, both, near_in, out_in)
    fetched_far = far(far_rows)
    out_rows, near_rows = call(
        fetch_ring, halo_out[1:], packed, both, far_in, out_in, near_in
    )
    fetched_out, fetched_near = out(out_rows), near(near_rows)
    first, part, known = call(
        first_own,
        [rows_of(nodes), rows_of(full), rows_of(duo)],
        base, pick, far_in, out_in, near_in, ham_top, ham_low, couple,
    )

    (far_rows,) = call(
        return_far, [rows_of(duo)], part, ham_top, ham_low, fetched_out, fetched_near
    )
    returned_far = far(far_rows)
    ghosts, out_rows, near_rows = call(
        return_ring,
        [rows_of(wide)] + halo_out[1:],
        part, ham_top, ham_low, fetched_far, adjust, fetched_out, fetched_near,
    )
    returned_out, returned_near = out(out_rows), near(near_rows)
    (result,) = call(
        second_base,
        [((block, nodes), F32)],
        part, ghosts, ham_top, ham_low, first, start, known, shuffle, hits,
    )
    (result,) = call(
        finish, [((block, nodes), F32)], result, hits, returned_far, returned_out, returned_near
    )
    return result


def solution(mesh):
    in_specs = (
        P("state", "mesh"),
        P("state", None),
        P("mesh", None, None),
        P("mesh", None),
        P("mesh", None, None),
    )
    out_specs = P("state", "mesh")
    return jax.shard_map(
        per_device, mesh=mesh, in_specs=in_specs, out_specs=out_specs, check_vma=False
    )
```
